32 devices in a mesh: dp: 4 (over z), seq: 8 (over y, x, core).
Axes of the slice: x: 2, y: 2, z: 4, core: 2. Of those that a mesh axis runs over, the one named last changes fastest.
Arguments:
- inputs: bfloat16 [4096, 1536], P(('dp', 'seq')), may hold values from -6 to 6
- output_grad: bfloat16 [4096, 1536], P(('dp', 'seq')), may hold values from -6 to 6
- document_starts: int32 [4, 4], P('dp'), may hold values from 0 to 1023, as said below
- joined_weight: float32 [1536, 2048], P(('dp', 'seq')), may hold values from -0.15625 to 0.15625
- out_weight: float32 [1536, 1536], P(('dp', 'seq')), may hold values from -1.25 to 1.25
- units_weight: float32 [8960, 3, 1536], P(('dp', 'seq')), may hold values from -0.15625 to 0.15625
- small_params: float32 [256, 20], P(('dp', 'seq')), may hold values from -1 to 2
- joined_first: float32 [1536, 2048], P(('dp', 'seq')), may hold values from -160 to 160
- joined_second: float32 [1536, 2048], P(('dp', 'seq')), may hold values from 1724.6316 to 13797.053
- out_first: float32 [1536, 1536], P(('dp', 'seq')), may hold values from -7 to 7
- out_second: float32 [1536, 1536], P(('dp', 'seq')), may hold values from 2.994152 to 23.953217
- units_first: float32 [8960, 3, 1536], P(('dp', 'seq')), may hold values from -20 to 20
- units_second: float32 [8960, 3, 1536], P(('dp', 'seq')), may hold values from 26.947369 to 215.57895
- small_first: float32 [256, 20], P(('dp', 'seq')), may hold values from -80 to 80
- small_second: float32 [256, 20], P(('dp', 'seq')), may hold values from 431.1579 to 3449.2632
Outputs:
- block_output: bfloat16 [4096, 1536], P(('dp', 'seq'))
- input_grad: float32 [4096, 1536], P(('dp', 'seq'))
- joined_next: float32 [1536, 2048], P(('dp', 'seq'))
- joined_first_next: float32 [1536, 2048], P(('dp', 'seq'))
- joined_second_next: float32 [1536, 2048], P(('dp', 'seq'))
- joined_low: bfloat16 [1536, 2048], P(('dp', 'seq'))
- out_next: float32 [1536, 1536], P(('dp', 'seq'))
- out_first_next: float32 [1536, 1536], P(('dp', 'seq'))
- out_second_next: float32 [1536, 1536], P(('dp', 'seq'))
- out_low: bfloat16 [1536, 1536], P(('dp', 'seq'))
- units_next: float32 [8960, 3, 1536], P(('dp', 'seq'))
- units_first_next: float32 [8960, 3, 1536], P(('dp', 'seq'))
- units_second_next: float32 [8960, 3, 1536], P(('dp', 'seq'))
- units_low: bfloat16 [8960, 3, 1536], P(('dp', 'seq'))
- small_next: float32 [256, 20], P(('dp', 'seq'))
- small_first_next: float32 [256, 20], P(('dp', 'seq'))
- small_second_next: float32 [256, 20], P(('dp', 'seq'))
- small_low: bfloat16 [256, 20], P(('dp', 'seq'))
The draws below stay inside these ranges and needn't reach their ends.
Inputs may be any that keep to these rules, and one draw needn't show every extreme that they name: `document_starts`: within a row the starts rise strictly and the first is 0; in each row one document begins among the group's first 128 tokens and ends among its last 128.
All inputs are finite; a program needn't handle non-finite values.
Results may differ from the reference program's by a relative error of at most 0.02.
Values may be sent and summed in bfloat16 or wider, within the bound.
No kernel may reach another device: no remote copies, remote signals or barrier semaphores. Data moves between devices by JAX's collectives and lax.ppermute only.
A program may use at most 448 MiB of HBM per device.

```python
import math
import jax
import jax.numpy as jnp
from jax import lax

D = 1536
HEADS = 12
KV_HEADS = 2
HEAD_DIM = 128
FF = 8960
TOK_DEV = 128
DOCS = 4
BLOCK = 256
STEP = 5
QW = 1536
KW = 256
QKV = 2048
SMALL_COLS = 20
TOK_GRP = 1024
TOKENS = 4096
N_DP = 4


def draw_document_starts(key, part):
    key = jax.random.fold_in(key, 11)
    pick_key, first_key, last_key = jax.random.split(key, 3)
    longest = jax.random.randint(pick_key, (N_DP, 1), 0, DOCS)
    leading = jax.random.randint(first_key, (N_DP, 1), 1, TOK_DEV // DOCS + 1)
    trailing = jax.random.randint(last_key, (N_DP, 1), 1, TOK_DEV // DOCS + 1)
    index = jnp.arange(DOCS, dtype=jnp.int32)[None, :]
    after = TOK_GRP - (DOCS - 1 - longest) * trailing + (index - longest - 1) * trailing
    return jnp.where(index <= longest, index * leading, after).astype(jnp.int32)


def draw_small_params(key, part):
    key = jax.random.fold_in(key, 7)
    first_key, second_key = jax.random.split(key)
    gain_cols = 2 * D // KW
    bias_cols = HEADS // KV_HEADS + 2
    gains = jax.random.uniform(first_key, (KW, gain_cols), jnp.float32, 0.6, 1.4)
    biases = 0.3 * jnp.clip(jax.random.normal(second_key, (KW, bias_cols), jnp.float32), -3.0, 3.0)
    return jnp.concatenate([gains, biases], axis=1)


def block_scale(own_key, extent, shards, smallest, largest):
    def one(dim, blocks):
        draws = jax.random.uniform(jax.random.fold_in(jax.random.fold_in(own_key, 6), dim), (blocks,), jnp.float32, smallest / len(shards), largest / len(shards))
        return jnp.repeat(jnp.exp(draws), extent[dim] // blocks).reshape((-1,) + (1,) * (len(extent) - dim - 1))

    factor_of = one(*shards[0])
    for cut in shards[1:]:
        factor_of = factor_of * one(*cut)
    return factor_of


def centred(stream_key, extent, spread, most, cuts=(), held_as=jnp.bfloat16):
    gain = block_scale(stream_key, extent, cuts, -0.22, 0.18) if cuts else 1.0
    entries = jax.random.normal(stream_key, extent, jnp.float32) * spread * gain
    return jnp.minimum(jnp.maximum(entries, -most), most).astype(held_as)


def setup_inputs(seed: int = 0) -> dict:
    seeds = jax.random.split(jax.random.key(seed), 16)
    inputs = centred(seeds[0], (TOKENS, D), 1.0, 6.0, ((0, 32),))
    output_grad = centred(seeds[1], (TOKENS, D), 1.0, 6.0, ((0, 32),))
    document_starts = draw_document_starts(jax.random.fold_in(seeds[15], 71), 0)
    joined_weight = centred(seeds[3], (D, QKV), D ** -0.5, 0.15625, ((0, 32),), jnp.float32)
    out_weight = centred(seeds[4], (QW, D), (QW // 64) ** -0.5, 1.25, ((0, 32),), jnp.float32)
    units_weight = centred(seeds[5], (FF, 3, D), D ** -0.5, 0.15625, ((0, 32),), jnp.float32)
    small_params = draw_small_params(jax.random.fold_in(seeds[15], 71), 0)
    joined_first = centred(seeds[7], (D, QKV), (4 * TOKENS ** 0.5 / 9), 160.0, ((0, 32),), jnp.float32)
    joined_second = jnp.clip(jnp.exp(math.log(13797.053) - 2.0794415 * jax.random.uniform(seeds[8], (D, QKV), jnp.float32) ** block_scale(seeds[8], (D, QKV), ((0, 32),), -0.2, 0.2)), 1724.6316, 13797.053)
    out_first = centred(seeds[9], (QW, D), (TOKENS ** 0.5 / 54), 7.0, ((0, 32),), jnp.float32)
    out_second = jnp.clip(jnp.exp(math.log(23.953217) - 2.0794415 * jax.random.uniform(seeds[10], (QW, D), jnp.float32) ** block_scale(seeds[10], (QW, D), ((0, 32),), -0.2, 0.2)), 2.994152, 23.953217)
    units_first = centred(seeds[11], (FF, 3, D), (TOKENS ** 0.5 / 18), 20.0, ((0, 32),), jnp.float32)
    units_second = jnp.clip(jnp.exp(math.log(215.57895) - 2.0794415 * jax.random.uniform(seeds[12], (FF, 3, D), jnp.float32) ** block_scale(seeds[12], (FF, 3, D), ((0, 32),), -0.2, 0.2)), 26.947369, 215.57895)
    small_first = centred(seeds[13], (KW, SMALL_COLS), (2 * TOKENS ** 0.5 / 9), 80.0, ((0, 32),), jnp.float32)
    small_second = jnp.clip(jnp.exp(math.log(3449.2632) - 2.0794415 * jax.random.uniform(seeds[14], (KW, SMALL_COLS), jnp.float32) ** block_scale(seeds[14], (KW, SMALL_COLS), ((0, 32),), -0.2, 0.2)), 431.1579, 3449.2632)
    return dict(inputs=inputs, output_grad=output_grad, document_starts=document_starts, joined_weight=joined_weight, out_weight=out_weight, units_weight=units_weight, small_params=small_params, joined_first=joined_first, joined_second=joined_second, out_first=out_first, out_second=out_second, units_first=units_first, units_second=units_second, small_first=small_first, small_second=small_second)


NORM_EPS = 1e-06
ROPE_BASE = 1000000.0
BETA_ONE = 0.9
BETA_TWO = 0.95
ADAM_EPS = 1e-08
DECAY = 0.1

@jax.custom_vjp
def low(v):
    return lax.optimization_barrier(v.astype(jnp.bfloat16)).astype(jnp.float32)

@jax.custom_vjp
def low_back(v):
    return v

def low_keep(v):
    return (low(v), None)

def low_pass(kept, grad):
    return (grad,)

def back_keep(v):
    return (v, None)

def back_low(kept, grad):
    return (low(grad),)
low.defvjp(low_keep, low_pass)
low_back.defvjp(back_keep, back_low)

def product(left, right, form):
    return jnp.einsum(form, left, right, precision=lax.Precision.HIGHEST)

def unpack_small(small):
    gain_cols = D // KW
    group = HEADS // KV_HEADS
    gain_one = small[:, :gain_cols].reshape(D)
    gain_two = small[:, gain_cols:2 * gain_cols].reshape(D)
    query_bias = small[:, 2 * gain_cols:2 * gain_cols + group].reshape(KV_HEADS, HEAD_DIM, group)
    query_bias = jnp.transpose(query_bias, (0, 2, 1)).reshape(QW)
    key_bias = small[:, 2 * gain_cols + group]
    value_bias = small[:, 2 * gain_cols + group + 1]
    return (gain_one, gain_two, jnp.concatenate([query_bias, key_bias, value_bias]))

def layout(starts_row, first, count):
    places = first + jnp.arange(count, dtype=jnp.int32)
    before = starts_row[None, :] <= places[:, None]
    documents = lax.optimization_barrier(jnp.sum(before.astype(jnp.int32), axis=1)) - 1
    begin = lax.optimization_barrier(jnp.max(jnp.where(before, starts_row[None, :], 0), axis=1))
    offset = places - begin
    return (documents, offset // BLOCK, offset)

def turning(offset):
    half = HEAD_DIM // 2
    frequency = ROPE_BASE ** (-(2.0 * jnp.arange(half, dtype=jnp.float32)) / HEAD_DIM)
    angle = offset.astype(jnp.float32)[:, None] * frequency[None, :]
    angle = jnp.concatenate([angle, angle], axis=1)
    return (jnp.cos(angle)[:, None, :], jnp.sin(angle)[:, None, :])

def rotate(values, cosine, sine):
    half = values.shape[-1] // 2
    turned = jnp.concatenate([-values[..., half:], values[..., :half]], axis=-1)
    return values * cosine + turned * sine

def group_layer(params, rows, starts_row):
    joined_low, out_low, units_low, small_low = [low(item) for item in params]
    count = rows.shape[0]
    group = HEADS // KV_HEADS
    gain_one, gain_two, bias = unpack_small(small_low)
    documents, blocks, offset = layout(starts_row, 0, count)
    cosine, sine = turning(offset)
    normed = low(rows * lax.rsqrt(lax.optimization_barrier(jnp.mean(rows * rows, axis=1, keepdims=True)) + NORM_EPS) * gain_one)
    mixed = low_back(product(normed, joined_low, 'td,de->te') + bias)
    query = low(rotate(mixed[:, :QW].reshape(count, HEADS, HEAD_DIM), cosine, sine))
    query = query.reshape(count, KV_HEADS, group, HEAD_DIM)
    keys = low(rotate(mixed[:, QW:QW + KW].reshape(count, KV_HEADS, HEAD_DIM), cosine, sine))
    values = low(mixed[:, QW + KW:].reshape(count, KV_HEADS, HEAD_DIM))
    span = min(512, count)
    scale = HEAD_DIM ** (-0.5)

    def attend(index):
        start = (index * span).astype(jnp.int32)
        part = lax.dynamic_slice_in_dim(query, start, span, 0)
        part_documents = lax.dynamic_slice_in_dim(documents, start, span, 0)
        part_blocks = lax.dynamic_slice_in_dim(blocks, start, span, 0)
        scores = low_back(product(part, keys, 'qcgd,kcd->cgqk') * scale)
        seen = (part_documents[:, None] == documents[None, :]) & (blocks[None, :] <= part_blocks[:, None])
        scores = jnp.where(seen, scores, -jnp.inf)
        total = jax.nn.logsumexp(scores, axis=-1, keepdims=True)
        weights = low(jnp.exp(scores - total))
        return product(weights, values, 'cgqk,kcd->qcgd')
    attended = lax.map(jax.checkpoint(attend), jnp.arange(count // span, dtype=jnp.int32))
    attended = low(low_back(attended.reshape(count, QW)))
    middle = rows + low_back(product(attended, out_low, 'te,ed->td'))
    normed_two = low(middle * lax.rsqrt(lax.optimization_barrier(jnp.mean(middle * middle, axis=1, keepdims=True)) + NORM_EPS) * gain_two)
    gate = low_back(product(normed_two, units_low[:, 0, :], 'td,ud->tu'))
    up = low_back(product(normed_two, units_low[:, 1, :], 'td,ud->tu'))
    hidden = low(jax.nn.silu(gate) * up)
    return middle + product(hidden, units_low[:, 2, :], 'tu,ud->td')

def optimizer_step(weight, grad, first, second, rate, decay):
    first = BETA_ONE * first + (1.0 - BETA_ONE) * grad
    second = BETA_TWO * second + (1.0 - BETA_TWO) * grad * grad
    fixed_first = first / (1.0 - BETA_ONE ** STEP)
    fixed_second = second / (1.0 - BETA_TWO ** STEP)
    weight = weight - rate * (fixed_first / (jnp.sqrt(fixed_second) + ADAM_EPS) + decay * weight)
    return (weight, first, second, weight.astype(jnp.bfloat16))

def reference(inputs, output_grad, document_starts, joined_weight, out_weight, units_weight, small_params, joined_first, joined_second, out_first, out_second, units_first, units_second, small_first, small_second):
    params = (joined_weight, out_weight, units_weight, small_params)
    rows = inputs.astype(jnp.float32).reshape(N_DP, TOK_GRP, D)
    backs = output_grad.astype(jnp.float32).reshape(N_DP, TOK_GRP, D)

    def one_group(totals, pieces):
        group_rows, group_back, starts_row = pieces
        result, pull = jax.vjp(lambda weights, entry: group_layer(weights, entry, starts_row), params, group_rows)
        grads, row_grad = pull(group_back)
        return (jax.tree.map(lambda left, right: left + right, totals, grads), (result, row_grad))
    zeros = jax.tree.map(jnp.zeros_like, params)
    grads, (results, row_grads) = lax.scan(one_group, zeros, (rows, backs, document_starts))
    joined = optimizer_step(joined_weight, grads[0], joined_first, joined_second, 2.0 / math.sqrt(D), DECAY)
    outer = optimizer_step(out_weight, grads[1], out_first, out_second, 2.0 / math.sqrt(QW // 64), DECAY)
    units = optimizer_step(units_weight, grads[2], units_first, units_second, 2.0 / math.sqrt(D), DECAY)
    small = optimizer_step(small_params, grads[3], small_first, small_second, 0.5, 0.0)
    return (results.reshape(TOKENS, D).astype(jnp.bfloat16), row_grads.reshape(TOKENS, D), joined[0], joined[1], joined[2], joined[3], outer[0], outer[1], outer[2], outer[3], units[0], units[1], units[2], units[3], small[0], small[1], small[2], small[3])
```

```python
import math

import jax
import jax.numpy as jnp
from jax import lax
from jax.sharding import Mesh
from jax.sharding import PartitionSpec as P

D = 1536
HEADS = 12
KV_HEADS = 2
HEAD_DIM = 128
FF = 8960
BLOCK = 256
STEP = 5
QW = 1536
KW = 256
QKV = 2048


NORM_EPS = 1e-06
ROPE_BASE = 1000000.0
BETA_ONE = 0.9
BETA_TWO = 0.95
ADAM_EPS = 1e-08
DECAY = 0.1


DP = ("zh", "zl")
SEQ = ("y", "x", "c")
ALL = DP + SEQ


def shift(value, axis, step):
    count = lax.axis_size(axis)
    return lax.ppermute(value, axis, [(i, (i + step) % count) for i in range(count)])


def rotations(value, axis):
    return [value] + [shift(value, axis, step) for step in range(1, lax.axis_size(axis))]


def gather_rows(value):
    result = []
    for number, block in enumerate(rotations(value, "zh")):
        if number % 2 == 0:
            grid = [rotations(item, "y") for item in rotations(block, "x")]
            grid = [[grid[i][j] for i in range(len(grid))] for j in range(len(grid[0]))]
        else:
            grid = [rotations(item, "x") for item in rotations(block, "y")]
        result.append([item for line in grid for item in line])
    return result


def low(value):
    return value.astype(jnp.bfloat16)


def wide(value):
    return value.astype(jnp.float32)


def add_back(blocks, axis):
    total = wide(blocks[0])
    for step in range(1, len(blocks)):
        total = total + wide(shift(low(blocks[step]), axis, -step))
    return total


def scatter_rows(parts):
    across, along = lax.axis_size("x"), lax.axis_size("y")
    lines = []
    for number, blocks in enumerate(parts):
        grid = [blocks[j * across : (j + 1) * across] for j in range(along)]
        if number % 2 == 0:
            sums = [add_back([grid[j][i] for j in range(along)], "y") for i in range(across)]
            lines.append(add_back(sums, "x"))
        else:
            sums = [add_back(grid[j], "x") for j in range(along)]
            lines.append(add_back(sums, "y"))
    return add_back(lines, "zh")


def norm_scale(rows):
    return lax.rsqrt(jnp.mean(rows * rows, axis=1, keepdims=True) + NORM_EPS)


def unpack_small(small):
    gain_cols = D // KW
    group = HEADS // KV_HEADS
    gain_one = small[:, :gain_cols].reshape(D)
    gain_two = small[:, gain_cols : 2 * gain_cols].reshape(D)
    query_bias = small[:, 2 * gain_cols : 2 * gain_cols + group].reshape(KV_HEADS, HEAD_DIM, group)
    query_bias = jnp.transpose(query_bias, (0, 2, 1)).reshape(QW)
    key_bias = small[:, 2 * gain_cols + group]
    value_bias = small[:, 2 * gain_cols + group + 1]
    return (gain_one, gain_two, jnp.concatenate([query_bias, key_bias, value_bias]))


def pack_small(gain_one, gain_two, bias):
    gain_cols = D // KW
    group = HEADS // KV_HEADS
    query_part = jnp.transpose(bias[:QW].reshape(KV_HEADS, group, HEAD_DIM), (0, 2, 1)).reshape(
        KW, group
    )
    return jnp.concatenate(
        [
            gain_one.reshape(KW, gain_cols),
            gain_two.reshape(KW, gain_cols),
            query_part,
            bias[QW : QW + KW][:, None],
            bias[QW + KW :][:, None],
        ],
        axis=1,
    )


def layout(starts_row, first, count):
    places = first + jnp.arange(count, dtype=jnp.int32)
    before = starts_row[None, :] <= places[:, None]
    documents = jnp.sum(before.astype(jnp.int32), axis=1) - 1
    begin = jnp.max(jnp.where(before, starts_row[None, :], 0), axis=1)
    offset = places - begin
    return (documents, offset // BLOCK, offset)


def turning(offset):
    half = HEAD_DIM // 2
    frequency = ROPE_BASE ** (-(2.0 * jnp.arange(half, dtype=jnp.float32)) / HEAD_DIM)
    angle = offset.astype(jnp.float32)[:, None] * frequency[None, :]
    angle = jnp.concatenate([angle, angle], axis=1)
    return (jnp.cos(angle)[:, None, :], jnp.sin(angle)[:, None, :])


def rotate(values, cosine, sine):
    half = values.shape[-1] // 2
    turned = jnp.concatenate([-values[..., half:], values[..., :half]], axis=-1)
    return values * cosine + turned * sine


def rotate_back(grads, cosine, sine):
    half = grads.shape[-1] // 2
    moved = grads * sine
    turned = jnp.concatenate([moved[..., half:], -moved[..., :half]], axis=-1)
    return grads * cosine + turned


def optimizer_step(weight, grad, first, second, rate, decay):
    first = BETA_ONE * first + (1.0 - BETA_ONE) * grad
    second = BETA_TWO * second + (1.0 - BETA_TWO) * grad * grad
    fixed_first = first / (1.0 - BETA_ONE**STEP)
    fixed_second = second / (1.0 - BETA_TWO**STEP)
    weight = weight - rate * (fixed_first / (jnp.sqrt(fixed_second) + ADAM_EPS) + decay * weight)
    return (weight, first, second, weight.astype(jnp.bfloat16))


def body(
    inputs,
    output_grad,
    document_starts,
    joined_weight,
    out_weight,
    units_weight,
    small_params,
    joined_first,
    joined_second,
    out_first,
    out_second,
    units_first,
    units_second,
    small_first,
    small_second,
):
    count = inputs.shape[0]
    seq_count = lax.axis_size(SEQ)
    dp_count = lax.axis_size(DP)
    devices = seq_count * dp_count
    seq_index = lax.axis_index(SEQ)
    group_len = count * seq_count
    first = seq_index * count
    starts_row = document_starts[0]
    group = HEADS // KV_HEADS
    scale = HEAD_DIM ** (-0.5)
    feature_width = joined_weight.shape[0]
    query_width = out_weight.shape[0]
    unit_width = units_weight.shape[0]

    small_rows, small_cols = small_params.shape
    small_block = jnp.pad(
        low(small_params), ((0, feature_width - small_rows), (0, 128 - small_cols))
    )
    packed = jnp.concatenate([low(joined_weight), low(out_weight), small_block], axis=1)
    packed = lax.all_gather(packed, ALL, axis=0, tiled=True)
    full_joined = packed[:, :QKV]
    full_out = packed[:, QKV : QKV + D]
    full_small = packed[:, QKV + D :].reshape(devices, feature_width, 128)
    full_small = full_small[:, :small_rows, :small_cols].reshape(devices * small_rows, small_cols)

    units_half = low(jnp.transpose(units_weight, (1, 0, 2)))
    mine = [units_half[2], units_half[0], units_half[1]]
    kinds = []
    for item in mine:
        slots = []
        for block in rotations(item, "zl"):
            slots += rotations(block, "c")
        kinds.append(jnp.concatenate(slots, axis=0))
    down_rows, gate_rows, up_rows = kinds

    back_blocks = gather_rows(output_grad)
    back_parts = [jnp.concatenate(blocks, axis=0) for blocks in back_blocks]

    gain_one, gain_two, bias = unpack_small(wide(full_small))
    rows = wide(inputs)
    scale_one = norm_scale(rows)
    normed_one = low(rows * scale_one * gain_one)
    mixed = jnp.dot(normed_one, full_joined, preferred_element_type=jnp.float32) + bias
    documents, blocks, offset = layout(starts_row, first, count)
    cosine, sine = turning(offset)
    query = low(rotate(mixed[:, :QW].reshape(count, HEADS, HEAD_DIM), cosine, sine))
    query = query.reshape(count, KV_HEADS, group, HEAD_DIM)
    keys_own = low(rotate(mixed[:, QW : QW + KW].reshape(count, KV_HEADS, HEAD_DIM), cosine, sine))
    values_own = low(mixed[:, QW + KW :])
    pair = jnp.concatenate([keys_own.reshape(count, KW), values_own], axis=1)
    pair_all = lax.all_gather(pair, SEQ, axis=0, tiled=True)
    keys = pair_all[:, :KW].reshape(group_len, KV_HEADS, HEAD_DIM)
    values = pair_all[:, KW:].reshape(group_len, KV_HEADS, HEAD_DIM)
    all_documents, all_blocks, unused_offset = layout(starts_row, 0, group_len)
    seen = (documents[:, None] == all_documents[None, :]) & (all_blocks[None, :] <= blocks[:, None])

    scores = jnp.einsum("qcgd,kcd->cgqk", query, keys, preferred_element_type=jnp.float32) * scale
    scores = jnp.where(seen, scores, -1e30)
    highest = jnp.max(scores, axis=-1, keepdims=True)
    total = jnp.sum(jnp.where(seen, jnp.exp(scores - highest), 0.0), axis=-1, keepdims=True)
    log_total = highest + jnp.log(total)
    weights = jnp.where(seen, jnp.exp(scores - log_total), 0.0)
    attended = jnp.einsum(
        "cgqk,kcd->qcgd", low(weights), values, preferred_element_type=jnp.float32
    )
    attended_low = low(attended.reshape(count, QW))
    middle = rows + jnp.dot(attended_low, full_out, preferred_element_type=jnp.float32)
    scale_two = norm_scale(middle)
    normed_two = low(middle * scale_two * gain_two)

    sent = jnp.concatenate(
        [
            normed_one.reshape(count, dp_count, seq_count, feature_width),
            attended_low.reshape(count, dp_count, seq_count, query_width),
        ],
        axis=3,
    )
    sent = jnp.transpose(sent, (2, 0, 1, 3)).reshape(
        seq_count * count, dp_count * (feature_width + query_width)
    )
    owned = lax.all_to_all(sent, SEQ, split_axis=0, concat_axis=0, tiled=True)
    owned = owned.reshape(group_len, dp_count, feature_width + query_width)
    normed_owned = owned[:, :, :feature_width].reshape(group_len, dp_count * feature_width)
    attended_owned = owned[:, :, feature_width:].reshape(group_len, dp_count * query_width)

    dot_rows = lambda left, right: jnp.einsum(
        "td,ud->tu", left, right, preferred_element_type=jnp.float32
    )
    dot_units = lambda left, right: jnp.einsum(
        "tu,ud->td", left, right, preferred_element_type=jnp.float32
    )
    normed_parts, hidden_parts, gate_parts, up_parts = [], [], [], []
    for part_blocks, back in zip(gather_rows(normed_two), back_parts):
        normed = jnp.concatenate(part_blocks, axis=0)
        pulled = dot_rows(back, down_rows)
        gate = dot_rows(normed, gate_rows)
        up = dot_rows(normed, up_rows)
        sigma = jax.nn.sigmoid(gate)
        active = gate * sigma
        normed_parts.append(normed)
        hidden_parts.append(low(active * up))
        gate_parts.append(low(pulled * up * sigma * (1.0 + gate * (1.0 - sigma))))
        up_parts.append(low(pulled * active))
    cut = lambda value: [value[i : i + count] for i in range(0, value.shape[0], count)]
    grad_terms = [
        cut(dot_units(gate, gate_rows) + dot_units(up, up_rows))
        for gate, up in zip(gate_parts, up_parts)
    ]
    normed_grad = scatter_rows(grad_terms)
    branch_terms = [cut(dot_units(hidden, down_rows)) for hidden in hidden_parts]
    branch_two = scatter_rows(branch_terms)
    block_output = low(middle + branch_two)

    total_over = lambda lefts, rights: sum(
        jnp.einsum("tu,td->ud", left, right, preferred_element_type=jnp.float32)
        for left, right in zip(lefts, rights)
    )
    units_term = jnp.stack(
        [
            total_over(gate_parts, normed_parts),
            total_over(up_parts, normed_parts),
            total_over(hidden_parts, back_parts),
        ]
    )
    low_count, core_count = lax.axis_size("zl"), lax.axis_size("c")
    units_term = units_term.reshape(3, low_count, core_count, unit_width, D)
    units_term = add_back([units_term[:, :, i] for i in range(core_count)], "c")
    units_grad = add_back([units_term[:, i] for i in range(low_count)], "zl")
    units_grad = jnp.transpose(units_grad, (1, 0, 2))

    weighted_two = gain_two * normed_grad
    middle_grad = (
        wide(output_grad)
        + scale_two * weighted_two
        - middle * scale_two**3 * jnp.mean(weighted_two * middle, axis=1, keepdims=True)
    )
    gain_two_grad = jnp.sum(normed_grad * middle * scale_two, axis=0)
    branch_grad = low(middle_grad)
    branch_all = lax.all_gather(branch_grad, SEQ, axis=0, tiled=True)
    attended_grad = low(
        jnp.einsum("td,ed->te", branch_grad, full_out, preferred_element_type=jnp.float32)
    ).reshape(count, KV_HEADS, group, HEAD_DIM)
    delta = jnp.einsum("qcgd,qcgd->cgq", wide(attended_grad), attended)
    pulled = jnp.einsum("qcgd,kcd->cgqk", attended_grad, values, preferred_element_type=jnp.float32)
    score_grad = low(weights * (pulled - delta[..., None]))
    query_grad = jnp.einsum(
        "cgqk,kcd->qcgd", score_grad, keys, preferred_element_type=jnp.float32
    )
    key_part = jnp.einsum("cgqk,qcgd->kcd", score_grad, query, preferred_element_type=jnp.float32)
    value_part = jnp.einsum(
        "cgqk,qcgd->kcd", low(weights), attended_grad, preferred_element_type=jnp.float32
    )
    pair_part = jnp.concatenate(
        [key_part.reshape(group_len, KW), value_part.reshape(group_len, KW)], axis=1
    )
    pair_sum = wide(lax.psum_scatter(low(pair_part), SEQ, scatter_dimension=0, tiled=True))
    query_pre = rotate_back(
        (query_grad * scale).reshape(count, HEADS, HEAD_DIM), cosine, sine
    ).reshape(count, QW)
    key_pre = rotate_back(
        (pair_sum[:, :KW] * scale).reshape(count, KV_HEADS, HEAD_DIM), cosine, sine
    ).reshape(count, KW)
    mixed_grad = low(jnp.concatenate([query_pre, key_pre, pair_sum[:, KW:]], axis=1))
    mixed_all = lax.all_gather(mixed_grad, SEQ, axis=0, tiled=True)
    bias_grad = jnp.sum(wide(mixed_grad), axis=0)
    normed_one_grad = jnp.einsum(
        "te,de->td", mixed_grad, full_joined, preferred_element_type=jnp.float32
    )
    weighted_one = gain_one * normed_one_grad
    input_grad = (
        middle_grad
        + scale_one * weighted_one
        - rows * scale_one**3 * jnp.mean(weighted_one * rows, axis=1, keepdims=True)
    )
    gain_one_grad = jnp.sum(normed_one_grad * rows * scale_one, axis=0)
    small_term = pack_small(gain_one_grad, gain_two_grad, bias_grad)
    small_grad = lax.psum_scatter(small_term, ALL, scatter_dimension=0, tiled=True)

    joined_term = jnp.einsum(
        "rc,re->ce", normed_owned, mixed_all, preferred_element_type=jnp.float32
    )
    outer_term = jnp.einsum(
        "rc,re->ce", attended_owned, branch_all, preferred_element_type=jnp.float32
    )
    joined_grad = wide(lax.psum_scatter(low(joined_term), DP, scatter_dimension=0, tiled=True))
    outer_grad = wide(lax.psum_scatter(low(outer_term), DP, scatter_dimension=0, tiled=True))
    joined = optimizer_step(
        joined_weight, joined_grad, joined_first, joined_second, 2.0 / math.sqrt(D), DECAY
    )
    outer = optimizer_step(
        out_weight, outer_grad, out_first, out_second, 2.0 / math.sqrt(QW // 64), DECAY
    )
    units_new = optimizer_step(
        units_weight, units_grad, units_first, units_second, 2.0 / math.sqrt(D), DECAY
    )
    small = optimizer_step(small_params, small_grad, small_first, small_second, 0.5, 0.0)
    return (block_output, input_grad) + joined + outer + units_new + small


def solution(mesh):
    groups, members = mesh.devices.shape
    fine = Mesh(mesh.devices.reshape(groups // 2, 2, members // 4, 2, 2), ALL)
    flat, cube = P(ALL, None), P(ALL, None, None)
    in_specs = (flat, flat, P(DP, None), flat, flat, cube, flat) + (flat,) * 4 + (cube,) * 2 + (flat,) * 2
    out_specs = (flat,) * 10 + (cube,) * 4 + (flat,) * 4
    return jax.shard_map(body, mesh=fine, in_specs=in_specs, out_specs=out_specs, check_vma=False)
```

```python
import math

import jax
import jax.numpy as jnp
from jax import lax
from jax.experimental import pallas as pl
from jax.experimental.pallas import tpu as pltpu
from jax.sharding import Mesh
from jax.sharding import PartitionSpec as P

D = 1536
HEADS = 12
KV_HEADS = 2
HEAD_DIM = 128
FF = 8960
BLOCK = 256
STEP = 5
QW = 1536
KW = 256
QKV = 2048


NORM_EPS = 1e-06
ROPE_BASE = 1000000.0
BETA_ONE = 0.9
BETA_TWO = 0.95
ADAM_EPS = 1e-08
DECAY = 0.1


DP = ("zh", "zl")
SEQ = ("y", "x", "c")
ALL = DP + SEQ


def low(value):
    return value.astype(jnp.bfloat16)


def wide(value):
    return value.astype(jnp.float32)


def after(value, *others):
    return lax.optimization_barrier((value,) + others)[0]


def shift(value, axis, step):
    count = lax.axis_size(axis)
    return lax.ppermute(value, axis, [(i, (i + step) % count) for i in range(count)])


def rotations(value, axis):
    return [value] + [shift(value, axis, step) for step in range(1, lax.axis_size(axis))]


def plane_steps():
    return [(j, i) for j in range(lax.axis_size("y")) for i in range(lax.axis_size("x"))]


def plane_shift(value, down, right):
    tall, broad = lax.axis_size("y"), lax.axis_size("x")
    pairs = [
        (j * broad + i, (j + down) % tall * broad + (i + right) % broad)
        for j in range(tall)
        for i in range(broad)
    ]
    return lax.ppermute(value, ("y", "x"), pairs)


def plane_pieces(value, dim, cut):
    across, along = rotations(value, "x"), rotations(value, "y")
    size = value.shape[dim]
    pieces = []
    for j, i in plane_steps():
        if j == 0 or i == 0:
            pieces.append((across[i] if j == 0 else along[j],))
        else:
            head = lax.slice_in_dim(across[i], 0, cut, axis=dim)
            tail = lax.slice_in_dim(along[j], cut, size, axis=dim)
            pieces.append((shift(head, "y", j), shift(tail, "x", i)))
    return pieces


def seq_gather_small(value):
    mine = [value] + [plane_shift(value, j, i) for j, i in plane_steps()[1:]]
    return jnp.concatenate(rotations(jnp.concatenate(mine, axis=0), "c"), axis=0)


def seq_scatter_small(value, rows):
    part = value.shape[0] // lax.axis_size("c")
    total = add_back(
        [value[step * part : (step + 1) * part] for step in range(lax.axis_size("c"))], "c"
    )
    result = [total[:rows]]
    for number, (j, i) in enumerate(plane_steps()[1:], 1):
        term = low(total[number * rows : (number + 1) * rows])
        result.append(plane_shift(term, -j, -i))
    return result


def seq_sources():
    tall, broad, cores = (lax.axis_size(name) for name in SEQ)
    row, col, core = (lax.axis_index(name) for name in SEQ)
    return [
        ((row - j) % tall * broad + (col - i) % broad) * cores + (core - k) % cores
        for k in range(cores)
        for j, i in plane_steps()
    ]


def wanted_columns(columns, width):
    tall, broad, cores = (lax.axis_size(name) for name in SEQ)
    row, col, core = (lax.axis_index(name) for name in SEQ)
    depth, z = lax.axis_size(DP), lax.axis_index(DP)
    place = jnp.arange(columns, dtype=jnp.int32)
    inner, rest = place % width, place // width
    dp_step, rest = rest % depth, rest // depth
    c_step, rest = rest % cores, rest // cores
    x_step, y_step = rest % broad, rest // broad
    seq = ((row - y_step) % tall * broad + (col - x_step) % broad) * cores + (core - c_step) % cores
    source = ((z - dp_step) % depth * (tall * broad * cores) + seq) * width + inner
    return low(jnp.arange(columns, dtype=jnp.int32)[:, None] == source[None, :])


def token_gather(value, order):
    result = []
    for number, block in enumerate(rotations(order(1, value), "zh")):
        block = value if number == 0 else order(2, block)
        if number % 2 == 0:
            grid = [rotations(item, "y") for item in rotations(block, "x")]
            grid = [[grid[i][j] for i in range(len(grid))] for j in range(len(grid[0]))]
        else:
            grid = [rotations(item, "x") for item in rotations(block, "y")]
        result.append([item for line in grid for item in line])
    return result


def add_back(blocks, axis, early=(), log=None):
    total = wide(blocks[0])
    for step in range(1, len(blocks)):
        got = shift(low(blocks[step]), axis, -step)
        if log is not None:
            log.append(got)
        total = total + wide(after(got, *early) if early else got)
    return total


def token_scatter(parts, early=()):
    across, along = lax.axis_size("x"), lax.axis_size("y")
    lines, first, second = [], [], []
    for number, blocks in reversed(list(enumerate(parts))):
        grid = [blocks[j * across : (j + 1) * across] for j in range(along)]
        axes = ("y", "x") if number % 2 == 0 else ("x", "y")
        if number % 2 == 0:
            grid = [list(column) for column in zip(*grid)]
        sums = [add_back(line, axes[0], log=first) for line in grid]
        lines.append(add_back(sums, axes[1], early, log=second))
    lines = lines[::-1]
    last = lines.pop()
    sent = shift(low(last), "zh", -len(lines))
    return lines + [last], add_back(lines, "zh"), sent, first, second


VMEM_BYTES = 56 * 2**20
ANYWHERE = pl.BlockSpec(memory_space=pl.ANY)
SCALARS = pl.BlockSpec(memory_space=pltpu.SMEM)


def projection_pieces(block):
    rows, columns = block.shape
    depth = lax.axis_size(DP)
    tall, broad, cores = (lax.axis_size(name) for name in SEQ)
    if rows % 16:
        whole = lax.all_gather(block, ALL, axis=0, tiled=True)
        return ([whole], None, None), whole, whole
    line = rotations(block, DP)
    cut = columns // 2
    z = lax.axis_index(DP)
    z_sources = [(z - k) % depth for k in range(depth)]
    sources = seq_sources()
    own = plane_pieces(jnp.stack(line), 2, cut)
    pieces, plan, targets = [], [], []
    for k in range(cores):
        for number, piece in enumerate(own):
            for part, value in enumerate(piece):
                pieces.append(value if k == 0 else shift(value, "c", k))
                place = (part * cut, cut) if len(piece) == 2 else (0, columns)
                plan.append([(slot, len(targets) + slot, place) for slot in range(depth)])
                seq = sources[k * len(own) + number]
                targets += [(z_sources[slot] * tall * broad * cores + seq) * rows for slot in range(depth)]
    return (pieces, plan, jnp.stack(targets).astype(jnp.int32)), line[-1], own[-1][-1]


def start_pieces(plan, where_ref, pieces, whole, sems):
    if plan is None:
        copies = [pltpu.make_async_copy(pieces[0], whole, sems.at[0])]
    else:
        copies = []
        for piece, jobs in zip(pieces, plan):
            for slot, target, columns in jobs:
                first = pl.multiple_of(where_ref[target], 16)
                copies.append(
                    pltpu.make_async_copy(
                        piece.at[slot],
                        whole.at[pl.ds(first, piece.shape[1]), pl.ds(*columns)],
                        sems.at[len(copies)],
                    )
                )
    for copy in copies:
        copy.start()
    return copies


def call_with_pieces(kernel, projection, operands, outs, name, micros):
    pieces, plan, targets = projection
    count = 1 if plan is None else sum(len(jobs) for jobs in plan)
    if targets is None:
        targets = jnp.zeros((8,), jnp.int32)
    size = len(operands)

    def run(*refs):
        where_ref, rest = refs[0], refs[1:]
        whole, sems = rest[-2], rest[-1]
        copies = start_pieces(plan, where_ref, rest[size : size + len(pieces)], whole, sems)

        def ready():
            for copy in copies:
                copy.wait()

        kernel(ready, whole, *rest[:size], *rest[size + len(pieces) : -2])

    return pl.pallas_call(
        run,
        out_shape=outs,
        in_specs=[SCALARS]
        + [pl.BlockSpec(memory_space=pltpu.VMEM)] * size
        + [ANYWHERE] * len(pieces),
        scratch_shapes=[
            pltpu.VMEM((D, QKV), jnp.bfloat16),
            pltpu.SemaphoreType.DMA((count,)),
        ],
        compiler_params=pltpu.CompilerParams(vmem_limit_bytes=VMEM_BYTES),
        cost_estimate=cost(micros),
        name=name,
    )(targets, *operands, *pieces)


def local_call(kernel, operands, outs, name, micros, scratch=()):
    return pl.pallas_call(
        kernel,
        out_shape=outs,
        scratch_shapes=list(scratch),
        compiler_params=pltpu.CompilerParams(vmem_limit_bytes=VMEM_BYTES),
        cost_estimate=cost(micros),
        name=name,
    )(*operands)


def cost(micros):
    return pl.CostEstimate(flops=int(micros * 1.1e9), bytes_accessed=0, transcendentals=0)


def shaped(shape, dtype):
    return jax.ShapeDtypeStruct(shape, dtype)


def dot(left, right, left_dim, right_dim):
    return lax.dot_general(
        left, right, (((left_dim,), (right_dim,)), ((), ())), preferred_element_type=jnp.float32
    )


def swap_halves(values):
    return pltpu.roll(values, HEAD_DIM // 2, 1)


def turned(values, cosine, sine):
    return values * cosine + swap_halves(values) * sine


def turned_back(grads, cosine, sine):
    return grads * cosine + swap_halves(grads * sine)


def front_kernel(
    ready, whole, rows_ref, gain_ref, bias_ref, cosine_ref, sine_ref, normed_ref, query_ref, pair_ref
):
    rows = wide(rows_ref[...])
    normed_ref[...] = low(rows * norm_scale(rows) * gain_ref[...])
    normed = normed_ref[...]
    cosine, sine = cosine_ref[...], sine_ref[...]
    ready()
    for first in range(0, QKV, 256):
        mixed = dot(normed, whole[:, first : first + 256], 1, 0) + bias_ref[:, first : first + 256]
        for start in (0, HEAD_DIM):
            part = mixed[:, start : start + HEAD_DIM]
            column = first + start
            if column < QW + KW:
                part = turned(part, cosine, sine)
            if column < QW:
                query_ref[:, column : column + HEAD_DIM] = low(part)
            else:
                pair_ref[:, column - QW : column - QW + HEAD_DIM] = low(part)


TOGETHER = 2


def head_views(step):
    heads = step * TOGETHER
    kind = heads // (HEADS // KV_HEADS)
    queries = [pl.ds(pl.multiple_of((heads + i) * HEAD_DIM, HEAD_DIM), HEAD_DIM) for i in range(TOGETHER)]
    keys = pl.ds(pl.multiple_of(kind * HEAD_DIM, HEAD_DIM), HEAD_DIM)
    values = pl.ds(pl.multiple_of(KW + kind * HEAD_DIM, HEAD_DIM), HEAD_DIM)
    return queries, keys, values


def visible(key_marks_ref, query_marks_ref):
    seen = (key_marks_ref[:, 0:1] == query_marks_ref[0:1, :]) & (
        key_marks_ref[:, 1:2] <= query_marks_ref[1:2, :]
    )
    return jnp.concatenate([jnp.where(seen, 0.0, -1e30)] * TOGETHER, axis=1)


def probabilities(keys, query, hidden):
    scores = dot(keys, query, 1, 1) * (HEAD_DIM**-0.5) + hidden
    grown = jnp.exp(scores - jnp.max(scores, axis=0, keepdims=True))
    return grown * (1.0 / jnp.sum(grown, axis=0, keepdims=True))


def attend_kernel(
    query_ref, pair_ref, key_marks_ref, query_marks_ref, rows_ref, out_ref, gain_ref,
    attended_ref, middle_ref, normed_ref, hidden_ref,
):
    hidden_ref[...] = visible(key_marks_ref, query_marks_ref)

    def step(index, unused):
        queries, keys, values = head_views(index)
        query = jnp.concatenate([query_ref[:, view] for view in queries], axis=0)
        weights = low(probabilities(pair_ref[:, keys], query, hidden_ref[...]))
        result = low(dot(weights, pair_ref[:, values], 0, 0))
        count = query_ref.shape[0]
        for i, view in enumerate(queries):
            attended_ref[:, view] = result[i * count : (i + 1) * count]
        return unused

    lax.fori_loop(0, HEADS // TOGETHER, step, 0)
    middle = wide(rows_ref[...]) + dot(attended_ref[...], out_ref[...], 1, 0)
    middle_ref[...] = middle
    normed_ref[...] = low(middle * norm_scale(middle) * gain_ref[...])


def attend_back_kernel(
    normed_grad_ref, received_ref, middle_ref, back_ref, gain_ref, out_ref, query_ref, pair_ref,
    key_marks_ref, query_marks_ref, cosine_ref, sine_ref,
    middle_grad_ref, branch_ref, mixed_ref, pair_grad_ref, gain_grad_ref,
    hidden_ref, attended_grad_ref,
):
    hidden_ref[...] = visible(key_marks_ref, query_marks_ref)
    normed_grad = normed_grad_ref[...] + wide(received_ref[...])
    middle = middle_ref[...]
    scale = norm_scale(middle)
    weighted = gain_ref[...] * normed_grad
    middle_grad = (
        wide(back_ref[...])
        + scale * weighted
        - middle * scale**3 * jnp.mean(weighted * middle, axis=1, keepdims=True)
    )
    gain_grad_ref[...] = jnp.sum(normed_grad * middle * scale, axis=0, keepdims=True)
    middle_grad_ref[...] = middle_grad
    branch_ref[...] = low(middle_grad)
    attended_grad_ref[...] = low(dot(branch_ref[...], out_ref[...], 1, 1))
    pair_grad_ref[...] = jnp.zeros_like(pair_grad_ref)
    cosine, sine = cosine_ref[...], sine_ref[...]

    def step(index, unused):
        queries, keys, values = head_views(index)
        query = jnp.concatenate([query_ref[:, view] for view in queries], axis=0)
        grad = jnp.concatenate([attended_grad_ref[:, view] for view in queries], axis=0)
        key = pair_ref[:, keys]
        weights = probabilities(key, query, hidden_ref[...])
        pulled = dot(pair_ref[:, values], grad, 1, 1)
        delta = jnp.sum(weights * pulled, axis=0, keepdims=True)
        score_grad = low(weights * (pulled - delta))
        query_grad = dot(score_grad, key, 0, 0) * (HEAD_DIM**-0.5)
        count = query_ref.shape[0]
        for i, view in enumerate(queries):
            mixed_ref[:, view] = low(
                turned_back(query_grad[i * count : (i + 1) * count], cosine, sine)
            )
        pair_grad_ref[:, keys] += dot(score_grad, query, 1, 0) * (HEAD_DIM**-0.5)
        pair_grad_ref[:, values] += dot(low(weights), grad, 1, 0)
        return unused

    lax.fori_loop(0, HEADS // TOGETHER, step, 0)


def query_kernel(ready, whole, mixed_ref, normed_grad_ref, bias_grad_ref, pair_rows_ref):
    mixed = mixed_ref[...]
    bias_grad_ref[...] = jnp.sum(wide(mixed), axis=0, keepdims=True)
    ready()
    normed_grad_ref[...] = dot(mixed, whole[:, :QW], 1, 1)
    pair_rows_ref[...] = whole[:, QW:]


def finish_kernel(count, *refs):
    terms, refs = refs[:count], refs[count:]
    cosine_ref, sine_ref, part_ref, pair_rows_ref, rows_ref, gain_ref, middle_grad_ref = refs[:7]
    pair_ref, input_grad_ref, gain_grad_ref, bias_grad_ref = refs[7:]
    total = terms[0][...]
    for term in terms[1:]:
        total = total + wide(term[...])
    for first in range(0, 2 * KW, HEAD_DIM):
        part = total[:, first : first + HEAD_DIM]
        if first < KW:
            part = turned_back(part, cosine_ref[...], sine_ref[...])
        pair_ref[:, first : first + HEAD_DIM] = low(part)
    rows = wide(rows_ref[...])
    scale = norm_scale(rows)
    pair = pair_ref[...]
    bias_grad_ref[...] = jnp.sum(wide(pair), axis=0, keepdims=True)
    normed_grad = part_ref[...] + dot(pair, pair_rows_ref[...], 1, 1)
    weighted = gain_ref[...] * normed_grad
    input_grad_ref[...] = (
        middle_grad_ref[...]
        + scale * weighted
        - rows * scale**3 * jnp.mean(weighted * rows, axis=1, keepdims=True)
    )
    gain_grad_ref[...] = jnp.sum(normed_grad * rows * scale, axis=0, keepdims=True)


def unit_tile(units):
    return units // 2 if units % 32 == 0 else units


def units_kernel(size, *refs):
    normed_refs, back_refs, units_ref = refs[:size], refs[size : 2 * size], refs[2 * size]
    hidden_ref, gate_ref, up_ref, *out_refs = refs[2 * size + 1 : 3 * size + 4]
    normed_rows, back_rows, total = refs[3 * size + 4 :]
    count = normed_refs[0].shape[0]
    step = pl.program_id(0)

    @pl.when(step == 0)
    def _():
        for number in range(size):
            view = slice(number * count, (number + 1) * count)
            normed_rows[view, :] = normed_refs[number][...]
            back_rows[view, :] = back_refs[number][...]
        total[...] = jnp.zeros_like(total)

    normed = normed_rows[...]
    gate = dot(units_ref[0], normed, 1, 1)
    up = dot(units_ref[1], normed, 1, 1)
    pulled = dot(units_ref[2], back_rows[...], 1, 1)
    sigma = jax.nn.sigmoid(gate)
    active = gate * sigma
    hidden_ref[...] = low(active * up)
    gate_grad = low(pulled * up * sigma * (1.0 + gate * (1.0 - sigma)))
    up_grad = low(pulled * active)
    gate_ref[...] = gate_grad
    up_ref[...] = up_grad
    total[...] += dot(gate_grad, units_ref[0], 0, 0) + dot(up_grad, units_ref[1], 0, 0)

    @pl.when(step == pl.num_programs(0) - 1)
    def _():
        for number in range(size):
            out_refs[number][...] = low(total[number * count : (number + 1) * count])


def whole_block(shape):
    return pl.BlockSpec(shape, lambda i: (0,) * len(shape))


def units_forward(normed, back, units):
    size, count = len(normed), normed[0].shape[0]
    tile, tokens = unit_tile(units.shape[1]), size * count
    token_block = whole_block((count, D))
    by_unit = pl.BlockSpec((tile, tokens), lambda i: (i, 0))
    return pl.pallas_call(
        lambda *refs: units_kernel(size, *refs),
        grid=(units.shape[1] // tile,),
        in_specs=[token_block] * (2 * size) + [pl.BlockSpec((3, tile, D), lambda i: (0, i, 0))],
        out_specs=[by_unit] * 3 + [token_block] * size,
        out_shape=[shaped((units.shape[1], tokens), jnp.bfloat16)] * 3
        + [shaped((count, D), jnp.bfloat16)] * size,
        scratch_shapes=[
            pltpu.VMEM((tokens, D), jnp.bfloat16),
            pltpu.VMEM((tokens, D), jnp.bfloat16),
            pltpu.VMEM((tokens, D), jnp.float32),
        ],
        compiler_params=pltpu.CompilerParams(vmem_limit_bytes=VMEM_BYTES),
        cost_estimate=cost(10),
        name="units_forward",
    )(*normed, *back, units)


def gradient_kernel(parts, size, *refs):
    by_unit, refs = refs[: 3 * parts], refs[3 * parts :]
    normed_refs, back_refs, out_ref = refs[:size], refs[size : 2 * size], refs[2 * size]
    normed_rows, back_rows = refs[2 * size + 1 :]
    count = normed_refs[0].shape[0]

    @pl.when(pl.program_id(0) == 0)
    def _():
        for number in range(size):
            view = slice(number * count, (number + 1) * count)
            normed_rows[view, :] = normed_refs[number][...]
            back_rows[view, :] = back_refs[number][...]

    for kind, rows in ((0, normed_rows), (1, normed_rows), (2, back_rows)):
        place = (kind + 1) % 3
        values = [by_unit[3 * part + place][...] for part in range(parts)]
        out_ref[kind] = low(dot(jnp.concatenate(values, axis=1), rows[...], 1, 0))


def units_gradient(parts, normed, back):
    units, tokens = parts[0][0].shape
    size, count = len(normed), normed[0].shape[0]
    tile = unit_tile(units)
    token_block = whole_block((count, D))
    return pl.pallas_call(
        lambda *refs: gradient_kernel(len(parts), size, *refs),
        grid=(units // tile,),
        in_specs=[pl.BlockSpec((tile, tokens), lambda i: (i, 0))] * (3 * len(parts))
        + [token_block] * (2 * size),
        out_specs=pl.BlockSpec((3, tile, D), lambda i: (0, i, 0)),
        out_shape=shaped((3, units, D), jnp.bfloat16),
        scratch_shapes=[
            pltpu.VMEM((size * count, D), jnp.bfloat16),
            pltpu.VMEM((size * count, D), jnp.bfloat16),
        ],
        compiler_params=pltpu.CompilerParams(vmem_limit_bytes=VMEM_BYTES),
        cost_estimate=cost(11),
        name="units_gradient",
    )(*[item for part in parts for item in part], *normed, *back)


def branch_kernel(parts, *refs):
    hidden_refs, units_ref, out_refs, total = refs[:parts], refs[parts], refs[parts + 1 : -1], refs[-1]
    step = pl.program_id(0)

    @pl.when(step == 0)
    def _():
        total[...] = jnp.zeros_like(total)

    hidden = jnp.concatenate([ref[...] for ref in hidden_refs], axis=1)
    total[...] += dot(hidden, units_ref[0], 0, 0)

    @pl.when(step == pl.num_programs(0) - 1)
    def _():
        count = out_refs[0].shape[0]
        for number, out_ref in enumerate(out_refs):
            out_ref[...] = low(total[number * count : (number + 1) * count])


def units_branch(hidden, units, count):
    tokens = sum(item.shape[1] for item in hidden)
    tile = unit_tile(units.shape[1])
    size = tokens // count
    return pl.pallas_call(
        lambda *refs: branch_kernel(len(hidden), *refs),
        grid=(units.shape[1] // tile,),
        in_specs=[pl.BlockSpec((tile, item.shape[1]), lambda i: (i, 0)) for item in hidden]
        + [pl.BlockSpec((1, tile, D), lambda i: (2, i, 0))],
        out_specs=[whole_block((count, D))] * size,
        out_shape=[shaped((count, D), jnp.bfloat16)] * size,
        scratch_shapes=[pltpu.VMEM((tokens, D), jnp.float32)],
        compiler_params=pltpu.CompilerParams(vmem_limit_bytes=VMEM_BYTES),
        cost_estimate=cost(5),
        name="units_branch",
    )(*hidden, units)


def weight_kernel(plan, *refs):
    count = max(job[0] for job in plan) + 1
    lefts, rights = refs[:count], refs[count:-2]
    kept_ref, sent_ref = refs[-2:]
    left, right = [], []
    for number, first, size in plan:
        left.append(lefts[number][first : first + size, :])
        right.append(rights[len(right)][...])
    total = dot(jnp.concatenate(left, axis=0), jnp.concatenate(right, axis=0), 0, 0)
    half = total.shape[0] // 2
    kept_ref[...] = total[:half]
    sent_ref[...] = low(total[half:])


def weight_term(lefts, pieces, name):
    plan, rights = [], []
    for number, piece in enumerate(pieces):
        first = 0
        for value in piece:
            plan.append((number, first, value.shape[0]))
            first += value.shape[0]
            rights.append(value)
    shape = (lefts[0].shape[1] // 2, rights[0].shape[1])
    kept, sent = local_call(
        lambda *refs: weight_kernel(plan, *refs),
        list(lefts) + rights,
        [shaped(shape, jnp.float32), shaped(shape, jnp.bfloat16)],
        name,
        3,
    )
    return kept, shift(sent, "c", -1)


def dp_scatter(total, early=()):
    depth = lax.axis_size(DP)
    width = total.shape[0] // depth
    return add_back([total[i * width : (i + 1) * width] for i in range(depth)], DP, early)


def norm_scale(rows):
    return lax.rsqrt(jnp.mean(rows * rows, axis=1, keepdims=True) + NORM_EPS)


def unpack_small(small):
    gain_cols = D // KW
    group = HEADS // KV_HEADS
    gain_one = small[:, :gain_cols].reshape(D)
    gain_two = small[:, gain_cols : 2 * gain_cols].reshape(D)
    query_bias = small[:, 2 * gain_cols : 2 * gain_cols + group].reshape(KV_HEADS, HEAD_DIM, group)
    query_bias = jnp.transpose(query_bias, (0, 2, 1)).reshape(QW)
    key_bias = small[:, 2 * gain_cols + group]
    value_bias = small[:, 2 * gain_cols + group + 1]
    return (gain_one, gain_two, jnp.concatenate([query_bias, key_bias, value_bias]))


def pack_small(gain_one, gain_two, bias):
    gain_cols = D // KW
    group = HEADS // KV_HEADS
    query_part = jnp.transpose(bias[:QW].reshape(KV_HEADS, group, HEAD_DIM), (0, 2, 1)).reshape(
        KW, group
    )
    return jnp.concatenate(
        [
            gain_one.reshape(KW, gain_cols),
            gain_two.reshape(KW, gain_cols),
            query_part,
            bias[QW : QW + KW][:, None],
            bias[QW + KW :][:, None],
        ],
        axis=1,
    )


def layout(starts_row, places):
    before = starts_row[None, :] <= places[:, None]
    documents = jnp.sum(before.astype(jnp.int32), axis=1) - 1
    begin = jnp.max(jnp.where(before, starts_row[None, :], 0), axis=1)
    offset = places - begin
    return (documents, offset // BLOCK, offset)


def turning(offset):
    half = HEAD_DIM // 2
    frequency = ROPE_BASE ** (-(2.0 * jnp.arange(half, dtype=jnp.float32)) / HEAD_DIM)
    angle = offset.astype(jnp.float32)[:, None] * frequency[None, :]
    angle = jnp.concatenate([angle, angle], axis=1)
    return (jnp.cos(angle)[:, None, :], jnp.sin(angle)[:, None, :])


def optimizer_step(weight, grad, first, second, rate, decay):
    first = BETA_ONE * first + (1.0 - BETA_ONE) * grad
    second = BETA_TWO * second + (1.0 - BETA_TWO) * grad * grad
    fixed_first = first / (1.0 - BETA_ONE**STEP)
    fixed_second = second / (1.0 - BETA_TWO**STEP)
    weight = weight - rate * (fixed_first / (jnp.sqrt(fixed_second) + ADAM_EPS) + decay * weight)
    return (weight, first, second, weight.astype(jnp.bfloat16))


def body(
    inputs,
    output_grad,
    document_starts,
    joined_weight,
    out_weight,
    units_weight,
    small_params,
    joined_first,
    joined_second,
    out_first,
    out_second,
    units_first,
    units_second,
    small_first,
    small_second,
):
    count = inputs.shape[0]
    seq_count = lax.axis_size(SEQ)
    devices = seq_count * lax.axis_size(DP)
    seq_index = lax.axis_index(SEQ)
    group_len = count * seq_count
    first = seq_index * count
    starts_row = document_starts[0]
    feature_width = joined_weight.shape[0]
    unit_width = units_weight.shape[0]

    device = lax.axis_index(ALL)
    small_rows, small_cols = small_params.shape
    vector = lax.dynamic_update_slice_in_dim(
        jnp.zeros((devices * small_rows, small_cols), jnp.float32),
        wide(low(small_params)),
        device * small_rows,
        0,
    )
    vector = jnp.concatenate(unpack_small(vector)).reshape(1, -1)
    for axis in ("c", "x", "y", DP):
        vector = sum(rotations(vector, axis))
    gain_one, gain_two, bias = vector[:, :D], vector[:, D : 2 * D], vector[:, 2 * D :]

    projection, along_dp, at_last = projection_pieces(low(joined_weight))
    full_out = lax.all_gather(low(out_weight), ALL, axis=0, tiled=True)
    documents, blocks, offset = layout(starts_row, first + jnp.arange(count, dtype=jnp.int32))
    cosine, sine = turning(offset)
    cosine, sine = cosine[:, 0], sine[:, 0]
    sine = jnp.concatenate([-sine[:, : HEAD_DIM // 2], sine[:, HEAD_DIM // 2 :]], axis=1)
    sources = seq_sources()
    places = jnp.concatenate([i * count + jnp.arange(count, dtype=jnp.int32) for i in sources])
    all_documents, all_blocks, unused_offset = layout(starts_row, places)
    key_marks = jnp.stack([all_documents, all_blocks], axis=1)
    query_marks = jnp.stack([documents, blocks], axis=0)
    wanted = wanted_columns(D, feature_width)

    sharing = ("zl", "c")
    units_half = after(low(units_weight), along_dp)
    units_all = lax.all_gather(units_half, sharing, axis=0, tiled=True)
    units_all = jnp.transpose(units_all, (1, 0, 2))

    normed_one, query, pair = call_with_pieces(
        front_kernel,
        projection,
        [inputs, gain_one, bias, cosine, sine],
        [
            shaped((count, D), jnp.bfloat16),
            shaped((count, QW), jnp.bfloat16),
            shaped((count, 2 * KW), jnp.bfloat16),
        ],
        "front",
        6,
    )
    pair_all = seq_gather_small(pair)

    back_blocks = token_gather(
        output_grad,
        lambda stage, value: after(value, along_dp) if stage == 1 else after(value, at_last),
    )

    attended, middle, normed_two = local_call(
        attend_kernel,
        [after(query, *back_blocks[0], *back_blocks[-1]), pair_all, key_marks, query_marks, inputs, full_out, gain_two],
        [
            shaped((count, QW), jnp.bfloat16),
            shaped((count, D), jnp.float32),
            shaped((count, D), jnp.bfloat16),
        ],
        "attend",
        12,
        [pltpu.VMEM((group_len, TOGETHER * count), jnp.float32)],
    )

    steps = plane_steps()
    normed_sent = low(dot(after(normed_one, normed_two), wanted, 1, 0))
    attended_sent = low(dot(attended, wanted, 1, 0))
    chip_width = D // len(steps)
    normed_owned, attended_owned = [], []
    for number, (j, i) in enumerate(steps):
        view = slice(number * chip_width, (number + 1) * chip_width)
        both = [normed_sent[:, view], attended_sent[:, view]]
        if number:
            moved = plane_shift(jnp.concatenate(both, axis=1), -j, -i)
            both = [moved[:, :chip_width], moved[:, chip_width:]]
        normed_owned.append(both[0])
        attended_owned.append(both[1])

    normed_blocks = token_gather(normed_two, lambda stage, value: value)
    unit_parts = [
        units_forward(normed, back, units_all)
        for normed, back in zip(normed_blocks, back_blocks)
    ]
    grad_terms = [part[3:] for part in unit_parts]
    hidden_parts = [part[0] for part in unit_parts]
    units_term = units_gradient(
        [part[:3] for part in unit_parts],
        [block for line in normed_blocks for block in line],
        [block for line in back_blocks for block in line],
    )
    units_grad = wide(
        lax.psum_scatter(
            jnp.transpose(units_term, (1, 0, 2)), sharing, scatter_dimension=0, tiled=True
        )
    )
    plane_sums, normed_grad_own, normed_grad_received, grads_first, unused = token_scatter(grad_terms)
    branch_terms = units_branch(hidden_parts, after(units_all, units_term, *grads_first), count)
    normed_grad_own = after(normed_grad_own, *branch_terms)
    branch_terms = [after(item, *plane_sums) for item in branch_terms]
    line = len(normed_blocks[0])
    branch_terms = [branch_terms[k : k + line] for k in range(0, len(branch_terms), line)]
    unused, branch_own, branch_received, branch_first, branch_second = token_scatter(branch_terms)
    block_output = low(middle + branch_own + wide(branch_received))

    middle = after(middle, *normed_owned, *attended_owned)
    middle_grad, branch_grad, mixed_grad, pair_grad, gain_two_grad = local_call(
        attend_back_kernel,
        [
            normed_grad_own,
            normed_grad_received,
            middle,
            output_grad,
            gain_two,
            full_out,
            query,
            pair_all,
            key_marks,
            query_marks,
            cosine,
            sine,
        ],
        [
            shaped((count, D), jnp.float32),
            shaped((count, D), jnp.bfloat16),
            shaped((count, QW), jnp.bfloat16),
            shaped((group_len, 2 * KW), jnp.float32),
            shaped((1, D), jnp.float32),
        ],
        "attend_back",
        16,
        [
            pltpu.VMEM((group_len, TOGETHER * count), jnp.float32),
            pltpu.VMEM((count, QW), jnp.bfloat16),
        ],
    )
    pair_terms = seq_scatter_small(pair_grad, count)
    query_pieces = plane_pieces(mixed_grad, 0, count // 2)
    branch_pieces = plane_pieces(branch_grad, 0, count // 2)
    normed_grad_part, query_bias_grad, pair_rows = call_with_pieces(
        query_kernel,
        projection,
        [mixed_grad],
        [
            shaped((count, D), jnp.float32),
            shaped((1, QW), jnp.float32),
            shaped((D, 2 * KW), jnp.bfloat16),
        ],
        "query_back",
        7,
    )
    straight = [piece[0] for piece in query_pieces + branch_pieces if len(piece) == 1]
    pair_terms[0] = after(pair_terms[0], *straight, *branch_first)
    pair_mixed, input_grad, gain_one_grad, pair_bias_grad = local_call(
        lambda *refs: finish_kernel(len(pair_terms), *refs),
        pair_terms
        + [cosine, sine, normed_grad_part, pair_rows, inputs, gain_one, middle_grad],
        [
            shaped((count, 2 * KW), jnp.bfloat16),
            shaped((count, D), jnp.float32),
            shaped((1, D), jnp.float32),
            shaped((1, 2 * KW), jnp.float32),
        ],
        "finish",
        4,
    )
    pair_pieces = [(pair_mixed,)] + [(plane_shift(pair_mixed, j, i),) for j, i in steps[1:]]
    vector = jnp.concatenate([gain_one_grad, gain_two_grad, query_bias_grad, pair_bias_grad], axis=1)
    vector = sum(rotations(vector, "c"))
    attended_owned[0] = after(attended_owned[0], vector)
    kept, got = weight_term(attended_owned, branch_pieces, "out_weights")
    vector = sum(rotations(vector, "x"))
    normed_owned[0] = after(normed_owned[0], got, vector, *branch_second)
    outer_grad = dp_scatter(kept + wide(got))
    query_kept, query_got = weight_term(normed_owned, query_pieces, "query_weights")
    vector = sum(rotations(vector, "y"))
    pair_pieces[0] = (after(pair_mixed, query_got, vector),)
    pair_kept, pair_got = weight_term(normed_owned, pair_pieces, "pair_weights")
    units_new = optimizer_step(
        units_weight, units_grad, units_first, units_second, 2.0 / math.sqrt(D), DECAY
    )
    joined_grad = dp_scatter(
        jnp.concatenate([query_kept + wide(query_got), pair_kept + wide(pair_got)], axis=1),
        [units_new[3]],
    )
    vector = sum(rotations(vector, DP)).reshape(-1)
    small_grad = pack_small(vector[:D], vector[D : 2 * D], vector[2 * D :])
    small_grad = lax.dynamic_slice_in_dim(small_grad, device * small_rows, small_rows, 0)

    joined = optimizer_step(
        joined_weight, joined_grad, joined_first, joined_second, 2.0 / math.sqrt(D), DECAY
    )
    outer = optimizer_step(
        out_weight, outer_grad, out_first, out_second, 2.0 / math.sqrt(QW // 64), DECAY
    )
    small = optimizer_step(small_params, small_grad, small_first, small_second, 0.5, 0.0)
    return (block_output, input_grad) + joined + outer + units_new + small


def solution(mesh):
    groups, members = mesh.devices.shape
    fine = Mesh(mesh.devices.reshape(groups // 2, 2, members // 4, 2, 2), ALL)
    flat, cube = P(ALL, None), P(ALL, None, None)
    in_specs = (flat, flat, P(DP, None), flat, flat, cube, flat) + (flat,) * 4 + (cube,) * 2 + (flat,) * 2
    out_specs = (flat,) * 10 + (cube,) * 4 + (flat,) * 4
    return jax.shard_map(body, mesh=fine, in_specs=in_specs, out_specs=out_specs, check_vma=False)
```

```python
import math

import jax
import jax.numpy as jnp
from jax import lax
from jax.experimental import pallas as pl
from jax.experimental.pallas import tpu as pltpu
from jax.sharding import Mesh
from jax.sharding import PartitionSpec as P

D = 1536
HEADS = 12
KV_HEADS = 2
HEAD_DIM = 128
FF = 8960
BLOCK = 256
STEP = 5
QW = 1536
KW = 256
QKV = 2048


NORM_EPS = 1e-06
ROPE_BASE = 1000000.0
BETA_ONE = 0.9
BETA_TWO = 0.95
ADAM_EPS = 1e-08
DECAY = 0.1


DP = ("zh", "zl")
SEQ = ("y", "x", "c")
ALL = DP + SEQ


def low(value):
    return value.astype(jnp.bfloat16)


def wide(value):
    return value.astype(jnp.float32)


def after(value, *others):
    return lax.optimization_barrier((value,) + others)[0]


def shift(value, axis, step):
    count = lax.axis_size(axis)
    return lax.ppermute(value, axis, [(i, (i + step) % count) for i in range(count)])


def rotations(value, axis):
    return [value] + [shift(value, axis, step) for step in range(1, lax.axis_size(axis))]


def plane_steps():
    return [(j, i) for j in range(lax.axis_size("y")) for i in range(lax.axis_size("x"))]


def plane_shift(value, down, right):
    tall, broad = lax.axis_size("y"), lax.axis_size("x")
    pairs = [
        (j * broad + i, (j + down) % tall * broad + (i + right) % broad)
        for j in range(tall)
        for i in range(broad)
    ]
    return lax.ppermute(value, ("y", "x"), pairs)


def plane_pieces(value, dim, cut, second):
    across, along = rotations(value, "x"), rotations(value, "y")
    size = value.shape[dim]
    pieces = []
    for j, i in plane_steps():
        if j == 0 or i == 0:
            pieces.append((across[i] if j == 0 else along[j],))
        else:
            head = after(lax.slice_in_dim(across[i], 0, cut, axis=dim), *second)
            tail = after(lax.slice_in_dim(along[j], cut, size, axis=dim), *second)
            pieces.append((shift(head, "y", j), shift(tail, "x", i)))
    return pieces


def plane_blocks(value):
    return [value] + [plane_shift(value, j, i) for j, i in plane_steps()[1:]]


def seq_gather_small(value):
    mine = jnp.concatenate(plane_blocks(value), axis=0)
    return jnp.concatenate(rotations(mine, "c"), axis=0)


def seq_scatter_small(value, rows):
    part = value.shape[0] // lax.axis_size("c")
    log = []
    total = add_back(
        [value[step * part : (step + 1) * part] for step in range(lax.axis_size("c"))], "c", log=log
    )
    result = [total[:rows]]
    for number, (j, i) in enumerate(plane_steps()[1:], 1):
        term = low(total[number * rows : (number + 1) * rows])
        result.append(plane_shift(term, -j, -i))
    return result, log


def seq_sources():
    tall, broad, cores = (lax.axis_size(name) for name in SEQ)
    row, col, core = (lax.axis_index(name) for name in SEQ)
    return [
        ((row - j) % tall * broad + (col - i) % broad) * cores + (core - k) % cores
        for k in range(cores)
        for j, i in plane_steps()
    ]


def wanted_columns(columns, width):
    tall, broad, cores = (lax.axis_size(name) for name in SEQ)
    row, col, core = (lax.axis_index(name) for name in SEQ)
    depth, z = lax.axis_size(DP), lax.axis_index(DP)
    place = jnp.arange(columns, dtype=jnp.int32)
    inner, rest = place % width, place // width
    dp_step, rest = rest % depth, rest // depth
    c_step, rest = rest % cores, rest // cores
    x_step, y_step = rest % broad, rest // broad
    seq = ((row - y_step) % tall * broad + (col - x_step) % broad) * cores + (core - c_step) % cores
    source = ((z - dp_step) % depth * (tall * broad * cores) + seq) * width + inner
    return low(jnp.arange(columns, dtype=jnp.int32)[:, None] == source[None, :])


def token_gather(value, order):
    result = []
    for number, block in enumerate(rotations(order(value), "zh")):
        block = value if number == 0 else block
        if number % 2 == 0:
            grid = [rotations(item, "y") for item in rotations(block, "x")]
            grid = [[grid[i][j] for i in range(len(grid))] for j in range(len(grid[0]))]
        else:
            grid = [rotations(item, "x") for item in rotations(block, "y")]
        result.append([item for line in grid for item in line])
    return result


def add_back(blocks, axis, early=(), log=None):
    total = wide(blocks[0])
    for step in range(1, len(blocks)):
        got = shift(low(blocks[step]), axis, -step)
        if log is not None:
            log.append(got)
        total = total + wide(after(got, *early) if early else got)
    return total


def token_scatter(parts, between=None):
    across, along = lax.axis_size("x"), lax.axis_size("y")
    lines, first, second = [], [], []
    for number, blocks in reversed(list(enumerate(parts))):
        grid = [blocks[j * across : (j + 1) * across] for j in range(along)]
        axis = "y" if number % 2 == 0 else "x"
        if number % 2 == 0:
            grid = [list(column) for column in zip(*grid)]
        lines.append([add_back(line, axis, log=first) for line in grid])
    early = between(first) if between else ()
    for number, sums in enumerate(lines):
        axis = "x" if (len(parts) - 1 - number) % 2 == 0 else "y"
        lines[number] = add_back(sums, axis, early, log=second)
    lines = lines[::-1]
    last = lines.pop()
    sent = low(last)
    sent = shift(sent, "zh", -len(lines))
    return lines + [last], add_back(lines, "zh"), sent, first, second


VMEM_BYTES = 56 * 2**20
COST_SHARE = 4
ANYWHERE = pl.BlockSpec(memory_space=pl.ANY)
SCALARS = pl.BlockSpec(memory_space=pltpu.SMEM)


def projection_pieces(block, line, first, second):
    rows, columns = block.shape
    depth = lax.axis_size(DP)
    tall, broad, cores = (lax.axis_size(name) for name in SEQ)
    if rows % 16:
        return [lax.all_gather(block, ALL, axis=0, tiled=True)], None, None
    cut = columns // 2
    z = lax.axis_index(DP)
    z_sources = [(z - k) % depth for k in range(depth)]
    sources = seq_sources()
    own = plane_pieces(after(jnp.stack(line), *first), 2, cut, second)
    pieces, plan, targets = [], [], []
    for k in range(cores):
        for number, piece in enumerate(own):
            for part, value in enumerate(piece):
                pieces.append(value if k == 0 else shift(value, "c", k))
                place = (part * cut, cut) if len(piece) == 2 else (0, columns)
                plan.append([(slot, len(targets) + slot, place) for slot in range(depth)])
                seq = sources[k * len(own) + number]
                targets += [(z_sources[slot] * tall * broad * cores + seq) * rows for slot in range(depth)]
    return pieces, plan, jnp.stack(targets).astype(jnp.int32)


def start_pieces(plan, where_ref, pieces, whole, sems):
    if plan is None:
        copies = [pltpu.make_async_copy(pieces[0], whole, sems.at[0])]
    else:
        copies = []
        for piece, jobs in zip(pieces, plan):
            for slot, target, columns in jobs:
                first = pl.multiple_of(where_ref[target], 16)
                copies.append(
                    pltpu.make_async_copy(
                        piece.at[slot],
                        whole.at[pl.ds(first, piece.shape[1]), pl.ds(*columns)],
                        sems.at[len(copies)],
                    )
                )
    for copy in copies:
        copy.start()
    return copies


def call_with_pieces(kernel, projection, operands, outs, name, micros, scratch=()):
    pieces, plan, targets = projection
    count = 1 if plan is None else sum(len(jobs) for jobs in plan)
    if targets is None:
        targets = jnp.zeros((8,), jnp.int32)
    size = len(operands)

    def run(*refs):
        where_ref, whole, sems = refs[0], refs[-2], refs[-1]
        rest = refs[1:]
        copies = start_pieces(plan, where_ref, rest[size : size + len(pieces)], whole, sems)

        def ready():
            for copy in copies:
                copy.wait()

        kernel(ready, whole, *rest[:size], *rest[size + len(pieces) : -2])

    return pl.pallas_call(
        run,
        out_shape=outs,
        in_specs=[SCALARS]
        + [pl.BlockSpec(memory_space=pltpu.VMEM)] * size
        + [ANYWHERE] * len(pieces),
        scratch_shapes=[
            *scratch,
            pltpu.VMEM((D, pieces[0].shape[-1]), jnp.bfloat16),
            pltpu.SemaphoreType.DMA((count,)),
        ],
        compiler_params=pltpu.CompilerParams(vmem_limit_bytes=VMEM_BYTES),
        cost_estimate=cost(micros),
        name=name,
    )(targets, *operands, *pieces)


def local_call(kernel, operands, outs, name, micros, scratch=()):
    return pl.pallas_call(
        kernel,
        out_shape=outs,
        scratch_shapes=list(scratch),
        compiler_params=pltpu.CompilerParams(vmem_limit_bytes=VMEM_BYTES),
        cost_estimate=cost(micros),
        name=name,
    )(*operands)


def cost(micros):
    return pl.CostEstimate(flops=int(micros * 1.1e9) // COST_SHARE, bytes_accessed=0, transcendentals=0)


def shaped(shape, dtype):
    return jax.ShapeDtypeStruct(shape, dtype)


def dot(left, right, left_dim, right_dim):
    return lax.dot_general(
        left, right, (((left_dim,), (right_dim,)), ((), ())), preferred_element_type=jnp.float32
    )


def swap_halves(values):
    return pltpu.roll(values, HEAD_DIM // 2, 1)


def turned(values, cosine, sine):
    return values * cosine + swap_halves(values) * sine


def turned_back(grads, cosine, sine):
    return grads * cosine + swap_halves(grads * sine)


def front_kernel(
    ready, whole, rows_ref, gain_ref, bias_ref, cosine_ref, sine_ref, normed_ref, query_ref, pair_ref
):
    rows = wide(rows_ref[...])
    normed_ref[...] = low(rows * norm_scale(rows) * gain_ref[...])
    normed = normed_ref[...]
    cosine, sine = cosine_ref[...], sine_ref[...]
    ready()
    for first in range(0, QKV, 256):
        mixed = dot(normed, whole[:, first : first + 256], 1, 0) + bias_ref[:, first : first + 256]
        for start in (0, HEAD_DIM):
            part = mixed[:, start : start + HEAD_DIM]
            column = first + start
            if column < QW + KW:
                part = turned(part, cosine, sine)
            if column < QW:
                query_ref[:, column : column + HEAD_DIM] = low(part)
            else:
                pair_ref[:, column - QW : column - QW + HEAD_DIM] = low(part)


TOGETHER = 2


def head_views(step):
    heads = step * TOGETHER
    kind = heads // (HEADS // KV_HEADS)
    queries = [pl.ds(pl.multiple_of((heads + i) * HEAD_DIM, HEAD_DIM), HEAD_DIM) for i in range(TOGETHER)]
    keys = pl.ds(pl.multiple_of(kind * HEAD_DIM, HEAD_DIM), HEAD_DIM)
    values = pl.ds(pl.multiple_of(KW + kind * HEAD_DIM, HEAD_DIM), HEAD_DIM)
    return queries, keys, values


def visible(key_marks_ref, query_marks_ref):
    seen = (key_marks_ref[:, 0:1] == query_marks_ref[0:1, :]) & (
        key_marks_ref[:, 1:2] <= query_marks_ref[1:2, :]
    )
    return jnp.concatenate([jnp.where(seen, 0.0, -1e30)] * TOGETHER, axis=1)


def probabilities(keys, query, hidden):
    scores = dot(keys, query, 1, 1) * (HEAD_DIM**-0.5) + hidden
    grown = jnp.exp(scores - jnp.max(scores, axis=0, keepdims=True))
    return grown * (1.0 / jnp.sum(grown, axis=0, keepdims=True))


def attend_kernel(
    ready, whole, query_ref, pair_ref, key_marks_ref, query_marks_ref, rows_ref, gain_ref,
    attended_ref, middle_ref, normed_ref, hidden_ref,
):
    hidden_ref[...] = visible(key_marks_ref, query_marks_ref)

    def step(index, unused):
        queries, keys, values = head_views(index)
        query = jnp.concatenate([query_ref[:, view] for view in queries], axis=0)
        weights = low(probabilities(pair_ref[:, keys], query, hidden_ref[...]))
        result = low(dot(weights, pair_ref[:, values], 0, 0))
        count = query_ref.shape[0]
        for i, view in enumerate(queries):
            attended_ref[:, view] = result[i * count : (i + 1) * count]
        return unused

    lax.fori_loop(0, HEADS // TOGETHER, step, 0)
    ready()
    middle = wide(rows_ref[...]) + dot(attended_ref[...], whole[...], 1, 0)
    middle_ref[...] = middle
    normed_ref[...] = low(middle * norm_scale(middle) * gain_ref[...])


def middle_back_kernel(
    ready, whole, normed_grad_ref, received_ref, middle_ref, back_ref, gain_ref,
    middle_grad_ref, branch_ref, gain_grad_ref, attended_grad_ref,
):
    normed_grad = normed_grad_ref[...] + wide(received_ref[...])
    middle = middle_ref[...]
    scale = norm_scale(middle)
    weighted = gain_ref[...] * normed_grad
    middle_grad = (
        wide(back_ref[...])
        + scale * weighted
        - middle * scale**3 * jnp.mean(weighted * middle, axis=1, keepdims=True)
    )
    gain_grad_ref[...] = jnp.sum(normed_grad * middle * scale, axis=0, keepdims=True)
    middle_grad_ref[...] = middle_grad
    branch_ref[...] = low(middle_grad)
    ready()
    attended_grad_ref[...] = low(dot(branch_ref[...], whole[...], 1, 1))


def attend_back_kernel(
    attended_grad_ref, query_ref, pair_ref, key_marks_ref, query_marks_ref, cosine_ref, sine_ref,
    mixed_ref, pair_grad_ref, hidden_ref,
):
    hidden_ref[...] = visible(key_marks_ref, query_marks_ref)
    pair_grad_ref[...] = jnp.zeros_like(pair_grad_ref)
    cosine, sine = cosine_ref[...], sine_ref[...]

    def step(index, unused):
        queries, keys, values = head_views(index)
        query = jnp.concatenate([query_ref[:, view] for view in queries], axis=0)
        grad = jnp.concatenate([attended_grad_ref[:, view] for view in queries], axis=0)
        key = pair_ref[:, keys]
        weights = probabilities(key, query, hidden_ref[...])
        pulled = dot(pair_ref[:, values], grad, 1, 1)
        delta = jnp.sum(weights * pulled, axis=0, keepdims=True)
        score_grad = low(weights * (pulled - delta))
        query_grad = dot(score_grad, key, 0, 0) * (HEAD_DIM**-0.5)
        count = query_ref.shape[0]
        for i, view in enumerate(queries):
            mixed_ref[:, view] = low(
                turned_back(query_grad[i * count : (i + 1) * count], cosine, sine)
            )
        pair_grad_ref[:, keys] += dot(score_grad, query, 1, 0) * (HEAD_DIM**-0.5)
        pair_grad_ref[:, values] += dot(low(weights), grad, 1, 0)
        return unused

    lax.fori_loop(0, HEADS // TOGETHER, step, 0)


def query_kernel(ready, whole, mixed_ref, normed_grad_ref, pair_rows_ref):
    ready()
    normed_grad_ref[...] = dot(mixed_ref[...], whole[:, :QW], 1, 1)
    pair_rows_ref[...] = whole[:, QW:]


def finish_kernel(size, *refs):
    terms, refs = refs[:size], refs[size:]
    cosine_ref, sine_ref, mixed_ref, part_ref, pair_rows_ref, rows_ref, gain_ref = refs[:7]
    middle_grad_ref, gain_two_grad_ref, block_ref, input_grad_ref = refs[7:]
    count = mixed_ref.shape[0]
    total = terms[0][...]
    for term in terms[1:]:
        total = total + wide(term[...])
    block_ref[:count, :QW] = mixed_ref[...]
    for first in range(0, 2 * KW, HEAD_DIM):
        part = total[:, first : first + HEAD_DIM]
        if first < KW:
            part = turned_back(part, cosine_ref[...], sine_ref[...])
        block_ref[:count, QW + first : QW + first + HEAD_DIM] = low(part)
    rows = wide(rows_ref[...])
    scale = norm_scale(rows)
    normed_grad = part_ref[...] + dot(block_ref[:count, QW:], pair_rows_ref[...], 1, 1)
    weighted = gain_ref[...] * normed_grad
    input_grad_ref[...] = (
        middle_grad_ref[...]
        + scale * weighted
        - rows * scale**3 * jnp.mean(weighted * rows, axis=1, keepdims=True)
    )
    gain_grad = jnp.sum(normed_grad * rows * scale, axis=0, keepdims=True)
    gains = jnp.concatenate([gain_grad, gain_two_grad_ref[...], jnp.zeros((14, D), jnp.float32)], axis=0)
    block_ref[count:, :D] = low(gains)
    block_ref[count:, D:] = jnp.zeros((16, QKV - D), jnp.bfloat16)


def gradient_kernel(parts, size, *refs):
    by_unit, blocks = refs[: 3 * parts], refs[3 * parts : 3 * parts + 2 * size]
    out_ref, values, rows, sems = refs[3 * parts + 2 * size :]
    count, tokens = blocks[0].shape[0], by_unit[0].shape[1]

    def copies(kind):
        result = []
        for part in range(parts):
            number = 3 * part + kind
            view = values.at[kind, :, pl.ds(part * tokens, tokens)]
            result.append(pltpu.make_async_copy(by_unit[number], view, sems.at[number]))
        if kind != 1:
            side = kind // 2
            for number in range(size):
                view = rows.at[side, pl.ds(number * count, count), :]
                place = 3 * parts + side * size + number
                result.append(pltpu.make_async_copy(blocks[side * size + number], view, sems.at[place]))
        return result

    step = pl.program_id(0)

    @pl.when(step == 0)
    def _():
        for kind in range(3):
            for copy in copies(kind):
                copy.start()

    for kind in range(3):

        @pl.when(step == 2 * kind)
        def _():
            for copy in copies(kind):
                copy.wait()

        for half in range(2):

            @pl.when(step == 2 * kind + half)
            def _():
                right = rows[kind // 2, :, half * (D // 2) : (half + 1) * (D // 2)]
                out_ref[...] = low(dot(values[kind], right, 1, 0))


def units_gradient(parts, normed, back):
    units, tokens = parts[0][0].shape
    size, count = len(normed), normed[0].shape[0]
    return pl.pallas_call(
        lambda *refs: gradient_kernel(len(parts), size, *refs),
        grid=(6,),
        in_specs=[ANYWHERE] * (3 * len(parts) + 2 * size),
        out_specs=pl.BlockSpec((units, D // 2), lambda i: (0, i)),
        out_shape=shaped((units, 3 * D), jnp.bfloat16),
        scratch_shapes=[
            pltpu.VMEM((3, units, tokens * len(parts)), jnp.bfloat16),
            pltpu.VMEM((2, size * count, D), jnp.bfloat16),
            pltpu.SemaphoreType.DMA((3 * len(parts) + 2 * size,)),
        ],
        compiler_params=pltpu.CompilerParams(vmem_limit_bytes=VMEM_BYTES),
        cost_estimate=cost(8),
        name="units_gradient",
    )(*[item for part in parts for item in part], *normed, *back)


def units_step_kernel(grad_ref, weight_ref, first_ref, second_ref, *out_refs):
    results = optimizer_step(
        weight_ref[...], wide(grad_ref[...])[None], first_ref[...], second_ref[...],
        2.0 / math.sqrt(D), DECAY,
    )
    for out_ref, result in zip(out_refs, results):
        out_ref[...] = result


def units_step(grad, weight, first, second):
    units = grad.shape[0]
    width = D // 2
    block = pl.BlockSpec((1, units, width), lambda i: (i // 2, 0, i % 2))
    turn = lambda value: jnp.transpose(value, (1, 0, 2))
    dtypes = [jnp.float32] * 3 + [jnp.bfloat16]
    results = pl.pallas_call(
        units_step_kernel,
        grid=(6,),
        in_specs=[pl.BlockSpec((units, width), lambda i: (0, i))] + [block] * 3,
        out_specs=[block] * 4,
        out_shape=[shaped((3, units, D), dtype) for dtype in dtypes],
        compiler_params=pltpu.CompilerParams(vmem_limit_bytes=VMEM_BYTES),
        cost_estimate=cost(12),
        name="units_step",
    )(grad, turn(weight), turn(first), turn(second))
    return tuple(turn(result) for result in results)


def weight_kernel(size, *refs):
    left = jnp.concatenate([ref[...] for ref in refs[:size]], axis=0)
    right = jnp.concatenate([ref[...] for ref in refs[size : 2 * size]], axis=0)
    kept_ref, sent_ref = refs[2 * size :]
    total = dot(left, right, 0, 0)
    half = total.shape[0] // 2
    kept_ref[...] = total[:half]
    sent_ref[...] = low(total[half:])


def joined_kernel(size, *refs):
    count = refs[0].shape[0]
    left = jnp.concatenate([ref[...] for ref in refs[:size]], axis=0)
    rights = refs[size : 2 * size]
    right = jnp.concatenate([ref[:count, :] for ref in rights], axis=0)
    kept_ref, vector_ref, sent_ref = refs[2 * size :]
    half = kept_ref.shape[0]
    gains = sum(wide(ref[count:, :]) for ref in rights)
    bias = jnp.sum(wide(right), axis=0, keepdims=True)
    vector = jnp.concatenate([gains[:2], bias, jnp.zeros((13, QKV), jnp.float32)], axis=0)
    vector_ref[...] = vector[:8]
    sent_ref[half:, :] = low(vector)
    total = dot(left, right, 0, 0)
    kept_ref[...] = total[:half]
    sent_ref[:half, :] = low(total[half:])


def dp_scatter(total, early=(), log=None):
    depth = lax.axis_size(DP)
    width = total.shape[0] // depth
    return add_back([total[i * width : (i + 1) * width] for i in range(depth)], DP, early, log)


def norm_scale(rows):
    return lax.rsqrt(jnp.mean(rows * rows, axis=1, keepdims=True) + NORM_EPS)


def unpack_small(small):
    gain_cols = D // KW
    group = HEADS // KV_HEADS
    gain_one = small[:, :gain_cols].reshape(D)
    gain_two = small[:, gain_cols : 2 * gain_cols].reshape(D)
    query_bias = small[:, 2 * gain_cols : 2 * gain_cols + group].reshape(KV_HEADS, HEAD_DIM, group)
    query_bias = jnp.transpose(query_bias, (0, 2, 1)).reshape(QW)
    key_bias = small[:, 2 * gain_cols + group]
    value_bias = small[:, 2 * gain_cols + group + 1]
    return (gain_one, gain_two, jnp.concatenate([query_bias, key_bias, value_bias]))


def pack_small(gain_one, gain_two, bias):
    gain_cols = D // KW
    group = HEADS // KV_HEADS
    query_part = jnp.transpose(bias[:QW].reshape(KV_HEADS, group, HEAD_DIM), (0, 2, 1)).reshape(
        KW, group
    )
    return jnp.concatenate(
        [
            gain_one.reshape(KW, gain_cols),
            gain_two.reshape(KW, gain_cols),
            query_part,
            bias[QW : QW + KW][:, None],
            bias[QW + KW :][:, None],
        ],
        axis=1,
    )


def layout(starts_row, places):
    before = starts_row[None, :] <= places[:, None]
    documents = jnp.sum(before.astype(jnp.int32), axis=1) - 1
    begin = jnp.max(jnp.where(before, starts_row[None, :], 0), axis=1)
    offset = places - begin
    return (documents, offset // BLOCK, offset)


def turning(offset):
    half = HEAD_DIM // 2
    frequency = ROPE_BASE ** (-(2.0 * jnp.arange(half, dtype=jnp.float32)) / HEAD_DIM)
    angle = offset.astype(jnp.float32)[:, None] * frequency[None, :]
    angle = jnp.concatenate([angle, angle], axis=1)
    return (jnp.cos(angle)[:, None, :], jnp.sin(angle)[:, None, :])


def optimizer_step(weight, grad, first, second, rate, decay):
    first = BETA_ONE * first + (1.0 - BETA_ONE) * grad
    second = BETA_TWO * second + (1.0 - BETA_TWO) * grad * grad
    fixed_first = first / (1.0 - BETA_ONE**STEP)
    fixed_second = second / (1.0 - BETA_TWO**STEP)
    weight = weight - rate * (fixed_first / (jnp.sqrt(fixed_second) + ADAM_EPS) + decay * weight)
    return (weight, first, second, weight.astype(jnp.bfloat16))


def body(
    inputs,
    output_grad,
    document_starts,
    joined_weight,
    out_weight,
    units_weight,
    small_params,
    joined_first,
    joined_second,
    out_first,
    out_second,
    units_first,
    units_second,
    small_first,
    small_second,
):
    count = inputs.shape[0]
    seq_count = lax.axis_size(SEQ)
    devices = seq_count * lax.axis_size(DP)
    seq_index = lax.axis_index(SEQ)
    group_len = count * seq_count
    first = seq_index * count
    starts_row = document_starts[0]
    feature_width = joined_weight.shape[0]
    unit_width = units_weight.shape[0]

    device = lax.axis_index(ALL)
    small_rows, small_cols = small_params.shape
    size = small_rows * small_cols
    vector = lax.dynamic_update_slice_in_dim(
        jnp.zeros((devices * size,), jnp.float32),
        wide(low(small_params)).reshape(-1),
        device * size,
        0,
    ).reshape(1, -1)
    for axis in (DP, "c", "x", "y"):
        vector = sum(rotations(vector, axis))
    vector = jnp.concatenate(unpack_small(vector.reshape(-1, small_cols))).reshape(1, -1)
    gain_one, gain_two, bias = vector[:, :D], vector[:, D : 2 * D], vector[:, 2 * D :]

    joined_half = low(joined_weight)
    line = rotations(joined_half, DP)
    back_blocks = token_gather(output_grad, lambda value: after(value, line[-1]))
    projection = projection_pieces(
        joined_half, line, back_blocks[0][1:3], [back_blocks[0][3], back_blocks[1][0]]
    )
    out_half = low(out_weight)
    out_line = rotations(after(out_half, line[-1]), DP)
    out_projection = projection_pieces(
        out_half, out_line, projection[0][1:3], projection[0][3:5]
    )
    documents, blocks, offset = layout(starts_row, first + jnp.arange(count, dtype=jnp.int32))
    cosine, sine = turning(offset)
    cosine, sine = cosine[:, 0], sine[:, 0]
    sine = jnp.concatenate([-sine[:, : HEAD_DIM // 2], sine[:, HEAD_DIM // 2 :]], axis=1)
    sources = seq_sources()
    places = jnp.concatenate([i * count + jnp.arange(count, dtype=jnp.int32) for i in sources])
    all_documents, all_blocks, unused_offset = layout(starts_row, places)
    key_marks = jnp.stack([all_documents, all_blocks], axis=1)
    query_marks = jnp.stack([documents, blocks], axis=0)
    wanted = wanted_columns(D, feature_width)

    sharing = ("zl", "c")
    units_half = low(units_weight)
    units_all = lax.all_gather(units_half, sharing, axis=0, tiled=True)
    units_all = jnp.transpose(units_all, (1, 0, 2))

    normed_one, query, pair = call_with_pieces(
        front_kernel,
        projection,
        [after(inputs, *back_blocks[1][1:3]), gain_one, bias, cosine, sine],
        [
            shaped((count, D), jnp.bfloat16),
            shaped((count, QW), jnp.bfloat16),
            shaped((count, 2 * KW), jnp.bfloat16),
        ],
        "front",
        6,
    )
    pair_all = seq_gather_small(pair)

    attended, middle, normed_two = call_with_pieces(
        attend_kernel,
        out_projection,
        [after(query, back_blocks[1][3]), pair_all, key_marks, query_marks, inputs, gain_two],
        [
            shaped((count, QW), jnp.bfloat16),
            shaped((count, D), jnp.float32),
            shaped((count, D), jnp.bfloat16),
        ],
        "attend",
        12,
        [pltpu.VMEM((group_len, TOGETHER * count), jnp.float32)],
    )

    steps = plane_steps()
    normed_sent = low(dot(after(normed_one, normed_two), wanted, 1, 0))
    attended_sent = low(dot(attended, wanted, 1, 0))
    chip_width = D // len(steps)
    normed_owned, attended_owned = [], []
    for number, (j, i) in enumerate(steps):
        view = slice(number * chip_width, (number + 1) * chip_width)
        both = [normed_sent[:, view], attended_sent[:, view]]
        if number:
            moved = plane_shift(jnp.concatenate(both, axis=1), -j, -i)
            both = [moved[:, :chip_width], moved[:, chip_width:]]
        normed_owned.append(both[0])
        attended_owned.append(both[1])

    normed_blocks = token_gather(normed_two, lambda value: value)
    by_unit = lambda rows, tokens: jnp.einsum(
        "ud,td->ut", rows, tokens, preferred_element_type=jnp.float32
    )
    by_token = lambda values, rows: jnp.einsum(
        "ut,ud->td", values, rows, preferred_element_type=jnp.float32
    )
    cut = lambda value: [value[i : i + count] for i in range(0, value.shape[0], count)]
    unit_parts, grad_terms = [], []
    for normed, back in zip(normed_blocks, back_blocks):
        pulled = by_unit(units_all[2], jnp.concatenate(back, axis=0))
        if unit_parts:
            normed = [after(normed[0], *normed_owned, *attended_owned)] + normed[1:]
        normed = jnp.concatenate(normed, axis=0)
        gate = by_unit(units_all[0], normed)
        up = by_unit(units_all[1], normed)
        sigma = jax.nn.sigmoid(gate)
        active = gate * sigma
        gate_grad = low(pulled * up * sigma * (1.0 + gate * (1.0 - sigma)))
        up_grad = low(pulled * active)
        unit_parts.append((gate_grad, up_grad, low(active * up)))
        grad_terms.append(by_token(gate_grad, units_all[0]) + by_token(up_grad, units_all[1]))
    branch_terms = []

    def between(received):
        branch_terms.extend(
            cut(low(by_token(after(part[2], received[0]), units_all[2]))) for part in unit_parts
        )
        return sum(branch_terms, [])

    plane_sums, normed_grad_own, normed_grad_received, *unused = token_scatter(
        [cut(item) for item in grad_terms], between
    )
    parts = [unit_parts[0][:2] + (after(unit_parts[0][2], *plane_sums),)] + unit_parts[1:]
    units_term = units_gradient(
        parts,
        [block for blocks in normed_blocks for block in blocks],
        [block for blocks in back_blocks for block in blocks],
    )
    units_sum = lax.psum_scatter(units_term, sharing, scatter_dimension=0, tiled=True)
    branch_terms = [[after(item, *plane_sums) for item in blocks] for blocks in branch_terms]
    unused, branch_own, branch_received, branch_first, branch_second = token_scatter(branch_terms)
    block_output = low(middle + branch_own + wide(branch_received))

    middle_grad, branch_grad, gain_two_grad, attended_grad = call_with_pieces(
        middle_back_kernel,
        out_projection,
        [normed_grad_own, normed_grad_received, middle, output_grad, gain_two],
        [
            shaped((count, D), jnp.float32),
            shaped((count, D), jnp.bfloat16),
            shaped((1, D), jnp.float32),
            shaped((count, QW), jnp.bfloat16),
        ],
        "middle_back",
        4,
    )
    branch_pieces = plane_blocks(branch_grad)
    mixed_grad, pair_grad = local_call(
        attend_back_kernel,
        [attended_grad, query, pair_all, key_marks, query_marks, cosine, sine],
        [shaped((count, QW), jnp.bfloat16), shaped((group_len, 2 * KW), jnp.float32)],
        "attend_back",
        800,
        [pltpu.VMEM((group_len, TOGETHER * count), jnp.float32)],
    )
    pair_terms, pair_got = seq_scatter_small(after(pair_grad, *branch_pieces[1:3]), count)
    query_operand = after(mixed_grad, *pair_got)
    normed_grad_part, pair_rows = call_with_pieces(
        query_kernel,
        projection,
        [query_operand],
        [shaped((count, D), jnp.float32), shaped((D, 2 * KW), jnp.bfloat16)],
        "query_back",
        7,
    )
    mixed_block, input_grad = local_call(
        lambda *refs: finish_kernel(len(pair_terms), *refs),
        pair_terms
        + [cosine, sine, mixed_grad, normed_grad_part, pair_rows, inputs, gain_one, middle_grad]
        + [gain_two_grad],
        [shaped((count + 16, QKV), jnp.bfloat16), shaped((count, D), jnp.float32)],
        "finish",
        4,
    )
    mixed_pieces = plane_blocks(mixed_block)
    attended_owned[0] = after(attended_owned[0], mixed_block, *branch_first)
    half = attended_owned[0].shape[1] // 2
    kept, sent = local_call(
        lambda *refs: weight_kernel(len(steps), *refs),
        attended_owned + branch_pieces,
        [shaped((half, D), jnp.float32), shaped((half, D), jnp.bfloat16)],
        "out_weights",
        3,
    )
    outer_sum = kept + wide(shift(sent, "c", -1))
    normed_owned[0] = after(normed_owned[0], *branch_second)
    kept, kept_vector, sent = local_call(
        lambda *refs: joined_kernel(len(steps), *refs),
        normed_owned + mixed_pieces,
        [
            shaped((half, QKV), jnp.float32),
            shaped((8, QKV), jnp.float32),
            shaped((half + 16, QKV), jnp.bfloat16),
        ],
        "joined_weights",
        5,
    )
    got = shift(sent, "c", -1)
    units_new = units_step(units_sum, units_weight, units_first, units_second)
    outer_grad = dp_scatter(outer_sum, [units_new[3]])
    joined_grad = dp_scatter(kept + wide(got[:half]), [units_new[3]])
    vector = sum(rotations(kept_vector + wide(got[half : half + 8]), DP))
    small_grad = pack_small(vector[0, :D], vector[1, :D], vector[2])
    small_grad = lax.dynamic_slice_in_dim(small_grad, device * small_rows, small_rows, 0)

    joined = optimizer_step(
        joined_weight, joined_grad, joined_first, joined_second, 2.0 / math.sqrt(D), DECAY
    )
    outer = optimizer_step(
        out_weight, outer_grad, out_first, out_second, 2.0 / math.sqrt(QW // 64), DECAY
    )
    small = optimizer_step(small_params, small_grad, small_first, small_second, 0.5, 0.0)
    return (block_output, input_grad) + joined + outer + units_new + small


def solution(mesh):
    groups, members = mesh.devices.shape
    fine = Mesh(mesh.devices.reshape(groups // 2, 2, members // 4, 2, 2), ALL)
    flat, cube = P(ALL, None), P(ALL, None, None)
    in_specs = (flat, flat, P(DP, None), flat, flat, cube, flat) + (flat,) * 4 + (cube,) * 2 + (flat,) * 2
    out_specs = (flat,) * 10 + (cube,) * 4 + (flat,) * 4
    return jax.shard_map(body, mesh=fine, in_specs=in_specs, out_specs=out_specs, check_vma=False)
```

```python
import math

import jax
import jax.numpy as jnp
from jax import lax
from jax.experimental import pallas as pl
from jax.experimental.pallas import tpu as pltpu
from jax.sharding import Mesh
from jax.sharding import PartitionSpec as P

D = 1536
HEADS = 12
KV_HEADS = 2
HEAD_DIM = 128
FF = 8960
BLOCK = 256
STEP = 5
QW = 1536
KW = 256
QKV = 2048


NORM_EPS = 1e-06
ROPE_BASE = 1000000.0
BETA_ONE = 0.9
BETA_TWO = 0.95
ADAM_EPS = 1e-08
DECAY = 0.1


DP = ("zh", "zl")
SEQ = ("y", "x", "c")
ALL = DP + SEQ


def low(value):
    return value.astype(jnp.bfloat16)


def wide(value):
    return value.astype(jnp.float32)


def after(value, *others):
    return lax.optimization_barrier((value,) + others)[0]


def shift(value, axis, step):
    count = lax.axis_size(axis)
    return lax.ppermute(value, axis, [(i, (i + step) % count) for i in range(count)])


def rotations(value, axis):
    return [value] + [shift(value, axis, step) for step in range(1, lax.axis_size(axis))]


def plane_steps():
    return [(j, i) for j in range(lax.axis_size("y")) for i in range(lax.axis_size("x"))]


def plane_shift(value, down, right):
    tall, broad = lax.axis_size("y"), lax.axis_size("x")
    pairs = [
        (j * broad + i, (j + down) % tall * broad + (i + right) % broad)
        for j in range(tall)
        for i in range(broad)
    ]
    return lax.ppermute(value, ("y", "x"), pairs)


def plane_pieces(value, dim, cut, second):
    across, along = rotations(value, "x"), rotations(value, "y")
    size = value.shape[dim]
    pieces = []
    for j, i in plane_steps():
        if j == 0 or i == 0:
            pieces.append((across[i] if j == 0 else along[j],))
        else:
            head = after(lax.slice_in_dim(across[i], 0, cut, axis=dim), *second)
            tail = after(lax.slice_in_dim(along[j], cut, size, axis=dim), *second)
            pieces.append((shift(head, "y", j), shift(tail, "x", i)))
    return pieces


def plane_blocks(value):
    return [value] + [plane_shift(value, j, i) for j, i in plane_steps()[1:]]


def seq_gather_small(value):
    mine = jnp.concatenate(plane_blocks(value), axis=0)
    return jnp.concatenate(rotations(mine, "c"), axis=0)


def seq_scatter_small(value, rows):
    part = value.shape[0] // lax.axis_size("c")
    log = []
    total = add_back(
        [value[step * part : (step + 1) * part] for step in range(lax.axis_size("c"))], "c", log=log
    )
    result = [total[:rows]]
    for number, (j, i) in enumerate(plane_steps()[1:], 1):
        term = low(total[number * rows : (number + 1) * rows])
        result.append(plane_shift(term, -j, -i))
    return result, log


def seq_sources():
    tall, broad, cores = (lax.axis_size(name) for name in SEQ)
    row, col, core = (lax.axis_index(name) for name in SEQ)
    return [
        ((row - j) % tall * broad + (col - i) % broad) * cores + (core - k) % cores
        for k in range(cores)
        for j, i in plane_steps()
    ]


def wanted_columns(columns, width):
    tall, broad, cores = (lax.axis_size(name) for name in SEQ)
    row, col, core = (lax.axis_index(name) for name in SEQ)
    depth, z = lax.axis_size(DP), lax.axis_index(DP)
    place = jnp.arange(columns, dtype=jnp.int32)
    inner, rest = place % width, place // width
    dp_step, rest = rest % depth, rest // depth
    c_step, rest = rest % cores, rest // cores
    x_step, y_step = rest % broad, rest // broad
    seq = ((row - y_step) % tall * broad + (col - x_step) % broad) * cores + (core - c_step) % cores
    source = ((z - dp_step) % depth * (tall * broad * cores) + seq) * width + inner
    return low(jnp.arange(columns, dtype=jnp.int32)[:, None] == source[None, :])


def token_gather(value, order):
    result = []
    for number, block in enumerate(rotations(order(value), "zh")):
        block = value if number == 0 else block
        if number % 2 == 0:
            grid = [rotations(item, "y") for item in rotations(block, "x")]
            grid = [[grid[i][j] for i in range(len(grid))] for j in range(len(grid[0]))]
        else:
            grid = [rotations(item, "x") for item in rotations(block, "y")]
            grid = [list(column) for column in zip(*grid)]
        result.append([item for line in grid for item in line])
    return result


def add_back(blocks, axis, early=(), log=None):
    total = wide(blocks[0])
    for step in range(1, len(blocks)):
        got = shift(low(blocks[step]), axis, -step)
        if log is not None:
            log.append(got)
        total = total + wide(after(got, *early) if early else got)
    return total


def slabs_back(value, axis, early=(), log=None):
    size = value.shape[0] // lax.axis_size(axis)
    slabs = [value[first : first + size] for first in range(0, value.shape[0], size)]
    return add_back(slabs, axis, early, log)


def scatter_first(parts, early=()):
    log = []
    order = reversed(list(enumerate(parts)))
    lines = [
        slabs_back(part, "yx"[number % 2], () if number else early, log) for number, part in order
    ]
    return lines[::-1], log


def scatter_second(lines, early):
    return [slabs_back(line, "xy"[number % 2], early) for number, line in enumerate(lines)]


def scatter_last(lines):
    return add_back(lines[:-1], "zh"), shift(low(lines[-1]), "zh", 1 - len(lines))


VMEM_BYTES = 56 * 2**20
COST_SHARE = 4
ANYWHERE = pl.BlockSpec(memory_space=pl.ANY)
SCALARS = pl.BlockSpec(memory_space=pltpu.SMEM)


def projection_pieces(block, line, first, second):
    rows, columns = block.shape
    depth = lax.axis_size(DP)
    tall, broad, cores = (lax.axis_size(name) for name in SEQ)
    if rows % 16:
        return [lax.all_gather(block, ALL, axis=0, tiled=True)], None, None
    cut = columns // 2
    z = lax.axis_index(DP)
    z_sources = [(z - k) % depth for k in range(depth)]
    sources = seq_sources()
    own = plane_pieces(after(jnp.stack(line), *first), 2, cut, second)
    pieces, plan, targets = [], [], []
    for k in range(cores):
        for number, piece in enumerate(own):
            for part, value in enumerate(piece):
                pieces.append(value if k == 0 else shift(value, "c", k))
                place = (part * cut, cut) if len(piece) == 2 else (0, columns)
                plan.append([(slot, len(targets) + slot, place) for slot in range(depth)])
                seq = sources[k * len(own) + number]
                targets += [(z_sources[slot] * tall * broad * cores + seq) * rows for slot in range(depth)]
    return pieces, plan, jnp.stack(targets).astype(jnp.int32)


def start_pieces(plan, where_ref, pieces, whole, sems):
    if plan is None:
        copies = [pltpu.make_async_copy(pieces[0], whole, sems.at[0])]
    else:
        copies = []
        for piece, jobs in zip(pieces, plan):
            for slot, target, columns in jobs:
                first = pl.multiple_of(where_ref[target], 16)
                copies.append(
                    pltpu.make_async_copy(
                        piece.at[slot],
                        whole.at[pl.ds(first, piece.shape[1]), pl.ds(*columns)],
                        sems.at[len(copies)],
                    )
                )
    for copy in copies:
        copy.start()
    return copies


def call_with_pieces(kernel, projection, operands, outs, name, micros, scratch=()):
    pieces, plan, targets = projection
    count = 1 if plan is None else sum(len(jobs) for jobs in plan)
    if targets is None:
        targets = jnp.zeros((8,), jnp.int32)
    size = len(operands)

    def run(*refs):
        where_ref, whole, sems = refs[0], refs[-2], refs[-1]
        rest = refs[1:]
        copies = start_pieces(plan, where_ref, rest[size : size + len(pieces)], whole, sems)

        def ready():
            for copy in copies:
                copy.wait()

        kernel(ready, whole, *rest[:size], *rest[size + len(pieces) : -2])

    return pl.pallas_call(
        run,
        out_shape=outs,
        in_specs=[SCALARS]
        + [pl.BlockSpec(memory_space=pltpu.VMEM)] * size
        + [ANYWHERE] * len(pieces),
        scratch_shapes=[
            *scratch,
            pltpu.VMEM((D, pieces[0].shape[-1]), jnp.bfloat16),
            pltpu.SemaphoreType.DMA((count,)),
        ],
        compiler_params=pltpu.CompilerParams(vmem_limit_bytes=VMEM_BYTES),
        cost_estimate=cost(micros),
        name=name,
    )(targets, *operands, *pieces)


def local_call(kernel, operands, outs, name, micros, scratch=()):
    return pl.pallas_call(
        kernel,
        out_shape=outs,
        scratch_shapes=list(scratch),
        compiler_params=pltpu.CompilerParams(vmem_limit_bytes=VMEM_BYTES),
        cost_estimate=cost(micros),
        name=name,
    )(*operands)


def cost(micros):
    return pl.CostEstimate(flops=int(micros * 1.1e9) // COST_SHARE, bytes_accessed=0, transcendentals=0)


def shaped(shape, dtype):
    return jax.ShapeDtypeStruct(shape, dtype)


def dot(left, right, left_dim, right_dim):
    return lax.dot_general(
        left, right, (((left_dim,), (right_dim,)), ((), ())), preferred_element_type=jnp.float32
    )


def swap_halves(values):
    return pltpu.roll(values, HEAD_DIM // 2, 1)


def turned(values, cosine, sine):
    return values * cosine + swap_halves(values) * sine


def turned_back(grads, cosine, sine):
    return grads * cosine + swap_halves(grads * sine)


def front_kernel(
    ready, whole, rows_ref, gain_ref, bias_ref, cosine_ref, sine_ref, normed_ref, query_ref, pair_ref
):
    rows = wide(rows_ref[...])
    normed_ref[...] = low(rows * norm_scale(rows) * gain_ref[...])
    normed = normed_ref[...]
    cosine, sine = cosine_ref[...], sine_ref[...]
    ready()
    for first in range(0, QKV, 256):
        mixed = dot(normed, whole[:, first : first + 256], 1, 0) + bias_ref[:, first : first + 256]
        for start in (0, HEAD_DIM):
            part = mixed[:, start : start + HEAD_DIM]
            column = first + start
            if column < QW + KW:
                part = turned(part, cosine, sine)
            if column < QW:
                query_ref[:, column : column + HEAD_DIM] = low(part)
            else:
                pair_ref[:, column - QW : column - QW + HEAD_DIM] = low(part)


TOGETHER = 2


def head_views(step):
    heads = step * TOGETHER
    kind = heads // (HEADS // KV_HEADS)
    queries = [pl.ds(pl.multiple_of((heads + i) * HEAD_DIM, HEAD_DIM), HEAD_DIM) for i in range(TOGETHER)]
    keys = pl.ds(pl.multiple_of(kind * HEAD_DIM, HEAD_DIM), HEAD_DIM)
    values = pl.ds(pl.multiple_of(KW + kind * HEAD_DIM, HEAD_DIM), HEAD_DIM)
    return queries, keys, values


def visible(key_marks_ref, query_marks_ref):
    seen = (key_marks_ref[:, 0:1] == query_marks_ref[0:1, :]) & (
        key_marks_ref[:, 1:2] <= query_marks_ref[1:2, :]
    )
    return jnp.concatenate([jnp.where(seen, 0.0, -1e30)] * TOGETHER, axis=1)


def probabilities(keys, query, hidden):
    scores = dot(keys, query, 1, 1) * (HEAD_DIM**-0.5) + hidden
    grown = jnp.exp(scores - jnp.max(scores, axis=0, keepdims=True))
    return grown * (1.0 / jnp.sum(grown, axis=0, keepdims=True))


def attend_kernel(
    ready, whole, query_ref, pair_ref, key_marks_ref, query_marks_ref, rows_ref, gain_ref,
    attended_ref, middle_ref, normed_ref, hidden_ref,
):
    hidden_ref[...] = visible(key_marks_ref, query_marks_ref)

    def step(index, unused):
        queries, keys, values = head_views(index)
        query = jnp.concatenate([query_ref[:, view] for view in queries], axis=0)
        weights = low(probabilities(pair_ref[:, keys], query, hidden_ref[...]))
        result = low(dot(weights, pair_ref[:, values], 0, 0))
        count = query_ref.shape[0]
        for i, view in enumerate(queries):
            attended_ref[:, view] = result[i * count : (i + 1) * count]
        return unused

    lax.fori_loop(0, HEADS // TOGETHER, step, 0)
    ready()
    middle = wide(rows_ref[...]) + dot(attended_ref[...], whole[...], 1, 0)
    middle_ref[...] = middle
    normed_ref[...] = low(middle * norm_scale(middle) * gain_ref[...])


def middle_back_kernel(
    ready, whole, normed_grad_ref, received_ref, middle_ref, back_ref, gain_ref,
    middle_grad_ref, branch_ref, gain_grad_ref, attended_grad_ref,
):
    normed_grad = normed_grad_ref[...] + wide(received_ref[...])
    middle = middle_ref[...]
    scale = norm_scale(middle)
    weighted = gain_ref[...] * normed_grad
    middle_grad = (
        wide(back_ref[...])
        + scale * weighted
        - middle * scale**3 * jnp.mean(weighted * middle, axis=1, keepdims=True)
    )
    gain_grad_ref[...] = jnp.sum(normed_grad * middle * scale, axis=0, keepdims=True)
    middle_grad_ref[...] = middle_grad
    branch_ref[...] = low(middle_grad)
    ready()
    attended_grad_ref[...] = low(dot(branch_ref[...], whole[...], 1, 1))


def attend_back_kernel(
    attended_grad_ref, query_ref, pair_ref, key_marks_ref, query_marks_ref, cosine_ref, sine_ref,
    mixed_ref, pair_grad_ref, hidden_ref,
):
    hidden_ref[...] = visible(key_marks_ref, query_marks_ref)
    pair_grad_ref[...] = jnp.zeros_like(pair_grad_ref)
    cosine, sine = cosine_ref[...], sine_ref[...]

    def step(index, unused):
        queries, keys, values = head_views(index)
        query = jnp.concatenate([query_ref[:, view] for view in queries], axis=0)
        grad = jnp.concatenate([attended_grad_ref[:, view] for view in queries], axis=0)
        key = pair_ref[:, keys]
        weights = probabilities(key, query, hidden_ref[...])
        pulled = dot(pair_ref[:, values], grad, 1, 1)
        delta = jnp.sum(weights * pulled, axis=0, keepdims=True)
        score_grad = low(weights * (pulled - delta))
        query_grad = dot(score_grad, key, 0, 0) * (HEAD_DIM**-0.5)
        count = query_ref.shape[0]
        for i, view in enumerate(queries):
            mixed_ref[:, view] = low(
                turned_back(query_grad[i * count : (i + 1) * count], cosine, sine)
            )
        pair_grad_ref[:, keys] += dot(score_grad, query, 1, 0) * (HEAD_DIM**-0.5)
        pair_grad_ref[:, values] += dot(low(weights), grad, 1, 0)
        return unused

    lax.fori_loop(0, HEADS // TOGETHER, step, 0)


def query_kernel(ready, whole, mixed_ref, normed_grad_ref, pair_rows_ref):
    ready()
    normed_grad_ref[...] = dot(mixed_ref[...], whole[:, :QW], 1, 1)
    pair_rows_ref[...] = whole[:, QW:]


def finish_kernel(size, *refs):
    terms, refs = refs[:size], refs[size:]
    cosine_ref, sine_ref, mixed_ref, part_ref, pair_rows_ref, rows_ref, gain_ref = refs[:7]
    middle_grad_ref, gain_two_grad_ref, block_ref, input_grad_ref = refs[7:]
    count = mixed_ref.shape[0]
    total = terms[0][...]
    for term in terms[1:]:
        total = total + wide(term[...])
    block_ref[:count, :QW] = mixed_ref[...]
    for first in range(0, 2 * KW, HEAD_DIM):
        part = total[:, first : first + HEAD_DIM]
        if first < KW:
            part = turned_back(part, cosine_ref[...], sine_ref[...])
        block_ref[:count, QW + first : QW + first + HEAD_DIM] = low(part)
    rows = wide(rows_ref[...])
    scale = norm_scale(rows)
    normed_grad = part_ref[...] + dot(block_ref[:count, QW:], pair_rows_ref[...], 1, 1)
    weighted = gain_ref[...] * normed_grad
    input_grad_ref[...] = (
        middle_grad_ref[...]
        + scale * weighted
        - rows * scale**3 * jnp.mean(weighted * rows, axis=1, keepdims=True)
    )
    gain_grad = jnp.sum(normed_grad * rows * scale, axis=0, keepdims=True)
    gains = jnp.concatenate([gain_grad, gain_two_grad_ref[...], jnp.zeros((14, D), jnp.float32)], axis=0)
    block_ref[count:, :D] = low(gains)
    block_ref[count:, D:] = jnp.zeros((16, QKV - D), jnp.bfloat16)


def gradient_kernel(parts, size, *refs):
    by_unit, blocks = refs[: 3 * parts], refs[3 * parts : 3 * parts + 2 * size]
    out_ref, values, rows, sems = refs[3 * parts + 2 * size :]
    count, tokens = blocks[0].shape[0], by_unit[0].shape[1]

    def copies(kind):
        result = []
        for part in range(parts):
            number = 3 * part + kind
            view = values.at[kind, :, pl.ds(part * tokens, tokens)]
            result.append(pltpu.make_async_copy(by_unit[number], view, sems.at[number]))
        if kind != 1:
            side = kind // 2
            for number in range(size):
                view = rows.at[side, pl.ds(number * count, count), :]
                place = 3 * parts + side * size + number
                result.append(pltpu.make_async_copy(blocks[side * size + number], view, sems.at[place]))
        return result

    step = pl.program_id(0)

    @pl.when(step == 0)
    def _():
        for kind in range(3):
            for copy in copies(kind):
                copy.start()

    for kind in range(3):

        @pl.when(step == 2 * kind)
        def _():
            for copy in copies(kind):
                copy.wait()

        for half in range(2):

            @pl.when(step == 2 * kind + half)
            def _():
                right = rows[kind // 2, :, half * (D // 2) : (half + 1) * (D // 2)]
                out_ref[...] = low(dot(values[kind], right, 1, 0))


def units_gradient(parts, normed, back):
    units, tokens = parts[0][0].shape
    size, count = len(normed), normed[0].shape[0]
    return pl.pallas_call(
        lambda *refs: gradient_kernel(len(parts), size, *refs),
        grid=(6,),
        in_specs=[ANYWHERE] * (3 * len(parts) + 2 * size),
        out_specs=pl.BlockSpec((units, D // 2), lambda i: (0, i)),
        out_shape=shaped((units, 3 * D), jnp.bfloat16),
        scratch_shapes=[
            pltpu.VMEM((3, units, tokens * len(parts)), jnp.bfloat16),
            pltpu.VMEM((2, size * count, D), jnp.bfloat16),
            pltpu.SemaphoreType.DMA((3 * len(parts) + 2 * size,)),
        ],
        compiler_params=pltpu.CompilerParams(vmem_limit_bytes=VMEM_BYTES),
        cost_estimate=cost(8),
        name="units_gradient",
    )(*[item for part in parts for item in part], *normed, *back)


def units_step_kernel(grad_ref, weight_ref, first_ref, second_ref, *out_refs):
    results = optimizer_step(
        weight_ref[...], wide(grad_ref[...])[None], first_ref[...], second_ref[...],
        2.0 / math.sqrt(D), DECAY,
    )
    for out_ref, result in zip(out_refs, results):
        out_ref[...] = result


def units_step(grad, weight, first, second):
    units = grad.shape[0]
    width = D // 2
    block = pl.BlockSpec((1, units, width), lambda i: (i // 2, 0, i % 2))
    turn = lambda value: jnp.transpose(value, (1, 0, 2))
    dtypes = [jnp.float32] * 3 + [jnp.bfloat16]
    results = pl.pallas_call(
        units_step_kernel,
        grid=(6,),
        in_specs=[pl.BlockSpec((units, width), lambda i: (0, i))] + [block] * 3,
        out_specs=[block] * 4,
        out_shape=[shaped((3, units, D), dtype) for dtype in dtypes],
        compiler_params=pltpu.CompilerParams(vmem_limit_bytes=VMEM_BYTES),
        cost_estimate=cost(12),
        name="units_step",
    )(grad, turn(weight), turn(first), turn(second))
    return tuple(turn(result) for result in results)


def weight_kernel(size, *refs):
    left = jnp.concatenate([ref[...] for ref in refs[:size]], axis=0)
    right = jnp.concatenate([ref[...] for ref in refs[size : 2 * size]], axis=0)
    kept_ref, sent_ref = refs[2 * size :]
    total = dot(left, right, 0, 0)
    half = total.shape[0] // 2
    kept_ref[...] = total[:half]
    sent_ref[...] = low(total[half:])


def joined_kernel(size, *refs):
    count = refs[0].shape[0]
    left = jnp.concatenate([ref[...] for ref in refs[:size]], axis=0)
    rights = refs[size : 2 * size]
    right = jnp.concatenate([ref[:count, :] for ref in rights], axis=0)
    kept_ref, sent_ref = refs[2 * size :]
    gains = sum(wide(ref[count:, :]) for ref in rights)
    bias = jnp.sum(wide(right), axis=0, keepdims=True)
    vector = jnp.concatenate([gains[:2], bias, jnp.zeros((5, QKV), jnp.float32)], axis=0)
    total = dot(left, right, 0, 0)
    depth, width = kept_ref.shape[0], kept_ref.shape[1] - 8
    for slot in range(depth):
        first, second = slot * width, (depth + slot) * width
        kept_ref[slot, :width, :] = total[first : first + width]
        kept_ref[slot, width:, :] = vector
        sent_ref[slot] = low(jnp.concatenate([total[second : second + width], vector], axis=0))


def dp_scatter(total, early=(), log=None):
    depth = lax.axis_size(DP)
    width = total.shape[0] // depth
    return add_back([total[i * width : (i + 1) * width] for i in range(depth)], DP, early, log)


def norm_scale(rows):
    return lax.rsqrt(jnp.mean(rows * rows, axis=1, keepdims=True) + NORM_EPS)


def unpack_small(small):
    gain_cols = D // KW
    group = HEADS // KV_HEADS
    gain_one = small[:, :gain_cols].reshape(D)
    gain_two = small[:, gain_cols : 2 * gain_cols].reshape(D)
    query_bias = small[:, 2 * gain_cols : 2 * gain_cols + group].reshape(KV_HEADS, HEAD_DIM, group)
    query_bias = jnp.transpose(query_bias, (0, 2, 1)).reshape(QW)
    key_bias = small[:, 2 * gain_cols + group]
    value_bias = small[:, 2 * gain_cols + group + 1]
    return (gain_one, gain_two, jnp.concatenate([query_bias, key_bias, value_bias]))


def own_small(vector, first, rows):
    group, width = HEADS // KV_HEADS, D // KW
    cut = lambda row, start, size: lax.dynamic_slice(vector, (row, start), (1, size))
    gains = [cut(row, first * width, rows * width).reshape(rows, width) for row in (0, 1)]
    head, place = first // HEAD_DIM * group * HEAD_DIM, first % HEAD_DIM
    queries = [cut(2, head + j * HEAD_DIM + place, rows) for j in range(group)]
    keys = [cut(2, start + first, rows) for start in (QW, QW + KW)]
    return jnp.concatenate(gains + [jnp.concatenate(queries + keys, axis=0).T], axis=1)


def layout(starts_row, places):
    before = starts_row[None, :] <= places[:, None]
    documents = jnp.sum(before.astype(jnp.int32), axis=1) - 1
    begin = jnp.max(jnp.where(before, starts_row[None, :], 0), axis=1)
    offset = places - begin
    return (documents, offset // BLOCK, offset)


def turning(offset):
    half = HEAD_DIM // 2
    frequency = ROPE_BASE ** (-(2.0 * jnp.arange(half, dtype=jnp.float32)) / HEAD_DIM)
    angle = offset.astype(jnp.float32)[:, None] * frequency[None, :]
    angle = jnp.concatenate([angle, angle], axis=1)
    return (jnp.cos(angle)[:, None, :], jnp.sin(angle)[:, None, :])


def optimizer_step(weight, grad, first, second, rate, decay):
    first = BETA_ONE * first + (1.0 - BETA_ONE) * grad
    second = BETA_TWO * second + (1.0 - BETA_TWO) * grad * grad
    fixed_first = first / (1.0 - BETA_ONE**STEP)
    fixed_second = second / (1.0 - BETA_TWO**STEP)
    weight = weight - rate * (fixed_first / (jnp.sqrt(fixed_second) + ADAM_EPS) + decay * weight)
    return (weight, first, second, weight.astype(jnp.bfloat16))


def body(
    inputs,
    output_grad,
    document_starts,
    joined_weight,
    out_weight,
    units_weight,
    small_params,
    joined_first,
    joined_second,
    out_first,
    out_second,
    units_first,
    units_second,
    small_first,
    small_second,
):
    count = inputs.shape[0]
    seq_count = lax.axis_size(SEQ)
    devices = seq_count * lax.axis_size(DP)
    seq_index = lax.axis_index(SEQ)
    group_len = count * seq_count
    first = seq_index * count
    starts_row = document_starts[0]
    feature_width = joined_weight.shape[0]
    unit_width = units_weight.shape[0]

    device = lax.axis_index(ALL)
    small_rows, small_cols = small_params.shape
    size = small_rows * small_cols
    vector = lax.dynamic_update_slice_in_dim(
        jnp.zeros((devices * size,), jnp.float32),
        wide(low(small_params)).reshape(-1),
        device * size,
        0,
    ).reshape(1, -1)
    for axis in (DP, "c", "x", "y"):
        vector = sum(rotations(vector, axis))
    vector = jnp.concatenate(unpack_small(vector.reshape(-1, small_cols))).reshape(1, -1)
    gain_one, gain_two, bias = vector[:, :D], vector[:, D : 2 * D], vector[:, 2 * D :]

    joined_half = low(joined_weight)
    line = rotations(joined_half, DP)
    back_blocks = token_gather(output_grad, lambda value: after(value, line[-1]))
    projection = projection_pieces(
        joined_half, line, back_blocks[0][1:3], [back_blocks[0][3], back_blocks[1][0]]
    )
    out_half = low(out_weight)
    out_line = rotations(after(out_half, line[-1]), DP)
    out_projection = projection_pieces(
        out_half, out_line, projection[0][1:3], projection[0][3:5]
    )
    documents, blocks, offset = layout(starts_row, first + jnp.arange(count, dtype=jnp.int32))
    cosine, sine = turning(offset)
    cosine, sine = cosine[:, 0], sine[:, 0]
    sine = jnp.concatenate([-sine[:, : HEAD_DIM // 2], sine[:, HEAD_DIM // 2 :]], axis=1)
    sources = seq_sources()
    places = jnp.concatenate([i * count + jnp.arange(count, dtype=jnp.int32) for i in sources])
    all_documents, all_blocks, unused_offset = layout(starts_row, places)
    key_marks = jnp.stack([all_documents, all_blocks], axis=1)
    query_marks = jnp.stack([documents, blocks], axis=0)
    wanted = wanted_columns(D, feature_width)

    sharing = ("zl", "c")
    units_half = low(units_weight)
    units_all = lax.all_gather(units_half, sharing, axis=0, tiled=True)
    units_all = jnp.transpose(units_all, (1, 0, 2))

    normed_one, query, pair = call_with_pieces(
        front_kernel,
        projection,
        [after(inputs, *back_blocks[1][1:3]), gain_one, bias, cosine, sine],
        [
            shaped((count, D), jnp.bfloat16),
            shaped((count, QW), jnp.bfloat16),
            shaped((count, 2 * KW), jnp.bfloat16),
        ],
        "front",
        6,
    )
    pair_all = seq_gather_small(pair)

    attended, middle, normed_two = call_with_pieces(
        attend_kernel,
        out_projection,
        [after(query, back_blocks[1][3]), pair_all, key_marks, query_marks, inputs, gain_two],
        [
            shaped((count, QW), jnp.bfloat16),
            shaped((count, D), jnp.float32),
            shaped((count, D), jnp.bfloat16),
        ],
        "attend",
        12,
        [pltpu.VMEM((group_len, TOGETHER * count), jnp.float32)],
    )

    steps = plane_steps()
    normed_sent = low(dot(after(normed_one, normed_two), wanted, 1, 0))
    attended_sent = low(dot(attended, wanted, 1, 0))
    chip_width = D // len(steps)
    normed_owned, attended_owned = [], []
    for number, (j, i) in enumerate(steps):
        view = slice(number * chip_width, (number + 1) * chip_width)
        both = [normed_sent[:, view], attended_sent[:, view]]
        if number:
            moved = plane_shift(jnp.concatenate(both, axis=1), -j, -i)
            both = [moved[:, :chip_width], moved[:, chip_width:]]
        normed_owned.append(both[0])
        attended_owned.append(both[1])

    normed_blocks = token_gather(normed_two, lambda value: value)
    by_unit = lambda rows, tokens: jnp.einsum(
        "ud,td->ut", rows, tokens, preferred_element_type=jnp.float32
    )
    by_token = lambda values, rows: jnp.einsum(
        "ut,ud->td", values, rows, preferred_element_type=jnp.float32
    )
    cut = lambda value: [value[i : i + count] for i in range(0, value.shape[0], count)]
    unit_parts, grad_terms = [], []
    for normed, back in zip(normed_blocks, back_blocks):
        pulled = by_unit(units_all[2], jnp.concatenate(back, axis=0))
        if unit_parts:
            normed = [after(normed[0], *normed_owned, *attended_owned)] + normed[1:]
        normed = jnp.concatenate(normed, axis=0)
        gate = by_unit(units_all[0], normed)
        up = by_unit(units_all[1], normed)
        sigma = jax.nn.sigmoid(gate)
        active = gate * sigma
        gate_grad = low(pulled * up * sigma * (1.0 + gate * (1.0 - sigma)))
        up_grad = low(pulled * active)
        unit_parts.append((gate_grad, up_grad, low(active * up)))
        grad_terms.append(by_token(gate_grad, units_all[0]) + by_token(up_grad, units_all[1]))
    branch_terms = [
        low(by_token(after(part[2], *grad_terms), units_all[2])) for part in unit_parts
    ]
    first_sums, received = scatter_first(grad_terms, branch_terms)
    plane_sums = scatter_second(first_sums, ())
    normed_grad_own, normed_grad_received = scatter_last(plane_sums)
    parts = [unit_parts[0][:2] + (after(unit_parts[0][2], *plane_sums),)] + unit_parts[1:]
    units_term = units_gradient(
        parts,
        [block for blocks in normed_blocks for block in blocks],
        [block for blocks in back_blocks for block in blocks],
    )
    units_sum = lax.psum_scatter(units_term, sharing, scatter_dimension=0, tiled=True)
    branch_sums, branch_first = scatter_first(
        [after(item, *plane_sums) for item in branch_terms]
    )
    middle_grad, branch_grad, gain_two_grad, attended_grad = call_with_pieces(
        middle_back_kernel,
        out_projection,
        [normed_grad_own, normed_grad_received, middle, output_grad, gain_two],
        [
            shaped((count, D), jnp.float32),
            shaped((count, D), jnp.bfloat16),
            shaped((1, D), jnp.float32),
            shaped((count, QW), jnp.bfloat16),
        ],
        "middle_back",
        4,
    )
    branch_pieces = plane_blocks(branch_grad)
    mixed_grad, pair_grad = local_call(
        attend_back_kernel,
        [attended_grad, query, pair_all, key_marks, query_marks, cosine, sine],
        [shaped((count, QW), jnp.bfloat16), shaped((group_len, 2 * KW), jnp.float32)],
        "attend_back",
        800,
        [pltpu.VMEM((group_len, TOGETHER * count), jnp.float32)],
    )
    pair_terms, pair_got = seq_scatter_small(after(pair_grad, *branch_pieces[1:3]), count)
    query_operand = after(mixed_grad, *pair_got)
    normed_grad_part, pair_rows = call_with_pieces(
        query_kernel,
        projection,
        [query_operand],
        [shaped((count, D), jnp.float32), shaped((D, 2 * KW), jnp.bfloat16)],
        "query_back",
        7,
    )
    mixed_block, input_grad = local_call(
        lambda *refs: finish_kernel(len(pair_terms), *refs),
        pair_terms
        + [cosine, sine, mixed_grad, normed_grad_part, pair_rows, inputs, gain_one, middle_grad]
        + [gain_two_grad],
        [shaped((count + 16, QKV), jnp.bfloat16), shaped((count, D), jnp.float32)],
        "finish",
        4,
    )
    mixed_pieces = plane_blocks(mixed_block)
    branch_sums = scatter_second(branch_sums, [mixed_block])
    branch_own, branch_received = scatter_last(branch_sums)
    block_output = low(middle + branch_own + wide(branch_received))
    attended_owned[0] = after(attended_owned[0], mixed_block)
    half = attended_owned[0].shape[1] // 2
    kept, sent = local_call(
        lambda *refs: weight_kernel(len(steps), *refs),
        attended_owned + branch_pieces,
        [shaped((half, D), jnp.float32), shaped((half, D), jnp.bfloat16)],
        "out_weights",
        3,
    )
    outer_sum = kept + wide(shift(sent, "c", -1))
    depth = lax.axis_size(DP)
    shape = (depth, half // depth + 8, QKV)
    kept, sent = local_call(
        lambda *refs: joined_kernel(len(steps), *refs),
        normed_owned + mixed_pieces,
        [shaped(shape, jnp.float32), shaped(shape, jnp.bfloat16)],
        "joined_weights",
        5,
    )
    got = shift(sent, "c", -1)
    units_new = units_step(units_sum, units_weight, units_first, units_second)
    outer_grad = dp_scatter(outer_sum, [units_new[3]])
    total = kept + wide(got)
    total = add_back([total[i] for i in range(depth)], DP, [units_new[3]])
    joined_grad, vector = total[:-8], total[-8:]
    small_grad = own_small(vector, device * small_rows, small_rows)

    joined = optimizer_step(
        joined_weight, joined_grad, joined_first, joined_second, 2.0 / math.sqrt(D), DECAY
    )
    outer = optimizer_step(
        out_weight, outer_grad, out_first, out_second, 2.0 / math.sqrt(QW // 64), DECAY
    )
    small = optimizer_step(small_params, small_grad, small_first, small_second, 0.5, 0.0)
    return (block_output, input_grad) + joined + outer + units_new + small


def solution(mesh):
    groups, members = mesh.devices.shape
    fine = Mesh(mesh.devices.reshape(groups // 2, 2, members // 4, 2, 2), ALL)
    flat, cube = P(ALL, None), P(ALL, None, None)
    in_specs = (flat, flat, P(DP, None), flat, flat, cube, flat) + (flat,) * 4 + (cube,) * 2 + (flat,) * 2
    out_specs = (flat,) * 10 + (cube,) * 4 + (flat,) * 4
    return jax.shard_map(body, mesh=fine, in_specs=in_specs, out_specs=out_specs, check_vma=False)
```

```python
import math

import jax
import jax.numpy as jnp
from jax import lax
from jax.experimental import pallas as pl
from jax.experimental.pallas import tpu as pltpu
from jax.sharding import Mesh
from jax.sharding import PartitionSpec as P

D = 1536
HEADS = 12
KV_HEADS = 2
HEAD_DIM = 128
FF = 8960
BLOCK = 256
STEP = 5
QW = 1536
KW = 256
QKV = 2048


NORM_EPS = 1e-06
ROPE_BASE = 1000000.0
BETA_ONE = 0.9
BETA_TWO = 0.95
ADAM_EPS = 1e-08
DECAY = 0.1


DP = ("zh", "zl")
SEQ = ("y", "x", "c")
ALL = DP + SEQ


def low(value):
    return value.astype(jnp.bfloat16)


def wide(value):
    return value.astype(jnp.float32)


def after(value, *others):
    return lax.optimization_barrier((value,) + others)[0]


def shift(value, axis, step):
    count = lax.axis_size(axis)
    return lax.ppermute(value, axis, [(i, (i + step) % count) for i in range(count)])


def rotations(value, axis):
    return [value] + [shift(value, axis, step) for step in range(1, lax.axis_size(axis))]


def plane_steps():
    return [(j, i) for j in range(lax.axis_size("y")) for i in range(lax.axis_size("x"))]


def plane_shift(value, down, right):
    tall, broad = lax.axis_size("y"), lax.axis_size("x")
    pairs = [
        (j * broad + i, (j + down) % tall * broad + (i + right) % broad)
        for j in range(tall)
        for i in range(broad)
    ]
    return lax.ppermute(value, ("y", "x"), pairs)


def plane_pieces(value, dim, cut, second):
    across, along = rotations(value, "x"), rotations(value, "y")
    size = value.shape[dim]
    pieces = []
    for j, i in plane_steps():
        if j == 0 or i == 0:
            pieces.append((across[i] if j == 0 else along[j],))
        else:
            head = after(lax.slice_in_dim(across[i], 0, cut, axis=dim), *second)
            tail = after(lax.slice_in_dim(along[j], cut, size, axis=dim), *second)
            pieces.append((shift(head, "y", j), shift(tail, "x", i)))
    return pieces


def plane_blocks(value):
    return [value] + [plane_shift(value, j, i) for j, i in plane_steps()[1:]]


def seq_gather_small(value):
    mine = jnp.concatenate(plane_blocks(value), axis=0)
    return jnp.concatenate(rotations(mine, "c"), axis=0)


def seq_scatter_small(value, rows):
    part = value.shape[0] // lax.axis_size("c")
    log = []
    total = add_back(
        [value[step * part : (step + 1) * part] for step in range(lax.axis_size("c"))], "c", log=log
    )
    result = [total[:rows]]
    for number, (j, i) in enumerate(plane_steps()[1:], 1):
        term = low(total[number * rows : (number + 1) * rows])
        result.append(plane_shift(term, -j, -i))
    return result, log


def seq_sources():
    tall, broad, cores = (lax.axis_size(name) for name in SEQ)
    row, col, core = (lax.axis_index(name) for name in SEQ)
    return [
        ((row - j) % tall * broad + (col - i) % broad) * cores + (core - k) % cores
        for k in range(cores)
        for j, i in plane_steps()
    ]


def wanted_columns(columns, width):
    tall, broad, cores = (lax.axis_size(name) for name in SEQ)
    row, col, core = (lax.axis_index(name) for name in SEQ)
    depth, z = lax.axis_size(DP), lax.axis_index(DP)
    place = jnp.arange(columns, dtype=jnp.int32)
    inner, rest = place % width, place // width
    dp_step, rest = rest % depth, rest // depth
    c_step, rest = rest % cores, rest // cores
    x_step, y_step = rest % broad, rest // broad
    seq = ((row - y_step) % tall * broad + (col - x_step) % broad) * cores + (core - c_step) % cores
    source = ((z - dp_step) % depth * (tall * broad * cores) + seq) * width + inner
    return low(jnp.arange(columns, dtype=jnp.int32)[:, None] == source[None, :])


def token_gather(value, order):
    result = []
    for number, block in enumerate(rotations(order(value), "zh")):
        block = value if number == 0 else block
        if number % 2 == 0:
            grid = [rotations(item, "y") for item in rotations(block, "x")]
            grid = [[grid[i][j] for i in range(len(grid))] for j in range(len(grid[0]))]
        else:
            grid = [rotations(item, "x") for item in rotations(block, "y")]
            grid = [list(column) for column in zip(*grid)]
        result.append([item for line in grid for item in line])
    return result


def add_back(blocks, axis, early=(), log=None):
    total = wide(blocks[0])
    for step in range(1, len(blocks)):
        got = shift(low(blocks[step]), axis, -step)
        if log is not None:
            log.append(got)
        total = total + wide(after(got, *early) if early else got)
    return total


def slabs_back(value, axis, early=(), log=None):
    size = value.shape[0] // lax.axis_size(axis)
    slabs = [value[first : first + size] for first in range(0, value.shape[0], size)]
    return add_back(slabs, axis, early, log)


def scatter_first(parts, early=()):
    log = []
    order = reversed(list(enumerate(parts)))
    lines = [
        slabs_back(part, "yx"[number % 2], () if number else early, log) for number, part in order
    ]
    return lines[::-1], log


def scatter_second(lines, early):
    return [slabs_back(line, "xy"[number % 2], early) for number, line in enumerate(lines)]


def scatter_last(lines):
    return add_back(lines[:-1], "zh"), shift(low(lines[-1]), "zh", 1 - len(lines))


VMEM_BYTES = 56 * 2**20
COST_SHARE = 4
ANYWHERE = pl.BlockSpec(memory_space=pl.ANY)
SCALARS = pl.BlockSpec(memory_space=pltpu.SMEM)


def projection_pieces(block, line, first, second):
    rows, columns = block.shape
    depth = lax.axis_size(DP)
    tall, broad, cores = (lax.axis_size(name) for name in SEQ)
    if rows % 16:
        return [lax.all_gather(block, ALL, axis=0, tiled=True)], None, None
    cut = columns // 2
    z = lax.axis_index(DP)
    z_sources = [(z - k) % depth for k in range(depth)]
    sources = seq_sources()
    own = plane_pieces(after(jnp.stack(line), *first), 2, cut, second)
    pieces, plan, targets = [], [], []
    for k in range(cores):
        for number, piece in enumerate(own):
            for part, value in enumerate(piece):
                pieces.append(value if k == 0 else shift(value, "c", k))
                place = (part * cut, cut) if len(piece) == 2 else (0, columns)
                plan.append([(slot, len(targets) + slot, place) for slot in range(depth)])
                seq = sources[k * len(own) + number]
                targets += [(z_sources[slot] * tall * broad * cores + seq) * rows for slot in range(depth)]
    return pieces, plan, jnp.stack(targets).astype(jnp.int32)


def start_pieces(plan, where_ref, pieces, whole, sems):
    if plan is None:
        copies = [pltpu.make_async_copy(pieces[0], whole, sems.at[0])]
    else:
        copies = []
        for piece, jobs in zip(pieces, plan):
            for slot, target, columns in jobs:
                first = pl.multiple_of(where_ref[target], 16)
                copies.append(
                    pltpu.make_async_copy(
                        piece.at[slot],
                        whole.at[pl.ds(first, piece.shape[1]), pl.ds(*columns)],
                        sems.at[len(copies)],
                    )
                )
    for copy in copies:
        copy.start()
    return copies


def call_with_pieces(kernel, projection, operands, outs, name, micros, scratch=()):
    pieces, plan, targets = projection
    count = 1 if plan is None else sum(len(jobs) for jobs in plan)
    if targets is None:
        targets = jnp.zeros((8,), jnp.int32)
    size = len(operands)

    def run(*refs):
        where_ref, whole, sems = refs[0], refs[-2], refs[-1]
        rest = refs[1:]
        copies = start_pieces(plan, where_ref, rest[size : size + len(pieces)], whole, sems)

        def ready():
            for copy in copies:
                copy.wait()

        kernel(ready, whole, *rest[:size], *rest[size + len(pieces) : -2])

    return pl.pallas_call(
        run,
        out_shape=outs,
        in_specs=[SCALARS]
        + [pl.BlockSpec(memory_space=pltpu.VMEM)] * size
        + [ANYWHERE] * len(pieces),
        scratch_shapes=[
            *scratch,
            pltpu.VMEM((D, pieces[0].shape[-1]), jnp.bfloat16),
            pltpu.SemaphoreType.DMA((count,)),
        ],
        compiler_params=pltpu.CompilerParams(vmem_limit_bytes=VMEM_BYTES),
        cost_estimate=cost(micros),
        name=name,
    )(targets, *operands, *pieces)


def local_call(kernel, operands, outs, name, micros, scratch=()):
    return pl.pallas_call(
        kernel,
        out_shape=outs,
        scratch_shapes=list(scratch),
        compiler_params=pltpu.CompilerParams(vmem_limit_bytes=VMEM_BYTES),
        cost_estimate=cost(micros),
        name=name,
    )(*operands)


def cost(micros):
    return pl.CostEstimate(flops=int(micros * 1.1e9) // COST_SHARE, bytes_accessed=0, transcendentals=0)


def shaped(shape, dtype):
    return jax.ShapeDtypeStruct(shape, dtype)


def dot(left, right, left_dim, right_dim):
    return lax.dot_general(
        left, right, (((left_dim,), (right_dim,)), ((), ())), preferred_element_type=jnp.float32
    )


def swap_halves(values):
    return pltpu.roll(values, HEAD_DIM // 2, 1)


def turned(values, cosine, sine):
    return values * cosine + swap_halves(values) * sine


def turned_back(grads, cosine, sine):
    return grads * cosine + swap_halves(grads * sine)


def front_kernel(
    ready, whole, rows_ref, gain_ref, bias_ref, cosine_ref, sine_ref, normed_ref, query_ref, pair_ref
):
    rows = wide(rows_ref[...])
    normed_ref[...] = low(rows * norm_scale(rows) * gain_ref[...])
    normed = normed_ref[...]
    cosine, sine = cosine_ref[...], sine_ref[...]
    ready()
    for first in range(0, QKV, 256):
        mixed = dot(normed, whole[:, first : first + 256], 1, 0) + bias_ref[:, first : first + 256]
        for start in (0, HEAD_DIM):
            part = mixed[:, start : start + HEAD_DIM]
            column = first + start
            if column < QW + KW:
                part = turned(part, cosine, sine)
            if column < QW:
                query_ref[:, column : column + HEAD_DIM] = low(part)
            else:
                pair_ref[:, column - QW : column - QW + HEAD_DIM] = low(part)


TOGETHER = 3


def head_views(step):
    heads = step * TOGETHER
    kind = heads // (HEADS // KV_HEADS)
    queries = [pl.ds(pl.multiple_of((heads + i) * HEAD_DIM, HEAD_DIM), HEAD_DIM) for i in range(TOGETHER)]
    keys = pl.ds(pl.multiple_of(kind * HEAD_DIM, HEAD_DIM), HEAD_DIM)
    values = pl.ds(pl.multiple_of(KW + kind * HEAD_DIM, HEAD_DIM), HEAD_DIM)
    return queries, keys, values


def visible(key_marks_ref, query_marks_ref):
    seen = (key_marks_ref[:, 0:1] == query_marks_ref[0:1, :]) & (
        key_marks_ref[:, 1:2] <= query_marks_ref[1:2, :]
    )
    return jnp.concatenate([jnp.where(seen, 0.0, -1e30)] * TOGETHER, axis=1)


def probabilities(keys, query, hidden):
    scores = dot(keys, query, 1, 1) * (HEAD_DIM**-0.5) + hidden
    grown = jnp.exp(scores - jnp.max(scores, axis=0, keepdims=True))
    return grown * (1.0 / jnp.sum(grown, axis=0, keepdims=True))


def attend_kernel(
    ready, whole, query_ref, pair_ref, key_marks_ref, query_marks_ref, rows_ref, gain_ref,
    attended_ref, middle_ref, normed_ref, hidden_ref,
):
    hidden_ref[...] = visible(key_marks_ref, query_marks_ref)

    def step(index, unused):
        queries, keys, values = head_views(index)
        query = jnp.concatenate([query_ref[:, view] for view in queries], axis=0)
        weights = low(probabilities(pair_ref[:, keys], query, hidden_ref[...]))
        result = low(dot(weights, pair_ref[:, values], 0, 0))
        count = query_ref.shape[0]
        for i, view in enumerate(queries):
            attended_ref[:, view] = result[i * count : (i + 1) * count]
        return unused

    lax.fori_loop(0, HEADS // TOGETHER, step, 0)
    ready()
    middle = wide(rows_ref[...]) + dot(attended_ref[...], whole[...], 1, 0)
    middle_ref[...] = middle
    normed_ref[...] = low(middle * norm_scale(middle) * gain_ref[...])


def middle_back_kernel(
    ready, whole, normed_grad_ref, received_ref, middle_ref, back_ref, gain_ref,
    middle_grad_ref, branch_ref, gain_grad_ref, attended_grad_ref,
):
    normed_grad = normed_grad_ref[...] + wide(received_ref[...])
    middle = middle_ref[...]
    scale = norm_scale(middle)
    weighted = gain_ref[...] * normed_grad
    middle_grad = (
        wide(back_ref[...])
        + scale * weighted
        - middle * scale**3 * jnp.mean(weighted * middle, axis=1, keepdims=True)
    )
    gain_grad_ref[...] = jnp.sum(normed_grad * middle * scale, axis=0, keepdims=True)
    middle_grad_ref[...] = middle_grad
    branch_ref[...] = low(middle_grad)
    ready()
    attended_grad_ref[...] = low(dot(branch_ref[...], whole[...], 1, 1))


def attend_back_kernel(
    attended_grad_ref, query_ref, pair_ref, key_marks_ref, query_marks_ref, cosine_ref, sine_ref,
    mixed_ref, pair_grad_ref, hidden_ref,
):
    hidden_ref[...] = visible(key_marks_ref, query_marks_ref)
    pair_grad_ref[...] = jnp.zeros_like(pair_grad_ref)
    cosine, sine = cosine_ref[...], sine_ref[...]

    def step(index, unused):
        queries, keys, values = head_views(index)
        query = jnp.concatenate([query_ref[:, view] for view in queries], axis=0)
        grad = jnp.concatenate([attended_grad_ref[:, view] for view in queries], axis=0)
        key = pair_ref[:, keys]
        weights = probabilities(key, query, hidden_ref[...])
        pulled = dot(pair_ref[:, values], grad, 1, 1)
        delta = jnp.sum(weights * pulled, axis=0, keepdims=True)
        score_grad = low(weights * (pulled - delta))
        query_grad = dot(score_grad, key, 0, 0) * (HEAD_DIM**-0.5)
        count = query_ref.shape[0]
        for i, view in enumerate(queries):
            mixed_ref[:, view] = low(
                turned_back(query_grad[i * count : (i + 1) * count], cosine, sine)
            )
        pair_grad_ref[:, keys] += dot(score_grad, query, 1, 0) * (HEAD_DIM**-0.5)
        pair_grad_ref[:, values] += dot(low(weights), grad, 1, 0)
        return unused

    lax.fori_loop(0, HEADS // TOGETHER, step, 0)


def query_kernel(ready, whole, mixed_ref, normed_grad_ref, pair_rows_ref):
    ready()
    normed_grad_ref[...] = dot(mixed_ref[...], whole[:, :QW], 1, 1)
    pair_rows_ref[...] = whole[:, QW:]


def finish_kernel(size, *refs):
    terms, refs = refs[:size], refs[size:]
    cosine_ref, sine_ref, mixed_ref, part_ref, pair_rows_ref, rows_ref, gain_ref = refs[:7]
    middle_grad_ref, gain_two_grad_ref, block_ref, input_grad_ref = refs[7:]
    count = mixed_ref.shape[0]
    total = terms[0][...]
    for term in terms[1:]:
        total = total + wide(term[...])
    block_ref[:count, :QW] = mixed_ref[...]
    for first in range(0, 2 * KW, HEAD_DIM):
        part = total[:, first : first + HEAD_DIM]
        if first < KW:
            part = turned_back(part, cosine_ref[...], sine_ref[...])
        block_ref[:count, QW + first : QW + first + HEAD_DIM] = low(part)
    rows = wide(rows_ref[...])
    scale = norm_scale(rows)
    normed_grad = part_ref[...] + dot(block_ref[:count, QW:], pair_rows_ref[...], 1, 1)
    weighted = gain_ref[...] * normed_grad
    input_grad_ref[...] = (
        middle_grad_ref[...]
        + scale * weighted
        - rows * scale**3 * jnp.mean(weighted * rows, axis=1, keepdims=True)
    )
    gain_grad = jnp.sum(normed_grad * rows * scale, axis=0, keepdims=True)
    gains = jnp.concatenate([gain_grad, gain_two_grad_ref[...], jnp.zeros((14, D), jnp.float32)], axis=0)
    block_ref[count:, :D] = low(gains)
    block_ref[count:, D:] = jnp.zeros((16, QKV - D), jnp.bfloat16)


def gradient_kernel(parts, size, *refs):
    by_unit, blocks = refs[: 3 * parts], refs[3 * parts : 3 * parts + 2 * size]
    out_ref, values, rows, sems = refs[3 * parts + 2 * size :]
    count, tokens = blocks[0].shape[0], by_unit[0].shape[1]

    def copies(kind):
        result = []
        for part in range(parts):
            number = 3 * part + kind
            view = values.at[kind, :, pl.ds(part * tokens, tokens)]
            result.append(pltpu.make_async_copy(by_unit[number], view, sems.at[number]))
        if kind != 1:
            side = kind // 2
            for number in range(size):
                view = rows.at[side, pl.ds(number * count, count), :]
                place = 3 * parts + side * size + number
                result.append(pltpu.make_async_copy(blocks[side * size + number], view, sems.at[place]))
        return result

    step = pl.program_id(0)

    @pl.when(step == 0)
    def _():
        for kind in range(3):
            for copy in copies(kind):
                copy.start()

    for kind in range(3):

        @pl.when(step == 2 * kind)
        def _():
            for copy in copies(kind):
                copy.wait()

        for half in range(2):

            @pl.when(step == 2 * kind + half)
            def _():
                right = rows[kind // 2, :, half * (D // 2) : (half + 1) * (D // 2)]
                out_ref[...] = low(dot(values[kind], right, 1, 0))


def units_gradient(parts, normed, back):
    units, tokens = parts[0][0].shape
    size, count = len(normed), normed[0].shape[0]
    return pl.pallas_call(
        lambda *refs: gradient_kernel(len(parts), size, *refs),
        grid=(6,),
        in_specs=[ANYWHERE] * (3 * len(parts) + 2 * size),
        out_specs=pl.BlockSpec((units, D // 2), lambda i: (0, i)),
        out_shape=shaped((units, 3 * D), jnp.bfloat16),
        scratch_shapes=[
            pltpu.VMEM((3, units, tokens * len(parts)), jnp.bfloat16),
            pltpu.VMEM((2, size * count, D), jnp.bfloat16),
            pltpu.SemaphoreType.DMA((3 * len(parts) + 2 * size,)),
        ],
        compiler_params=pltpu.CompilerParams(vmem_limit_bytes=VMEM_BYTES),
        cost_estimate=cost(8),
        name="units_gradient",
    )(*[item for part in parts for item in part], *normed, *back)


def units_step_kernel(grad_ref, weight_ref, first_ref, second_ref, *out_refs):
    results = optimizer_step(
        weight_ref[...], wide(grad_ref[...])[None], first_ref[...], second_ref[...],
        2.0 / math.sqrt(D), DECAY,
    )
    for out_ref, result in zip(out_refs, results):
        out_ref[...] = result


def units_step(grad, weight, first, second):
    units = grad.shape[0]
    width = D // 2
    block = pl.BlockSpec((1, units, width), lambda i: (i // 2, 0, i % 2))
    turn = lambda value: jnp.transpose(value, (1, 0, 2))
    dtypes = [jnp.float32] * 3 + [jnp.bfloat16]
    results = pl.pallas_call(
        units_step_kernel,
        grid=(6,),
        in_specs=[pl.BlockSpec((units, width), lambda i: (0, i))] + [block] * 3,
        out_specs=[block] * 4,
        out_shape=[shaped((3, units, D), dtype) for dtype in dtypes],
        compiler_params=pltpu.CompilerParams(vmem_limit_bytes=VMEM_BYTES),
        cost_estimate=cost(12),
        name="units_step",
    )(grad, turn(weight), turn(first), turn(second))
    return tuple(turn(result) for result in results)


def weight_kernel(size, *refs):
    left = jnp.concatenate([ref[...] for ref in refs[:size]], axis=0)
    right = jnp.concatenate([ref[...] for ref in refs[size : 2 * size]], axis=0)
    kept_ref, sent_ref = refs[2 * size :]
    total = dot(left, right, 0, 0)
    half = total.shape[0] // 2
    kept_ref[...] = total[:half]
    sent_ref[...] = low(total[half:])


def joined_kernel(size, *refs):
    count = refs[0].shape[0]
    left = jnp.concatenate([ref[...] for ref in refs[:size]], axis=0)
    rights = refs[size : 2 * size]
    right = jnp.concatenate([ref[:count, :] for ref in rights], axis=0)
    kept_ref, sent_ref = refs[2 * size :]
    gains = sum(wide(ref[count:, :]) for ref in rights)
    bias = jnp.sum(wide(right), axis=0, keepdims=True)
    vector = jnp.concatenate([gains[:2], bias, jnp.zeros((5, QKV), jnp.float32)], axis=0)
    total = dot(left, right, 0, 0)
    depth, width = kept_ref.shape[0], kept_ref.shape[1] - 8
    for slot in range(depth):
        first, second = slot * width, (depth + slot) * width
        kept_ref[slot, :width, :] = total[first : first + width]
        kept_ref[slot, width:, :] = vector
        sent_ref[slot] = low(jnp.concatenate([total[second : second + width], vector], axis=0))


def dp_scatter(total, early=(), log=None):
    depth = lax.axis_size(DP)
    width = total.shape[0] // depth
    return add_back([total[i * width : (i + 1) * width] for i in range(depth)], DP, early, log)


def norm_scale(rows):
    return lax.rsqrt(jnp.mean(rows * rows, axis=1, keepdims=True) + NORM_EPS)


def unpack_small(small):
    gain_cols = D // KW
    group = HEADS // KV_HEADS
    gain_one = small[:, :gain_cols].reshape(D)
    gain_two = small[:, gain_cols : 2 * gain_cols].reshape(D)
    query_bias = small[:, 2 * gain_cols : 2 * gain_cols + group].reshape(KV_HEADS, HEAD_DIM, group)
    query_bias = jnp.transpose(query_bias, (0, 2, 1)).reshape(QW)
    key_bias = small[:, 2 * gain_cols + group]
    value_bias = small[:, 2 * gain_cols + group + 1]
    return (gain_one, gain_two, jnp.concatenate([query_bias, key_bias, value_bias]))


def own_small(vector, first, rows):
    group, width = HEADS // KV_HEADS, D // KW
    cut = lambda row, start, size: lax.dynamic_slice(vector, (row, start), (1, size))
    gains = [cut(row, first * width, rows * width).reshape(rows, width) for row in (0, 1)]
    head, place = first // HEAD_DIM * group * HEAD_DIM, first % HEAD_DIM
    queries = [cut(2, head + j * HEAD_DIM + place, rows) for j in range(group)]
    keys = [cut(2, start + first, rows) for start in (QW, QW + KW)]
    return jnp.concatenate(gains + [jnp.concatenate(queries + keys, axis=0).T], axis=1)


def layout(starts_row, places):
    before = starts_row[None, :] <= places[:, None]
    documents = jnp.sum(before.astype(jnp.int32), axis=1) - 1
    begin = jnp.max(jnp.where(before, starts_row[None, :], 0), axis=1)
    offset = places - begin
    return (documents, offset // BLOCK, offset)


def turning(offset):
    half = HEAD_DIM // 2
    frequency = ROPE_BASE ** (-(2.0 * jnp.arange(half, dtype=jnp.float32)) / HEAD_DIM)
    angle = offset.astype(jnp.float32)[:, None] * frequency[None, :]
    angle = jnp.concatenate([angle, angle], axis=1)
    return (jnp.cos(angle)[:, None, :], jnp.sin(angle)[:, None, :])


def optimizer_step(weight, grad, first, second, rate, decay):
    first = BETA_ONE * first + (1.0 - BETA_ONE) * grad
    second = BETA_TWO * second + (1.0 - BETA_TWO) * grad * grad
    fixed_first = first / (1.0 - BETA_ONE**STEP)
    fixed_second = second / (1.0 - BETA_TWO**STEP)
    weight = weight - rate * (fixed_first / (jnp.sqrt(fixed_second) + ADAM_EPS) + decay * weight)
    return (weight, first, second, weight.astype(jnp.bfloat16))


def body(
    inputs,
    output_grad,
    document_starts,
    joined_weight,
    out_weight,
    units_weight,
    small_params,
    joined_first,
    joined_second,
    out_first,
    out_second,
    units_first,
    units_second,
    small_first,
    small_second,
):
    count = inputs.shape[0]
    seq_count = lax.axis_size(SEQ)
    devices = seq_count * lax.axis_size(DP)
    seq_index = lax.axis_index(SEQ)
    group_len = count * seq_count
    first = seq_index * count
    starts_row = document_starts[0]
    feature_width = joined_weight.shape[0]
    unit_width = units_weight.shape[0]

    device = lax.axis_index(ALL)
    small_rows, small_cols = small_params.shape
    size = small_rows * small_cols
    vector = lax.dynamic_update_slice_in_dim(
        jnp.zeros((devices * size,), jnp.float32),
        wide(low(small_params)).reshape(-1),
        device * size,
        0,
    ).reshape(1, -1)
    for axis in (DP, "c", "x", "y"):
        vector = sum(rotations(vector, axis))
    vector = jnp.concatenate(unpack_small(vector.reshape(-1, small_cols))).reshape(1, -1)
    gain_one, gain_two, bias = vector[:, :D], vector[:, D : 2 * D], vector[:, 2 * D :]

    joined_half = low(joined_weight)
    line = rotations(joined_half, DP)
    back_blocks = token_gather(output_grad, lambda value: after(value, line[-1]))
    projection = projection_pieces(
        joined_half, line, back_blocks[0][1:3], [back_blocks[0][3], back_blocks[1][0]]
    )
    out_half = low(out_weight)
    out_line = rotations(after(out_half, line[-1]), DP)
    out_projection = projection_pieces(
        out_half, out_line, projection[0][1:3], projection[0][3:5]
    )
    documents, blocks, offset = layout(starts_row, first + jnp.arange(count, dtype=jnp.int32))
    cosine, sine = turning(offset)
    cosine, sine = cosine[:, 0], sine[:, 0]
    sine = jnp.concatenate([-sine[:, : HEAD_DIM // 2], sine[:, HEAD_DIM // 2 :]], axis=1)
    sources = seq_sources()
    places = jnp.concatenate([i * count + jnp.arange(count, dtype=jnp.int32) for i in sources])
    all_documents, all_blocks, unused_offset = layout(starts_row, places)
    key_marks = jnp.stack([all_documents, all_blocks], axis=1)
    query_marks = jnp.stack([documents, blocks], axis=0)
    wanted = wanted_columns(D, feature_width)

    sharing = ("zl", "c")
    units_half = low(units_weight)
    units_all = lax.all_gather(units_half, sharing, axis=0, tiled=True)
    units_all = jnp.transpose(units_all, (1, 0, 2))

    normed_one, query, pair = call_with_pieces(
        front_kernel,
        projection,
        [after(inputs, *back_blocks[1][1:3]), gain_one, bias, cosine, sine],
        [
            shaped((count, D), jnp.bfloat16),
            shaped((count, QW), jnp.bfloat16),
            shaped((count, 2 * KW), jnp.bfloat16),
        ],
        "front",
        6,
    )
    pair_all = seq_gather_small(pair)

    attended, middle, normed_two = call_with_pieces(
        attend_kernel,
        out_projection,
        [after(query, back_blocks[1][3]), pair_all, key_marks, query_marks, inputs, gain_two],
        [
            shaped((count, QW), jnp.bfloat16),
            shaped((count, D), jnp.float32),
            shaped((count, D), jnp.bfloat16),
        ],
        "attend",
        12,
        [pltpu.VMEM((group_len, TOGETHER * count), jnp.float32)],
    )

    steps = plane_steps()
    normed_sent = low(dot(after(normed_one, normed_two), wanted, 1, 0))
    attended_sent = low(dot(attended, wanted, 1, 0))
    chip_width = D // len(steps)
    normed_owned, attended_owned = [], []
    for number, (j, i) in enumerate(steps):
        view = slice(number * chip_width, (number + 1) * chip_width)
        both = [normed_sent[:, view], attended_sent[:, view]]
        if number:
            moved = plane_shift(jnp.concatenate(both, axis=1), -j, -i)
            both = [moved[:, :chip_width], moved[:, chip_width:]]
        normed_owned.append(both[0])
        attended_owned.append(both[1])

    normed_blocks = token_gather(normed_two, lambda value: value)
    by_unit = lambda rows, tokens: jnp.einsum(
        "ud,td->ut", rows, tokens, preferred_element_type=jnp.float32
    )
    by_token = lambda values, rows: jnp.einsum(
        "ut,ud->td", values, rows, preferred_element_type=jnp.float32
    )
    cut = lambda value: [value[i : i + count] for i in range(0, value.shape[0], count)]
    unit_parts, grad_terms = [], []
    for normed, back in zip(normed_blocks, back_blocks):
        pulled = by_unit(units_all[2], jnp.concatenate(back, axis=0))
        if unit_parts:
            normed = [after(normed[0], *normed_owned, *attended_owned)] + normed[1:]
        normed = jnp.concatenate(normed, axis=0)
        gate = by_unit(units_all[0], normed)
        up = by_unit(units_all[1], normed)
        sigma = jax.nn.sigmoid(gate)
        active = gate * sigma
        gate_grad = low(pulled * up * sigma * (1.0 + gate * (1.0 - sigma)))
        up_grad = low(pulled * active)
        unit_parts.append((gate_grad, up_grad, low(active * up)))
        grad_terms.append(by_token(gate_grad, units_all[0]) + by_token(up_grad, units_all[1]))
    branch_terms = [
        low(by_token(after(part[2], *grad_terms), units_all[2])) for part in unit_parts
    ]
    first_sums, received = scatter_first(grad_terms, branch_terms)
    plane_sums = scatter_second(first_sums, ())
    normed_grad_own, normed_grad_received = scatter_last(plane_sums)
    parts = [unit_parts[0][:2] + (after(unit_parts[0][2], *plane_sums),)] + unit_parts[1:]
    units_term = units_gradient(
        parts,
        [block for blocks in normed_blocks for block in blocks],
        [block for blocks in back_blocks for block in blocks],
    )
    units_sum = lax.psum_scatter(units_term, sharing, scatter_dimension=0, tiled=True)
    branch_sums, branch_first = scatter_first(
        [after(item, *plane_sums) for item in branch_terms]
    )
    middle_grad, branch_grad, gain_two_grad, attended_grad = call_with_pieces(
        middle_back_kernel,
        out_projection,
        [normed_grad_own, normed_grad_received, middle, output_grad, gain_two],
        [
            shaped((count, D), jnp.float32),
            shaped((count, D), jnp.bfloat16),
            shaped((1, D), jnp.float32),
            shaped((count, QW), jnp.bfloat16),
        ],
        "middle_back",
        4,
    )
    branch_pieces = plane_blocks(branch_grad)
    mixed_grad, pair_grad = local_call(
        attend_back_kernel,
        [attended_grad, query, pair_all, key_marks, query_marks, cosine, sine],
        [shaped((count, QW), jnp.bfloat16), shaped((group_len, 2 * KW), jnp.float32)],
        "attend_back",
        800,
        [pltpu.VMEM((group_len, TOGETHER * count), jnp.float32)],
    )
    pair_terms, pair_got = seq_scatter_small(after(pair_grad, *branch_pieces[1:3]), count)
    query_operand = after(mixed_grad, *pair_got)
    normed_grad_part, pair_rows = call_with_pieces(
        query_kernel,
        projection,
        [query_operand],
        [shaped((count, D), jnp.float32), shaped((D, 2 * KW), jnp.bfloat16)],
        "query_back",
        7,
    )
    mixed_block, input_grad = local_call(
        lambda *refs: finish_kernel(len(pair_terms), *refs),
        pair_terms
        + [cosine, sine, mixed_grad, normed_grad_part, pair_rows, inputs, gain_one, middle_grad]
        + [gain_two_grad],
        [shaped((count + 16, QKV), jnp.bfloat16), shaped((count, D), jnp.float32)],
        "finish",
        4,
    )
    mixed_pieces = plane_blocks(mixed_block)
    branch_sums = scatter_second(branch_sums, [mixed_block])
    branch_own, branch_received = scatter_last(branch_sums)
    block_output = low(middle + branch_own + wide(branch_received))
    attended_owned[0] = after(attended_owned[0], mixed_block)
    half = attended_owned[0].shape[1] // 2
    kept, sent = local_call(
        lambda *refs: weight_kernel(len(steps), *refs),
        attended_owned + branch_pieces,
        [shaped((half, D), jnp.float32), shaped((half, D), jnp.bfloat16)],
        "out_weights",
        3,
    )
    outer_sum = kept + wide(shift(sent, "c", -1))
    depth = lax.axis_size(DP)
    shape = (depth, half // depth + 8, QKV)
    kept, sent = local_call(
        lambda *refs: joined_kernel(len(steps), *refs),
        normed_owned + mixed_pieces,
        [shaped(shape, jnp.float32), shaped(shape, jnp.bfloat16)],
        "joined_weights",
        5,
    )
    got = shift(sent, "c", -1)
    units_new = units_step(units_sum, units_weight, units_first, units_second)
    outer_grad = dp_scatter(outer_sum, [units_new[3]])
    total = kept + wide(got)
    total = add_back([total[i] for i in range(depth)], DP, [units_new[3]])
    joined_grad, vector = total[:-8], total[-8:]
    small_grad = own_small(vector, device * small_rows, small_rows)

    joined = optimizer_step(
        joined_weight, joined_grad, joined_first, joined_second, 2.0 / math.sqrt(D), DECAY
    )
    outer = optimizer_step(
        out_weight, outer_grad, out_first, out_second, 2.0 / math.sqrt(QW // 64), DECAY
    )
    small = optimizer_step(small_params, small_grad, small_first, small_second, 0.5, 0.0)
    return (block_output, input_grad) + joined + outer + units_new + small


def solution(mesh):
    groups, members = mesh.devices.shape
    fine = Mesh(mesh.devices.reshape(groups // 2, 2, members // 4, 2, 2), ALL)
    flat, cube = P(ALL, None), P(ALL, None, None)
    in_specs = (flat, flat, P(DP, None), flat, flat, cube, flat) + (flat,) * 4 + (cube,) * 2 + (flat,) * 2
    out_specs = (flat,) * 10 + (cube,) * 4 + (flat,) * 4
    return jax.shard_map(body, mesh=fine, in_specs=in_specs, out_specs=out_specs, check_vma=False)
```

```python
import math

import jax
import jax.numpy as jnp
from jax import lax
from jax.experimental import pallas as pl
from jax.experimental.pallas import tpu as pltpu
from jax.sharding import Mesh
from jax.sharding import PartitionSpec as P

D = 1536
HEADS = 12
KV_HEADS = 2
HEAD_DIM = 128
FF = 8960
BLOCK = 256
STEP = 5
QW = 1536
KW = 256
QKV = 2048


NORM_EPS = 1e-06
ROPE_BASE = 1000000.0
BETA_ONE = 0.9
BETA_TWO = 0.95
ADAM_EPS = 1e-08
DECAY = 0.1


DP = ("zh", "zl")
SEQ = ("y", "x", "c")
ALL = DP + SEQ


def low(value):
    return value.astype(jnp.bfloat16)


def wide(value):
    return value.astype(jnp.float32)


def after(value, *others):
    return lax.optimization_barrier((value,) + others)[0]


def shift(value, axis, step):
    count = lax.axis_size(axis)
    return lax.ppermute(value, axis, [(i, (i + step) % count) for i in range(count)])


def rotations(value, axis):
    return [value] + [shift(value, axis, step) for step in range(1, lax.axis_size(axis))]


def plane_steps():
    return [(j, i) for j in range(lax.axis_size("y")) for i in range(lax.axis_size("x"))]


def plane_shift(value, down, right):
    tall, broad = lax.axis_size("y"), lax.axis_size("x")
    pairs = [
        (j * broad + i, (j + down) % tall * broad + (i + right) % broad)
        for j in range(tall)
        for i in range(broad)
    ]
    return lax.ppermute(value, ("y", "x"), pairs)


def plane_pieces(value, dim, cut, second):
    across, along = rotations(value, "x"), rotations(value, "y")
    size = value.shape[dim]
    pieces = []
    for j, i in plane_steps():
        if j == 0 or i == 0:
            pieces.append((across[i] if j == 0 else along[j],))
        else:
            head = after(lax.slice_in_dim(across[i], 0, cut, axis=dim), *second)
            tail = after(lax.slice_in_dim(along[j], cut, size, axis=dim), *second)
            pieces.append((shift(head, "y", j), shift(tail, "x", i)))
    return pieces


def plane_blocks(value):
    return [value] + [plane_shift(value, j, i) for j, i in plane_steps()[1:]]


def seq_gather_small(value):
    mine = jnp.concatenate(plane_blocks(value), axis=0)
    return jnp.concatenate(rotations(mine, "c"), axis=0)


def seq_scatter_small(value, rows):
    part = value.shape[0] // lax.axis_size("c")
    log = []
    total = add_back(
        [value[step * part : (step + 1) * part] for step in range(lax.axis_size("c"))], "c", log=log
    )
    result = [total[:rows]]
    for number, (j, i) in enumerate(plane_steps()[1:], 1):
        term = low(total[number * rows : (number + 1) * rows])
        result.append(plane_shift(term, -j, -i))
    return result, log


def seq_sources():
    tall, broad, cores = (lax.axis_size(name) for name in SEQ)
    row, col, core = (lax.axis_index(name) for name in SEQ)
    return [
        ((row - j) % tall * broad + (col - i) % broad) * cores + (core - k) % cores
        for k in range(cores)
        for j, i in plane_steps()
    ]


def wanted_columns(columns, width):
    tall, broad, cores = (lax.axis_size(name) for name in SEQ)
    row, col, core = (lax.axis_index(name) for name in SEQ)
    depth, z = lax.axis_size(DP), lax.axis_index(DP)
    place = jnp.arange(columns, dtype=jnp.int32)
    inner, rest = place % width, place // width
    dp_step, rest = rest % depth, rest // depth
    c_step, rest = rest % cores, rest // cores
    x_step, y_step = rest % broad, rest // broad
    seq = ((row - y_step) % tall * broad + (col - x_step) % broad) * cores + (core - c_step) % cores
    source = ((z - dp_step) % depth * (tall * broad * cores) + seq) * width + inner
    return low(jnp.arange(columns, dtype=jnp.int32)[:, None] == source[None, :])


def token_gather(value, order):
    result = []
    for number, block in enumerate(rotations(order(value), "zh")):
        block = value if number == 0 else block
        if number % 2 == 0:
            grid = [rotations(item, "y") for item in rotations(block, "x")]
            grid = [[grid[i][j] for i in range(len(grid))] for j in range(len(grid[0]))]
        else:
            grid = [rotations(item, "x") for item in rotations(block, "y")]
            grid = [list(column) for column in zip(*grid)]
        result.append([item for line in grid for item in line])
    return result


def add_back(blocks, axis, early=(), log=None):
    total = wide(blocks[0])
    for step in range(1, len(blocks)):
        got = shift(low(blocks[step]), axis, -step)
        if log is not None:
            log.append(got)
        total = total + wide(after(got, *early) if early else got)
    return total


def slabs_back(value, axis, early=(), log=None):
    size = value.shape[0] // lax.axis_size(axis)
    slabs = [value[first : first + size] for first in range(0, value.shape[0], size)]
    return add_back(slabs, axis, early, log)


def scatter_first(parts, early=()):
    log = []
    order = reversed(list(enumerate(parts)))
    lines = [
        slabs_back(part, "yx"[number % 2], () if number else early, log) for number, part in order
    ]
    return lines[::-1], log


def scatter_second(lines, early):
    return [slabs_back(line, "xy"[number % 2], early) for number, line in enumerate(lines)]


def scatter_last(lines):
    return add_back(lines[:-1], "zh"), shift(low(lines[-1]), "zh", 1 - len(lines))


VMEM_BYTES = 56 * 2**20
COST_SHARE = 4
ANYWHERE = pl.BlockSpec(memory_space=pl.ANY)
SCALARS = pl.BlockSpec(memory_space=pltpu.SMEM)


def projection_pieces(block, line, first, second):
    rows, columns = block.shape
    depth = lax.axis_size(DP)
    tall, broad, cores = (lax.axis_size(name) for name in SEQ)
    if rows % 16:
        return [lax.all_gather(block, ALL, axis=0, tiled=True)], None, None
    cut = columns // 2
    z = lax.axis_index(DP)
    z_sources = [(z - k) % depth for k in range(depth)]
    sources = seq_sources()
    own = plane_pieces(after(jnp.stack(line), *first), 2, cut, second)
    pieces, plan, targets = [], [], []
    for k in range(cores):
        for number, piece in enumerate(own):
            for part, value in enumerate(piece):
                pieces.append(value if k == 0 else shift(value, "c", k))
                place = (part * cut, cut) if len(piece) == 2 else (0, columns)
                plan.append([(slot, len(targets) + slot, place) for slot in range(depth)])
                seq = sources[k * len(own) + number]
                targets += [(z_sources[slot] * tall * broad * cores + seq) * rows for slot in range(depth)]
    return pieces, plan, jnp.stack(targets).astype(jnp.int32)


def start_pieces(plan, where_ref, pieces, whole, sems):
    if plan is None:
        copies = [pltpu.make_async_copy(pieces[0], whole, sems.at[0])]
    else:
        copies = []
        for piece, jobs in zip(pieces, plan):
            for slot, target, columns in jobs:
                first = pl.multiple_of(where_ref[target], 16)
                copies.append(
                    pltpu.make_async_copy(
                        piece.at[slot],
                        whole.at[pl.ds(first, piece.shape[1]), pl.ds(*columns)],
                        sems.at[len(copies)],
                    )
                )
    for copy in copies:
        copy.start()
    return copies


def call_with_pieces(kernel, projection, operands, outs, name, micros, scratch=()):
    pieces, plan, targets = projection
    count = 1 if plan is None else sum(len(jobs) for jobs in plan)
    if targets is None:
        targets = jnp.zeros((8,), jnp.int32)
    size = len(operands)

    def run(*refs):
        where_ref, whole, sems = refs[0], refs[-2], refs[-1]
        rest = refs[1:]
        copies = start_pieces(plan, where_ref, rest[size : size + len(pieces)], whole, sems)

        def ready():
            for copy in copies:
                copy.wait()

        kernel(ready, whole, *rest[:size], *rest[size + len(pieces) : -2])

    return pl.pallas_call(
        run,
        out_shape=outs,
        in_specs=[SCALARS]
        + [pl.BlockSpec(memory_space=pltpu.VMEM)] * size
        + [ANYWHERE] * len(pieces),
        scratch_shapes=[
            *scratch,
            pltpu.VMEM((D, pieces[0].shape[-1]), jnp.bfloat16),
            pltpu.SemaphoreType.DMA((count,)),
        ],
        compiler_params=pltpu.CompilerParams(vmem_limit_bytes=VMEM_BYTES),
        cost_estimate=cost(micros),
        name=name,
    )(targets, *operands, *pieces)


def local_call(kernel, operands, outs, name, micros, scratch=()):
    return pl.pallas_call(
        kernel,
        out_shape=outs,
        scratch_shapes=list(scratch),
        compiler_params=pltpu.CompilerParams(vmem_limit_bytes=VMEM_BYTES),
        cost_estimate=cost(micros),
        name=name,
    )(*operands)


def cost(micros):
    return pl.CostEstimate(flops=int(micros * 1.1e9) // COST_SHARE, bytes_accessed=0, transcendentals=0)


def shaped(shape, dtype):
    return jax.ShapeDtypeStruct(shape, dtype)


def dot(left, right, left_dim, right_dim):
    return lax.dot_general(
        left, right, (((left_dim,), (right_dim,)), ((), ())), preferred_element_type=jnp.float32
    )


def swap_halves(values):
    return pltpu.roll(values, HEAD_DIM // 2, 1)


def turned(values, cosine, sine):
    return values * cosine + swap_halves(values) * sine


def turned_back(grads, cosine, sine):
    return grads * cosine + swap_halves(grads * sine)


def front_kernel(
    ready, whole, rows_ref, gain_ref, bias_ref, cosine_ref, sine_ref, normed_ref, query_ref, pair_ref
):
    rows = wide(rows_ref[...])
    normed_ref[...] = low(rows * norm_scale(rows) * gain_ref[...])
    normed = normed_ref[...]
    cosine, sine = cosine_ref[...], sine_ref[...]
    ready()
    for first in range(0, QKV, 256):
        mixed = dot(normed, whole[:, first : first + 256], 1, 0) + bias_ref[:, first : first + 256]
        for start in (0, HEAD_DIM):
            part = mixed[:, start : start + HEAD_DIM]
            column = first + start
            if column < QW + KW:
                part = turned(part, cosine, sine)
            if column < QW:
                query_ref[:, column : column + HEAD_DIM] = low(part)
            else:
                pair_ref[:, column - QW : column - QW + HEAD_DIM] = low(part)


TOGETHER = 3


def head_views(step):
    heads = step * TOGETHER
    kind = heads // (HEADS // KV_HEADS)
    queries = [pl.ds(pl.multiple_of((heads + i) * HEAD_DIM, HEAD_DIM), HEAD_DIM) for i in range(TOGETHER)]
    keys = pl.ds(pl.multiple_of(kind * HEAD_DIM, HEAD_DIM), HEAD_DIM)
    values = pl.ds(pl.multiple_of(KW + kind * HEAD_DIM, HEAD_DIM), HEAD_DIM)
    return queries, keys, values


def visible(key_marks_ref, query_marks_ref):
    seen = (key_marks_ref[:, 0:1] == query_marks_ref[0:1, :]) & (
        key_marks_ref[:, 1:2] <= query_marks_ref[1:2, :]
    )
    return jnp.concatenate([jnp.where(seen, 0.0, -1e30)] * TOGETHER, axis=1)


def probabilities(keys, query, hidden):
    scores = dot(keys, query, 1, 1) * (HEAD_DIM**-0.5) + hidden
    grown = jnp.exp(scores - jnp.max(scores, axis=0, keepdims=True))
    return grown * (1.0 / jnp.sum(grown, axis=0, keepdims=True))


def attend_kernel(
    ready, whole, query_ref, pair_ref, key_marks_ref, query_marks_ref, rows_ref, gain_ref,
    attended_ref, middle_ref, normed_ref, hidden_ref,
):
    hidden_ref[...] = visible(key_marks_ref, query_marks_ref)

    def step(index, unused):
        queries, keys, values = head_views(index)
        query = jnp.concatenate([query_ref[:, view] for view in queries], axis=0)
        weights = low(probabilities(pair_ref[:, keys], query, hidden_ref[...]))
        result = low(dot(weights, pair_ref[:, values], 0, 0))
        count = query_ref.shape[0]
        for i, view in enumerate(queries):
            attended_ref[:, view] = result[i * count : (i + 1) * count]
        return unused

    lax.fori_loop(0, HEADS // TOGETHER, step, 0)
    ready()
    middle = wide(rows_ref[...]) + dot(attended_ref[...], whole[...], 1, 0)
    middle_ref[...] = middle
    normed_ref[...] = low(middle * norm_scale(middle) * gain_ref[...])


def middle_back_kernel(
    ready, whole, normed_grad_ref, received_ref, middle_ref, back_ref, gain_ref,
    middle_grad_ref, branch_ref, gain_grad_ref, attended_grad_ref,
):
    normed_grad = normed_grad_ref[...] + wide(received_ref[...])
    middle = middle_ref[...]
    scale = norm_scale(middle)
    weighted = gain_ref[...] * normed_grad
    middle_grad = (
        wide(back_ref[...])
        + scale * weighted
        - middle * scale**3 * jnp.mean(weighted * middle, axis=1, keepdims=True)
    )
    gain_grad_ref[...] = jnp.sum(normed_grad * middle * scale, axis=0, keepdims=True)
    middle_grad_ref[...] = middle_grad
    branch_ref[...] = low(middle_grad)
    ready()
    attended_grad_ref[...] = low(dot(branch_ref[...], whole[...], 1, 1))


def attend_back_kernel(
    attended_grad_ref, query_ref, pair_ref, key_marks_ref, query_marks_ref, cosine_ref, sine_ref,
    mixed_ref, pair_grad_ref, hidden_ref,
):
    hidden_ref[...] = visible(key_marks_ref, query_marks_ref)
    pair_grad_ref[...] = jnp.zeros_like(pair_grad_ref)
    cosine, sine = cosine_ref[...], sine_ref[...]

    def step(index, unused):
        queries, keys, values = head_views(index)
        query = jnp.concatenate([query_ref[:, view] for view in queries], axis=0)
        grad = jnp.concatenate([attended_grad_ref[:, view] for view in queries], axis=0)
        key = pair_ref[:, keys]
        weights = probabilities(key, query, hidden_ref[...])
        pulled = dot(pair_ref[:, values], grad, 1, 1)
        delta = jnp.sum(weights * pulled, axis=0, keepdims=True)
        score_grad = low(weights * (pulled - delta))
        query_grad = dot(score_grad, key, 0, 0) * (HEAD_DIM**-0.5)
        count = query_ref.shape[0]
        for i, view in enumerate(queries):
            mixed_ref[:, view] = low(
                turned_back(query_grad[i * count : (i + 1) * count], cosine, sine)
            )
        pair_grad_ref[:, keys] += dot(score_grad, query, 1, 0) * (HEAD_DIM**-0.5)
        pair_grad_ref[:, values] += dot(low(weights), grad, 1, 0)
        return unused

    lax.fori_loop(0, HEADS // TOGETHER, step, 0)


def query_kernel(ready, whole, mixed_ref, normed_grad_ref, pair_rows_ref):
    ready()
    normed_grad_ref[...] = dot(mixed_ref[...], whole[:, :QW], 1, 1)
    pair_rows_ref[...] = whole[:, QW:]


def finish_kernel(size, *refs):
    terms, refs = refs[:size], refs[size:]
    cosine_ref, sine_ref, mixed_ref, part_ref, pair_rows_ref, rows_ref, gain_ref = refs[:7]
    middle_grad_ref, gain_two_grad_ref, block_ref, input_grad_ref = refs[7:]
    count = mixed_ref.shape[0]
    total = terms[0][...]
    for term in terms[1:]:
        total = total + wide(term[...])
    block_ref[:count, :QW] = mixed_ref[...]
    for first in range(0, 2 * KW, HEAD_DIM):
        part = total[:, first : first + HEAD_DIM]
        if first < KW:
            part = turned_back(part, cosine_ref[...], sine_ref[...])
        block_ref[:count, QW + first : QW + first + HEAD_DIM] = low(part)
    rows = wide(rows_ref[...])
    scale = norm_scale(rows)
    normed_grad = part_ref[...] + dot(block_ref[:count, QW:], pair_rows_ref[...], 1, 1)
    weighted = gain_ref[...] * normed_grad
    input_grad_ref[...] = (
        middle_grad_ref[...]
        + scale * weighted
        - rows * scale**3 * jnp.mean(weighted * rows, axis=1, keepdims=True)
    )
    gain_grad = jnp.sum(normed_grad * rows * scale, axis=0, keepdims=True)
    gains = jnp.concatenate([gain_grad, gain_two_grad_ref[...], jnp.zeros((14, D), jnp.float32)], axis=0)
    block_ref[count:, :D] = low(gains)
    block_ref[count:, D:] = jnp.zeros((16, QKV - D), jnp.bfloat16)


def gradient_kernel(parts, size, *refs):
    by_unit, blocks = refs[: 3 * parts], refs[3 * parts : 3 * parts + 2 * size]
    out_ref, values, rows, sems = refs[3 * parts + 2 * size :]
    count, tokens = blocks[0].shape[0], by_unit[0].shape[1]

    def copies(kind):
        result = []
        for part in range(parts):
            number = 3 * part + kind
            view = values.at[kind, :, pl.ds(part * tokens, tokens)]
            result.append(pltpu.make_async_copy(by_unit[number], view, sems.at[number]))
        if kind != 1:
            side = kind // 2
            for number in range(size):
                view = rows.at[side, pl.ds(number * count, count), :]
                place = 3 * parts + side * size + number
                result.append(pltpu.make_async_copy(blocks[side * size + number], view, sems.at[place]))
        return result

    step = pl.program_id(0)

    @pl.when(step == 0)
    def _():
        for kind in range(3):
            for copy in copies(kind):
                copy.start()

    for kind in range(3):

        @pl.when(step == 2 * kind)
        def _():
            for copy in copies(kind):
                copy.wait()

        for half in range(2):

            @pl.when(step == 2 * kind + half)
            def _():
                right = rows[kind // 2, :, half * (D // 2) : (half + 1) * (D // 2)]
                out_ref[...] = low(dot(values[kind], right, 1, 0))


def units_gradient(parts, normed, back):
    units, tokens = parts[0][0].shape
    size, count = len(normed), normed[0].shape[0]
    return pl.pallas_call(
        lambda *refs: gradient_kernel(len(parts), size, *refs),
        grid=(6,),
        in_specs=[ANYWHERE] * (3 * len(parts) + 2 * size),
        out_specs=pl.BlockSpec((units, D // 2), lambda i: (0, i)),
        out_shape=shaped((units, 3 * D), jnp.bfloat16),
        scratch_shapes=[
            pltpu.VMEM((3, units, tokens * len(parts)), jnp.bfloat16),
            pltpu.VMEM((2, size * count, D), jnp.bfloat16),
            pltpu.SemaphoreType.DMA((3 * len(parts) + 2 * size,)),
        ],
        compiler_params=pltpu.CompilerParams(vmem_limit_bytes=VMEM_BYTES),
        cost_estimate=cost(8),
        name="units_gradient",
    )(*[item for part in parts for item in part], *normed, *back)


def units_step_kernel(grad_ref, weight_ref, first_ref, second_ref, *out_refs):
    results = optimizer_step(
        weight_ref[...], wide(grad_ref[...])[None], first_ref[...], second_ref[...],
        2.0 / math.sqrt(D), DECAY,
    )
    for out_ref, result in zip(out_refs, results):
        out_ref[...] = result


def units_step(grad, weight, first, second):
    units = grad.shape[0]
    width = D // 4
    block = pl.BlockSpec((1, units, width), lambda i: (i // 4, 0, i % 4))
    turn = lambda value: jnp.transpose(value, (1, 0, 2))
    dtypes = [jnp.float32] * 3 + [jnp.bfloat16]
    results = pl.pallas_call(
        units_step_kernel,
        grid=(12,),
        in_specs=[pl.BlockSpec((units, width), lambda i: (0, i))] + [block] * 3,
        out_specs=[block] * 4,
        out_shape=[shaped((3, units, D), dtype) for dtype in dtypes],
        compiler_params=pltpu.CompilerParams(vmem_limit_bytes=VMEM_BYTES),
        cost_estimate=cost(12),
        name="units_step",
    )(grad, turn(weight), turn(first), turn(second))
    return tuple(turn(result) for result in results)


def weight_kernel(size, *refs):
    left = jnp.concatenate([ref[...] for ref in refs[:size]], axis=0)
    right = jnp.concatenate([ref[...] for ref in refs[size : 2 * size]], axis=0)
    kept_ref, sent_ref = refs[2 * size :]
    total = dot(left, right, 0, 0)
    half = total.shape[0] // 2
    kept_ref[...] = total[:half]
    sent_ref[...] = low(total[half:])


def joined_kernel(size, *refs):
    count = refs[0].shape[0]
    left = jnp.concatenate([ref[...] for ref in refs[:size]], axis=0)
    rights = refs[size : 2 * size]
    right = jnp.concatenate([ref[:count, :] for ref in rights], axis=0)
    kept_ref, sent_ref = refs[2 * size :]
    gains = sum(wide(ref[count:, :]) for ref in rights)
    bias = jnp.sum(wide(right), axis=0, keepdims=True)
    vector = jnp.concatenate([gains[:2], bias, jnp.zeros((5, QKV), jnp.float32)], axis=0)
    total = dot(left, right, 0, 0)
    depth, width = kept_ref.shape[0], kept_ref.shape[1] - 8
    for slot in range(depth):
        first, second = slot * width, (depth + slot) * width
        kept_ref[slot, :width, :] = total[first : first + width]
        kept_ref[slot, width:, :] = vector
        sent_ref[slot] = low(jnp.concatenate([total[second : second + width], vector], axis=0))


def dp_scatter(total, early=(), log=None):
    depth = lax.axis_size(DP)
    width = total.shape[0] // depth
    return add_back([total[i * width : (i + 1) * width] for i in range(depth)], DP, early, log)


def norm_scale(rows):
    return lax.rsqrt(jnp.mean(rows * rows, axis=1, keepdims=True) + NORM_EPS)


def unpack_small(small):
    gain_cols = D // KW
    group = HEADS // KV_HEADS
    gain_one = small[:, :gain_cols].reshape(D)
    gain_two = small[:, gain_cols : 2 * gain_cols].reshape(D)
    query_bias = small[:, 2 * gain_cols : 2 * gain_cols + group].reshape(KV_HEADS, HEAD_DIM, group)
    query_bias = jnp.transpose(query_bias, (0, 2, 1)).reshape(QW)
    key_bias = small[:, 2 * gain_cols + group]
    value_bias = small[:, 2 * gain_cols + group + 1]
    return (gain_one, gain_two, jnp.concatenate([query_bias, key_bias, value_bias]))


def own_small(vector, first, rows):
    group, width = HEADS // KV_HEADS, D // KW
    cut = lambda row, start, size: lax.dynamic_slice(vector, (row, start), (1, size))
    gains = [cut(row, first * width, rows * width).reshape(rows, width) for row in (0, 1)]
    head, place = first // HEAD_DIM * group * HEAD_DIM, first % HEAD_DIM
    queries = [cut(2, head + j * HEAD_DIM + place, rows) for j in range(group)]
    keys = [cut(2, start + first, rows) for start in (QW, QW + KW)]
    return jnp.concatenate(gains + [jnp.concatenate(queries + keys, axis=0).T], axis=1)


def layout(starts_row, places):
    before = starts_row[None, :] <= places[:, None]
    documents = jnp.sum(before.astype(jnp.int32), axis=1) - 1
    begin = jnp.max(jnp.where(before, starts_row[None, :], 0), axis=1)
    offset = places - begin
    return (documents, offset // BLOCK, offset)


def turning(offset):
    half = HEAD_DIM // 2
    frequency = ROPE_BASE ** (-(2.0 * jnp.arange(half, dtype=jnp.float32)) / HEAD_DIM)
    angle = offset.astype(jnp.float32)[:, None] * frequency[None, :]
    angle = jnp.concatenate([angle, angle], axis=1)
    return (jnp.cos(angle)[:, None, :], jnp.sin(angle)[:, None, :])


def optimizer_step(weight, grad, first, second, rate, decay):
    first = BETA_ONE * first + (1.0 - BETA_ONE) * grad
    second = BETA_TWO * second + (1.0 - BETA_TWO) * grad * grad
    fixed_first = first / (1.0 - BETA_ONE**STEP)
    fixed_second = second / (1.0 - BETA_TWO**STEP)
    weight = weight - rate * (fixed_first / (jnp.sqrt(fixed_second) + ADAM_EPS) + decay * weight)
    return (weight, first, second, weight.astype(jnp.bfloat16))


def body(
    inputs,
    output_grad,
    document_starts,
    joined_weight,
    out_weight,
    units_weight,
    small_params,
    joined_first,
    joined_second,
    out_first,
    out_second,
    units_first,
    units_second,
    small_first,
    small_second,
):
    count = inputs.shape[0]
    seq_count = lax.axis_size(SEQ)
    devices = seq_count * lax.axis_size(DP)
    seq_index = lax.axis_index(SEQ)
    group_len = count * seq_count
    first = seq_index * count
    starts_row = document_starts[0]
    feature_width = joined_weight.shape[0]
    unit_width = units_weight.shape[0]

    device = lax.axis_index(ALL)
    small_rows, small_cols = small_params.shape
    size = small_rows * small_cols
    vector = lax.dynamic_update_slice_in_dim(
        jnp.zeros((devices * size,), jnp.float32),
        wide(low(small_params)).reshape(-1),
        device * size,
        0,
    ).reshape(1, -1)
    for axis in (DP, "c", "x", "y"):
        vector = sum(rotations(vector, axis))
    vector = jnp.concatenate(unpack_small(vector.reshape(-1, small_cols))).reshape(1, -1)
    gain_one, gain_two, bias = vector[:, :D], vector[:, D : 2 * D], vector[:, 2 * D :]

    joined_half = low(joined_weight)
    line = rotations(joined_half, DP)
    back_blocks = token_gather(output_grad, lambda value: after(value, line[-1]))
    projection = projection_pieces(
        joined_half, line, back_blocks[0][1:3], [back_blocks[0][3], back_blocks[1][0]]
    )
    out_half = low(out_weight)
    out_line = rotations(after(out_half, line[-1]), DP)
    out_projection = projection_pieces(
        out_half, out_line, projection[0][1:3], projection[0][3:5]
    )
    documents, blocks, offset = layout(starts_row, first + jnp.arange(count, dtype=jnp.int32))
    cosine, sine = turning(offset)
    cosine, sine = cosine[:, 0], sine[:, 0]
    sine = jnp.concatenate([-sine[:, : HEAD_DIM // 2], sine[:, HEAD_DIM // 2 :]], axis=1)
    sources = seq_sources()
    places = jnp.concatenate([i * count + jnp.arange(count, dtype=jnp.int32) for i in sources])
    all_documents, all_blocks, unused_offset = layout(starts_row, places)
    key_marks = jnp.stack([all_documents, all_blocks], axis=1)
    query_marks = jnp.stack([documents, blocks], axis=0)
    wanted = wanted_columns(D, feature_width)

    sharing = ("zl", "c")
    units_half = low(units_weight)
    units_all = lax.all_gather(units_half, sharing, axis=0, tiled=True)
    units_all = jnp.transpose(units_all, (1, 0, 2))

    normed_one, query, pair = call_with_pieces(
        front_kernel,
        projection,
        [after(inputs, *back_blocks[1][1:3]), gain_one, bias, cosine, sine],
        [
            shaped((count, D), jnp.bfloat16),
            shaped((count, QW), jnp.bfloat16),
            shaped((count, 2 * KW), jnp.bfloat16),
        ],
        "front",
        6,
    )
    pair_all = seq_gather_small(pair)

    attended, middle, normed_two = call_with_pieces(
        attend_kernel,
        out_projection,
        [after(query, back_blocks[1][3]), pair_all, key_marks, query_marks, inputs, gain_two],
        [
            shaped((count, QW), jnp.bfloat16),
            shaped((count, D), jnp.float32),
            shaped((count, D), jnp.bfloat16),
        ],
        "attend",
        12,
        [pltpu.VMEM((group_len, TOGETHER * count), jnp.float32)],
    )

    steps = plane_steps()
    normed_sent = low(dot(after(normed_one, normed_two), wanted, 1, 0))
    attended_sent = low(dot(attended, wanted, 1, 0))
    chip_width = D // len(steps)
    normed_owned, attended_owned = [], []
    for number, (j, i) in enumerate(steps):
        view = slice(number * chip_width, (number + 1) * chip_width)
        both = [normed_sent[:, view], attended_sent[:, view]]
        if number:
            moved = plane_shift(jnp.concatenate(both, axis=1), -j, -i)
            both = [moved[:, :chip_width], moved[:, chip_width:]]
        normed_owned.append(both[0])
        attended_owned.append(both[1])

    normed_blocks = token_gather(normed_two, lambda value: value)
    by_unit = lambda rows, tokens: jnp.einsum(
        "ud,td->ut", rows, tokens, preferred_element_type=jnp.float32
    )
    by_token = lambda values, rows: jnp.einsum(
        "ut,ud->td", values, rows, preferred_element_type=jnp.float32
    )
    cut = lambda value: [value[i : i + count] for i in range(0, value.shape[0], count)]
    unit_parts, grad_terms = [], []
    for normed, back in zip(normed_blocks, back_blocks):
        pulled = by_unit(units_all[2], jnp.concatenate(back, axis=0))
        if unit_parts:
            normed = [after(normed[0], *normed_owned, *attended_owned)] + normed[1:]
        normed = jnp.concatenate(normed, axis=0)
        gate = by_unit(units_all[0], normed)
        up = by_unit(units_all[1], normed)
        sigma = jax.nn.sigmoid(gate)
        active = gate * sigma
        gate_grad = low(pulled * up * sigma * (1.0 + gate * (1.0 - sigma)))
        up_grad = low(pulled * active)
        unit_parts.append((gate_grad, up_grad, low(active * up)))
        grad_terms.append(by_token(gate_grad, units_all[0]) + by_token(up_grad, units_all[1]))
    branch_terms = [
        low(by_token(after(part[2], *grad_terms), units_all[2])) for part in unit_parts
    ]
    first_sums, received = scatter_first(grad_terms, branch_terms)
    plane_sums = scatter_second(first_sums, ())
    normed_grad_own, normed_grad_received = scatter_last(plane_sums)
    parts = [unit_parts[0][:2] + (after(unit_parts[0][2], *plane_sums),)] + unit_parts[1:]
    units_term = units_gradient(
        parts,
        [block for blocks in normed_blocks for block in blocks],
        [block for blocks in back_blocks for block in blocks],
    )
    units_sum = lax.psum_scatter(units_term, sharing, scatter_dimension=0, tiled=True)
    branch_sums, branch_first = scatter_first(
        [after(item, *plane_sums) for item in branch_terms]
    )
    middle_grad, branch_grad, gain_two_grad, attended_grad = call_with_pieces(
        middle_back_kernel,
        out_projection,
        [normed_grad_own, normed_grad_received, middle, output_grad, gain_two],
        [
            shaped((count, D), jnp.float32),
            shaped((count, D), jnp.bfloat16),
            shaped((1, D), jnp.float32),
            shaped((count, QW), jnp.bfloat16),
        ],
        "middle_back",
        4,
    )
    branch_pieces = plane_blocks(branch_grad)
    mixed_grad, pair_grad = local_call(
        attend_back_kernel,
        [attended_grad, query, pair_all, key_marks, query_marks, cosine, sine],
        [shaped((count, QW), jnp.bfloat16), shaped((group_len, 2 * KW), jnp.float32)],
        "attend_back",
        800,
        [pltpu.VMEM((group_len, TOGETHER * count), jnp.float32)],
    )
    pair_terms, pair_got = seq_scatter_small(after(pair_grad, *branch_pieces[1:3]), count)
    query_operand = after(mixed_grad, *pair_got)
    normed_grad_part, pair_rows = call_with_pieces(
        query_kernel,
        projection,
        [query_operand],
        [shaped((count, D), jnp.float32), shaped((D, 2 * KW), jnp.bfloat16)],
        "query_back",
        7,
    )
    mixed_block, input_grad = local_call(
        lambda *refs: finish_kernel(len(pair_terms), *refs),
        pair_terms
        + [cosine, sine, mixed_grad, normed_grad_part, pair_rows, inputs, gain_one, middle_grad]
        + [gain_two_grad],
        [shaped((count + 16, QKV), jnp.bfloat16), shaped((count, D), jnp.float32)],
        "finish",
        4,
    )
    mixed_pieces = plane_blocks(mixed_block)
    branch_sums = scatter_second(branch_sums, [mixed_block])
    branch_own, branch_received = scatter_last(branch_sums)
    block_output = low(middle + branch_own + wide(branch_received))
    attended_owned[0] = after(attended_owned[0], mixed_block)
    half = attended_owned[0].shape[1] // 2
    kept, sent = local_call(
        lambda *refs: weight_kernel(len(steps), *refs),
        attended_owned + branch_pieces,
        [shaped((half, D), jnp.float32), shaped((half, D), jnp.bfloat16)],
        "out_weights",
        3,
    )
    outer_sum = kept + wide(shift(sent, "c", -1))
    depth = lax.axis_size(DP)
    shape = (depth, half // depth + 8, QKV)
    kept, sent = local_call(
        lambda *refs: joined_kernel(len(steps), *refs),
        normed_owned + mixed_pieces,
        [shaped(shape, jnp.float32), shaped(shape, jnp.bfloat16)],
        "joined_weights",
        5,
    )
    got = shift(sent, "c", -1)
    units_new = units_step(units_sum, units_weight, units_first, units_second)
    outer_grad = dp_scatter(outer_sum, [units_new[3]])
    total = kept + wide(got)
    total = add_back([total[i] for i in range(depth)], DP, [units_new[3]])
    joined_grad, vector = total[:-8], total[-8:]
    small_grad = own_small(vector, device * small_rows, small_rows)

    joined = optimizer_step(
        joined_weight, joined_grad, joined_first, joined_second, 2.0 / math.sqrt(D), DECAY
    )
    outer = optimizer_step(
        out_weight, outer_grad, out_first, out_second, 2.0 / math.sqrt(QW // 64), DECAY
    )
    small = optimizer_step(small_params, small_grad, small_first, small_second, 0.5, 0.0)
    return (block_output, input_grad) + joined + outer + units_new + small


def solution(mesh):
    groups, members = mesh.devices.shape
    fine = Mesh(mesh.devices.reshape(groups // 2, 2, members // 4, 2, 2), ALL)
    flat, cube = P(ALL, None), P(ALL, None, None)
    in_specs = (flat, flat, P(DP, None), flat, flat, cube, flat) + (flat,) * 4 + (cube,) * 2 + (flat,) * 2
    out_specs = (flat,) * 10 + (cube,) * 4 + (flat,) * 4
    return jax.shard_map(body, mesh=fine, in_specs=in_specs, out_specs=out_specs, check_vma=False)
```
